128 devices in a mesh: blk: 4 (over y_lo, core), grp: 32 (over x, z, y_hi).
Axes of the slice: x: 4, y: 4 (y_hi: 2, y_lo: 2; y = y_hi * 2 + y_lo), z: 4, core: 2. Of those that a mesh axis runs over, the one named last changes fastest.
Arguments:
- picture_vectors_raw: bfloat16 [16384, 1152], P(('blk', 'grp')), may hold values from -0.1875 to 0.1875
- caption_vectors_raw: bfloat16 [16384, 1152], P(('blk', 'grp')), may hold values from -0.1875 to 0.1875
- logit_multiplier: float32 [1], replicated, may hold values from 60 to 120
- offset_term: float32 [1], replicated, may hold values from -3 to -1
- incoming_adjoint: float32 [1], replicated, may hold values from 100 to 300
Outputs:
- image_grad: float32 [16384, 1152], P(('blk', 'grp'))
- text_grad: float32 [16384, 1152], P(('blk', 'grp'))
The draws below stay inside these ranges and needn't reach their ends.
All inputs are finite; a program needn't handle non-finite values.
Results may differ from the reference program's by a relative error of at most 0.0079.
The reference program's roundings to bfloat16 on the way (of `image_half`, `text_half` and `coupling`) count: a program that leaves them out, or rounds other values in their place, can miss the bound.
Values may be sent and summed in bfloat16 or wider, within the bound.
No kernel may reach another device: no remote copies, remote signals or barrier semaphores. Data moves between devices by JAX's collectives and lax.ppermute only.
A program may use at most 128 MiB of HBM per device.

```python
import math
import jax
import jax.numpy as jnp
from jax import lax

EMBED = 1152
MATCHED_SAMPLES = 16384


def levels(stream_key, dims, split, least, largest):
    loudness, own = 1.0, jax.random.fold_in(stream_key, 6)
    for dim, parts in split:
        heights = jnp.exp(jax.random.uniform(jax.random.fold_in(own, dim), (parts,), jnp.float32, least / len(split), largest / len(split)))
        loudness = loudness * jnp.repeat(heights, dims[dim] // parts).reshape([-1 if axis == dim else 1 for axis in range(len(dims))])
    return loudness


def gaussian(own_key, shape, deviation, bound, cuts=(), kind=jnp.bfloat16):
    entries = deviation * jax.random.normal(own_key, shape, jnp.float32)
    if cuts:
        entries = entries * levels(own_key, shape, cuts, -0.22, 0.18)
    return jnp.clip(entries, -bound, bound).astype(kind)


def setup_inputs(seed: int = 0) -> dict:
    streams_of = jax.random.split(jax.random.key(seed), 6)
    picture_vectors_raw = gaussian(streams_of[0], (MATCHED_SAMPLES, EMBED), EMBED ** -0.5, 0.1875, ((0, 128),))
    caption_vectors_raw = gaussian(streams_of[1], (MATCHED_SAMPLES, EMBED), EMBED ** -0.5, 0.1875, ((0, 128),))
    logit_multiplier = jnp.clip(jax.random.uniform(streams_of[2], (1,), jnp.float32, 60.0, 120.0), 60.0, 120.0)
    offset_term = jnp.clip(jax.random.uniform(streams_of[3], (1,), jnp.float32, -3.0, -1.0), -3.0, -1.0)
    incoming_adjoint = jnp.clip(jax.random.uniform(streams_of[4], (1,), jnp.float32, 100.0, 300.0), 100.0, 300.0)
    return dict(picture_vectors_raw=picture_vectors_raw, caption_vectors_raw=caption_vectors_raw, logit_multiplier=logit_multiplier, offset_term=offset_term, incoming_adjoint=incoming_adjoint)


def unit_rows(embedding):
    values = embedding.astype(jnp.float32)
    row_scale = lax.rsqrt(lax.optimization_barrier(jnp.mean(values * values, axis=1, keepdims=True)) + 1e-06) / math.sqrt(values.shape[1])
    return (values * row_scale, row_scale)

def unit_grad(unit_vals, row_scale, upstream_grad):
    return row_scale * (upstream_grad - unit_vals * lax.optimization_barrier(jnp.sum(unit_vals * upstream_grad, axis=1, keepdims=True)))

def reference(picture_vectors_raw, caption_vectors_raw, logit_multiplier, offset_term, incoming_adjoint):
    image_unit, image_scale = unit_rows(picture_vectors_raw)
    text_unit, text_scale = unit_rows(caption_vectors_raw)
    image_half = image_unit.astype(jnp.bfloat16)
    text_half = text_unit.astype(jnp.bfloat16)
    block_rows = math.gcd(MATCHED_SAMPLES, 1024)
    block_total = MATCHED_SAMPLES // block_rows
    derivative_multiplier = incoming_adjoint[0] * logit_multiplier[0] / MATCHED_SAMPLES
    target_position = jnp.arange(MATCHED_SAMPLES, dtype=jnp.int32)

    def advance(text_total, which):
        first_row = (which * block_rows).astype(jnp.int32)
        images = lax.dynamic_slice_in_dim(image_half, first_row, block_rows, 0)
        similarity_energies = lax.dot_general(images, text_half, (((1,), (1,)), ((), ())), preferred_element_type=jnp.float32)
        similarity_matrix = logit_multiplier[0] * similarity_energies + offset_term[0]
        source_position = first_row + jnp.arange(block_rows, dtype=jnp.int32)
        diag_mask = (source_position[:, None] == target_position[None, :]).astype(jnp.float32)
        coupling = (jax.nn.sigmoid(similarity_matrix) - diag_mask).astype(jnp.bfloat16)
        image_part = jnp.dot(coupling, text_half, preferred_element_type=jnp.float32)
        text_total = text_total + lax.dot_general(coupling, images, (((0,), (0,)), ((), ())), preferred_element_type=jnp.float32)
        return (text_total, image_part)
    start_total = jnp.zeros((MATCHED_SAMPLES, EMBED), jnp.float32)
    text_total, image_parts = lax.scan(advance, start_total, jnp.arange(block_total, dtype=jnp.int32))
    image_total = image_parts.reshape(MATCHED_SAMPLES, EMBED)
    image_grad = unit_grad(image_unit, image_scale, derivative_multiplier * image_total)
    text_grad = unit_grad(text_unit, text_scale, derivative_multiplier * text_total)
    return (image_grad, text_grad)
```

```python
import functools
import math

import jax
import jax.numpy as jnp
from jax import lax
from jax.experimental import pallas as pl
from jax.experimental.pallas import tpu as pltpu
from jax.sharding import Mesh
from jax.sharding import PartitionSpec as P

FINE_AXES = ("y_lo", "core", "x", "z", "y_hi")
FINE_SIZES = (2, 2, 4, 4, 2)
RING = 4
SIDE = 8
VMEM_BYTES = 48 * 1024 * 1024


def along(value, axis, steps):
    return lax.ppermute(value, axis, [(k, (k + steps) % RING) for k in range(RING)])


def other_core(value):
    return lax.ppermute(value, "core", [(0, 1), (1, 0)])


def y_partner(value, wrapped):
    place = lambda y: (y % 2) * 2 + y // 2
    pairs = []
    for y in range(RING):
        if wrapped:
            mate = (y + 1) % RING if y % 2 else (y - 1) % RING
        else:
            mate = y ^ 1
        pairs.append((place(y), place(mate)))
    return lax.ppermute(value, ("y_lo", "y_hi"), pairs)


def gathered(own, axis, wrapped):
    partner = y_partner(own, wrapped)
    left_own = along(own, axis, 1)
    right_own = along(own, axis, -1)
    left_partner = along(partner, axis, 1)
    right_partner = along(partner, axis, -1)
    far_own = along(left_own, axis, 1)
    far_partner = along(right_partner, axis, -1)
    return [own, partner, left_own, left_partner, right_own, right_partner, far_own, far_partner]


def plus(*terms):
    total = terms[0].astype(jnp.float32)
    for term in terms[1:]:
        total = total + term.astype(jnp.float32)
    return total


def scattered(parts, axis, wrapped):
    own, partner, left_own, left_partner, right_own, right_partner, far_own, far_partner = parts
    half = jnp.bfloat16
    from_far_partner = along(far_partner, axis, 1)
    from_far_own = along(far_own, axis, -1)
    partner_a = along(left_partner, axis, -1)
    partner_b = along(plus(right_partner, from_far_partner).astype(half), axis, 1)
    own_a = along(right_own, axis, 1)
    own_b = along(plus(left_own, from_far_own).astype(half), axis, -1)
    from_partner = y_partner(plus(partner, partner_a, partner_b).astype(half), wrapped)
    return plus(own, own_a, own_b, from_partner)


def unit_rows(embedding):
    values = embedding.astype(jnp.float32)
    row_scale = lax.rsqrt(jnp.mean(values * values, axis=1, keepdims=True) + 1e-06) / math.sqrt(
        values.shape[1]
    )
    return (values * row_scale, row_scale)


def unit_grad(unit_vals, row_scale, upstream_grad):
    return row_scale * (
        upstream_grad - unit_vals * jnp.sum(unit_vals * upstream_grad, axis=1, keepdims=True)
    )


def coupling_kernel(diagonal, rows, *refs):
    affine = refs[0]
    image_refs = refs[1 : 1 + SIDE]
    text_refs = refs[1 + SIDE : 1 + 2 * SIDE]
    coupling_ref = refs[1 + 2 * SIDE]
    part_refs = refs[2 + 2 * SIDE : 2 + 3 * SIDE]
    images, texts, image_sems, text_sems = refs[2 + 3 * SIDE :]
    copies = []
    for k in range(SIDE):
        copies.append(
            pltpu.make_async_copy(text_refs[k], texts.at[pl.ds(k * rows, rows)], text_sems.at[k])
        )
        copies.append(
            pltpu.make_async_copy(image_refs[k], images.at[pl.ds(k * rows, rows)], image_sems.at[k])
        )
    for copy in copies:
        copy.start()
    for copy in copies:
        copy.wait()
    slope = affine[0]
    shift = affine[1]
    block = 2 * rows
    for k in range(SIDE // 2):
        here = images[pl.ds(k * block, block), :]
        energies = lax.dot_general(
            here, texts[...], (((1,), (1,)), ((), ())), preferred_element_type=jnp.float32
        )
        coupling = 0.5 * jnp.tanh(slope * energies + shift) + 0.5
        if diagonal and k == 0:
            row = lax.broadcasted_iota(jnp.int32, coupling.shape, 0)
            column = lax.broadcasted_iota(jnp.int32, coupling.shape, 1)
            coupling = coupling - jnp.where((row == column) & (row < rows), 1.0, 0.0)
        coupling = coupling.astype(jnp.bfloat16)
        coupling_ref[pl.ds(k * block, block), :] = coupling
        part = jnp.dot(coupling, texts[...], preferred_element_type=jnp.float32)
        part = part.astype(jnp.bfloat16)
        part_refs[2 * k][...] = part[:rows]
        part_refs[2 * k + 1][...] = part[rows:]


def coupled(affine, image_shards, text_shards, diagonal):
    rows, width = image_shards[0].shape
    whole = pl.BlockSpec(memory_space=pltpu.VMEM)
    anywhere = pl.BlockSpec(memory_space=pl.ANY)
    shard = jax.ShapeDtypeStruct((rows, width), jnp.bfloat16)
    out = pl.pallas_call(
        functools.partial(coupling_kernel, diagonal, rows),
        out_shape=[jax.ShapeDtypeStruct((SIDE * rows, SIDE * rows), jnp.bfloat16)] + [shard] * SIDE,
        in_specs=[pl.BlockSpec(memory_space=pltpu.SMEM)] + [anywhere] * (2 * SIDE),
        out_specs=[whole] * (1 + SIDE),
        scratch_shapes=[
            pltpu.VMEM((SIDE * rows, width), jnp.bfloat16),
            pltpu.VMEM((SIDE * rows, width), jnp.bfloat16),
            pltpu.SemaphoreType.DMA((SIDE,)),
            pltpu.SemaphoreType.DMA((SIDE,)),
        ],
        cost_estimate=pl.CostEstimate(
            flops=4 * (SIDE * rows) ** 2 * width,
            bytes_accessed=6 * SIDE * rows * width + 2 * (SIDE * rows) ** 2,
            transcendentals=(SIDE * rows) ** 2,
        ),
        compiler_params=pltpu.CompilerParams(vmem_limit_bytes=VMEM_BYTES),
    )(affine, *image_shards, *text_shards)
    return out[0], out[1:]


def text_kernel(rows, *refs):
    couplings = refs[:2]
    image_refs = refs[2 : 2 + 2 * SIDE]
    part_refs = refs[2 + 2 * SIDE : 2 + 3 * SIDE]
    images, image_sems = refs[2 + 3 * SIDE :]
    copies = [
        pltpu.make_async_copy(image_refs[k], images.at[pl.ds(k * rows, rows)], image_sems.at[k])
        for k in range(2 * SIDE)
    ]
    for copy in copies:
        copy.start()
    for copy in copies:
        copy.wait()
    block = 2 * rows
    for k in range(SIDE // 2 - 1, -1, -1):
        part = None
        for which in range(2):
            term = lax.dot_general(
                couplings[which][:, pl.ds(k * block, block)],
                images[pl.ds(which * SIDE * rows, SIDE * rows), :],
                (((0,), (0,)), ((), ())),
                preferred_element_type=jnp.float32,
            )
            part = term if part is None else part + term
        part = part.astype(jnp.bfloat16)
        part_refs[2 * k][...] = part[:rows]
        part_refs[2 * k + 1][...] = part[rows:]


def text_parts(couplings, image_shards):
    rows, width = image_shards[0].shape
    whole = pl.BlockSpec(memory_space=pltpu.VMEM)
    anywhere = pl.BlockSpec(memory_space=pl.ANY)
    shard = jax.ShapeDtypeStruct((rows, width), jnp.bfloat16)
    return pl.pallas_call(
        functools.partial(text_kernel, rows),
        out_shape=[shard] * SIDE,
        in_specs=[whole] * 2 + [anywhere] * (2 * SIDE),
        out_specs=[whole] * SIDE,
        scratch_shapes=[
            pltpu.VMEM((2 * SIDE * rows, width), jnp.bfloat16),
            pltpu.SemaphoreType.DMA((2 * SIDE,)),
        ],
        cost_estimate=pl.CostEstimate(
            flops=4 * (SIDE * rows) ** 2 * width,
            bytes_accessed=6 * SIDE * rows * width + 4 * (SIDE * rows) ** 2,
            transcendentals=0,
        ),
        compiler_params=pltpu.CompilerParams(vmem_limit_bytes=VMEM_BYTES),
    )(*couplings, *image_shards)


def on_device(
    picture_vectors_raw, caption_vectors_raw, logit_multiplier, offset_term, incoming_adjoint
):
    image_unit, image_scale = unit_rows(picture_vectors_raw)
    text_unit, text_scale = unit_rows(caption_vectors_raw)
    pairs = picture_vectors_raw.shape[0] * math.prod(FINE_SIZES)
    derivative_multiplier = incoming_adjoint[0] * logit_multiplier[0] / pairs
    affine = jnp.concatenate([0.5 * logit_multiplier, 0.5 * offset_term])
    images = gathered(image_unit.astype(jnp.bfloat16), "x", False)
    texts = gathered(text_unit.astype(jnp.bfloat16), "z", True)
    images_there = [other_core(shard) for shard in images]
    coupling_there, parts_there = coupled(affine, images_there, texts, False)
    coupling_here, parts_here = coupled(affine, images, texts, True)
    parts_back = [other_core(part) for part in parts_there]
    image_sums = [plus(a, b).astype(jnp.bfloat16) for a, b in zip(parts_here, parts_back)]
    text_sums = text_parts([coupling_there, coupling_here], images_there + images)
    image_total = scattered(image_sums, "x", False)
    text_total = scattered(text_sums, "z", True)
    image_grad = unit_grad(image_unit, image_scale, derivative_multiplier * image_total)
    text_grad = unit_grad(text_unit, text_scale, derivative_multiplier * text_total)
    return (image_grad, text_grad)


def solution(mesh):
    fine = Mesh(mesh.devices.reshape(FINE_SIZES), FINE_AXES)
    rows = P(FINE_AXES, None)
    return jax.shard_map(
        on_device,
        mesh=fine,
        in_specs=(rows, rows, P(), P(), P()),
        out_specs=(rows, rows),
        check_vma=False,
    )
```

```python
import functools
import math

import jax
import jax.numpy as jnp
from jax import lax
from jax.experimental import pallas as pl
from jax.experimental.pallas import tpu as pltpu
from jax.sharding import Mesh
from jax.sharding import PartitionSpec as P

FINE_AXES = ("y_lo", "core", "x", "z", "y_hi")
FINE_SIZES = (2, 2, 4, 4, 2)
RING = 4
VMEM_BYTES = 40 * 1024 * 1024
HALF = jnp.bfloat16
FULL = jnp.float32

VMEM = pl.BlockSpec(memory_space=pltpu.VMEM)
SMEM = pl.BlockSpec(memory_space=pltpu.SMEM)
ANY = pl.BlockSpec(memory_space=pl.ANY)
PARAMS = pltpu.CompilerParams(vmem_limit_bytes=VMEM_BYTES)


def both_ways(value, axis, sign):
    pairs = []
    for core in range(2):
        step = sign if core == 0 else -sign
        for k in range(RING):
            pairs.append((core * RING + k, core * RING + (k + step) % RING))
    return lax.ppermute(value, ("core", axis), pairs)


def other_core(value):
    return lax.ppermute(value, "core", [(0, 1), (1, 0)])


def y_partner(value, wrapped):
    pairs = []
    for y in range(RING):
        if wrapped:
            mate = (y + 1) % RING if y % 2 else (y - 1) % RING
        else:
            mate = y ^ 1
        pairs.append(((y % 2) * 2 + y // 2, (mate % 2) * 2 + mate // 2))
    return lax.ppermute(value, ("y_lo", "y_hi"), pairs)


def local(body, outs, scalars, arrays, passed=()):
    n_scalars, n_arrays, n_outs, n_passed = len(scalars), len(arrays), len(outs), len(passed)

    def kernel(*refs):
        given = refs[: n_scalars + n_arrays]
        results = refs[n_scalars + n_arrays + n_passed :][:n_outs]
        for ref, value in zip(results, body(given[:n_scalars], given[n_scalars:]), strict=True):
            ref[...] = value.astype(ref.dtype)

    first = n_scalars + n_arrays
    return pl.pallas_call(
        kernel,
        out_shape=[jax.ShapeDtypeStruct(s, d) for s, d in outs]
        + [jax.ShapeDtypeStruct(a.shape, a.dtype) for a in passed],
        in_specs=[SMEM] * n_scalars + [VMEM] * n_arrays + [ANY] * n_passed,
        out_specs=[VMEM] * n_outs + [ANY] * n_passed,
        input_output_aliases={first + k: n_outs + k for k in range(n_passed)},
        compiler_params=PARAMS,
    )(*scalars, *arrays, *passed)


def assembled(body, outs, scalars, whole, stacks, flops):
    flat = [piece for stack in stacks for piece in stack]
    n_scalars, n_whole, n_flat, n_outs = len(scalars), len(whole), len(flat), len(outs)

    def kernel(*refs):
        scalar_refs, refs = refs[:n_scalars], refs[n_scalars:]
        whole_refs, refs = refs[:n_whole], refs[n_whole:]
        piece_refs, refs = refs[:n_flat], refs[n_flat:]
        out_refs, refs = refs[:n_outs], refs[n_outs:]
        buffers, sems = refs[: len(stacks)], refs[len(stacks)]
        copies = []
        for buffer, stack in zip(buffers, stacks, strict=True):
            row = 0
            for piece in stack:
                rows = piece.shape[0]
                k = len(copies)
                copies.append(
                    pltpu.make_async_copy(
                        piece_refs[k], buffer.at[pl.ds(row, rows)], sems.at[k]
                    )
                )
                row += rows
        for copy in copies:
            copy.start()
        for copy in copies:
            copy.wait()
        body(scalar_refs, whole_refs, buffers, out_refs)

    return pl.pallas_call(
        kernel,
        out_shape=[jax.ShapeDtypeStruct(s, d) for s, d in outs],
        in_specs=[SMEM] * n_scalars + [VMEM] * n_whole + [ANY] * n_flat,
        out_specs=[VMEM] * n_outs,
        scratch_shapes=[
            pltpu.VMEM((sum(p.shape[0] for p in stack), stack[0].shape[1]), stack[0].dtype)
            for stack in stacks
        ]
        + [pltpu.SemaphoreType.DMA((n_flat,))],
        cost_estimate=pl.CostEstimate(
            flops=flops,
            bytes_accessed=sum(a.size * a.dtype.itemsize for a in flat),
            transcendentals=0,
        ),
        compiler_params=PARAMS,
    )(*scalars, *whole, *flat)


def dot(a, b, contract):
    return lax.dot_general(a, b, ((contract[:1], contract[1:]), ((), ())), preferred_element_type=FULL)


def unit_rows(raw):
    values = raw.astype(FULL)
    scale = lax.rsqrt(jnp.mean(values * values, axis=1, keepdims=True) + 1e-06) / math.sqrt(
        values.shape[1]
    )
    return values * scale, scale


def coupling_block(affine, texts, images):
    energies = dot(texts, images, (1, 1))
    return 0.5 * jnp.tanh(affine[0] * energies + affine[1]) + 0.5


def on_device(
    picture_vectors_raw, caption_vectors_raw, logit_multiplier, offset_term, incoming_adjoint
):
    rows, width = picture_vectors_raw.shape
    pairs = rows * math.prod(FINE_SIZES)
    is_first = (lax.axis_index("core") == 0).astype(FULL).reshape(1)
    affine = jnp.concatenate([0.5 * logit_multiplier, 0.5 * offset_term])
    derivative_multiplier = incoming_adjoint * logit_multiplier / pairs
    one, two = ((rows, width), HALF), ((2 * rows, width), HALF)
    one_full = ((rows, width), FULL)
    block = 2 * rows
    block_flops = 2 * block * block * width


    image_raw_there = other_core(picture_vectors_raw)
    text_raw_there = other_core(caption_vectors_raw)

    def normalize(_, refs):
        image, image_there, text, text_there = [unit_rows(ref[...])[0].astype(HALF) for ref in refs]
        return [
            jnp.concatenate([image, image_there], 0),
            jnp.concatenate([text, text_there], 0),
            image,
            text,
        ]

    io, to, image_own, text_own = local(
        normalize,
        [two, two, one, one],
        [],
        [picture_vectors_raw, image_raw_there, caption_vectors_raw, text_raw_there],
    )
    ia = both_ways(io, "x", 1)
    ta = both_ways(to, "z", 1)
    ip_mine = y_partner(image_own, False)
    tp_mine = y_partner(text_own, True)

    i_on, t_on, ia, ta, ip_mine, tp_mine = local(
        lambda _, refs: [refs[0][:rows], refs[1][:rows]],
        [one, one],
        [],
        [ia, ta],
        [ia, ta, ip_mine, tp_mine],
    )
    im = both_ways(i_on, "x", 1)
    tm = both_ways(t_on, "z", 1)
    ip_there = other_core(ip_mine)
    tp_there = other_core(tp_mine)
    ib = other_core(ia)

    def partners(scalars, refs):
        image_mine, image_there, text_mine, text_there, text_own_chip = [ref[...] for ref in refs]
        image_pair = jnp.concatenate([image_mine, image_there], 0)
        text_pair = jnp.concatenate([text_mine, text_there], 0)
        return [image_pair, text_pair, jnp.where(scalars[0][0] > 0, text_own_chip, text_pair)]

    ip, tp, te, im, tm, ib = local(
        partners,
        [two, two, two],
        [is_first],
        [ip_mine, ip_there, tp_mine, tp_there, to],
        [im, tm, ib],
    )
    ia2 = both_ways(ip, "x", 1)
    ta2 = both_ways(tp, "z", 1)
    im2 = y_partner(im, False)
    tm2 = y_partner(tm, True)
    it = other_core(im)

    images_early = [io, ip, ia, ib, im, it]
    texts_early = [te, ta, tm]
    n_ie, n_te, n_il, n_tl = 10 * rows, 5 * rows, 6 * rows, 3 * rows
    n_t = n_te + n_tl

    def early(scalars, _, stacks, outs):
        images, texts = stacks
        for k in range(n_ie // block):
            cols = pl.ds(k * block, block)
            tile = coupling_block(scalars[0], texts[...], images[cols, :])
            if k == 0:
                row = lax.broadcasted_iota(jnp.int32, tile.shape, 0)
                column = lax.broadcasted_iota(jnp.int32, tile.shape, 1)
                tile = tile - jnp.where(row == column, scalars[1][0], 0.0)
            outs[0][:, cols] = tile.astype(HALF)

    (c_ee,) = assembled(
        early,
        [((n_te, n_ie), HALF)],
        [affine, is_first],
        [],
        [images_early, texts_early],
        12 * block_flops,
    )

    ia2, ta2, im2, tm2, it, c_ee = local(lambda *_: [], [], [], [], [ia2, ta2, im2, tm2, it, c_ee])
    images_early = [io, ip, ia, ib, im, it]
    texts_late = [ta2, tm2]
    ib2 = other_core(ia2)
    it2 = other_core(im2)

    def late_texts(scalars, _, stacks, outs):
        images, texts = stacks
        for k in range(n_ie // block):
            cols = pl.ds(k * block, block)
            outs[0][:, cols] = coupling_block(scalars[0], texts[...], images[cols, :]).astype(HALF)

    (c_le,) = assembled(
        late_texts,
        [((n_tl, n_ie), HALF)],
        [affine],
        [],
        [images_early, texts_late],
        8 * block_flops,
    )

    images_late = [ia2, ib2, im2, it2]

    def late_images(scalars, _, stacks, outs):
        images, texts = stacks
        for k in range(n_il // block):
            cols = pl.ds(k * block, block)
            tile = coupling_block(scalars[0], texts[...], images[cols, :]).astype(HALF)
            outs[0][:, cols] = tile
            part = dot(tile, texts[...], (0, 0)).astype(HALF)
            if k < 2:
                outs[1 + k][:block, :] = part
            else:
                outs[1][block:, :] = part[:rows]
                outs[2][block:, :] = part[rows:]

    c_l, gi_late, gi_late_there = assembled(
        late_images,
        [((n_t, n_il), HALF), ((3 * rows, width), HALF), ((3 * rows, width), HALF)],
        [affine],
        [],
        [images_late, texts_early + texts_late],
        24 * block_flops,
    )
    gi_late_back = other_core(gi_late_there)

    def late_text_parts(_, whole, stacks, outs):
        c_le, c_l = whole
        (images,) = stacks
        part = dot(c_le[...], images[:n_ie, :], (1, 0))
        part = part + dot(c_l[n_te:, :], images[n_ie:, :], (1, 0))
        part = part.astype(HALF)
        outs[0][...] = part[:block]
        outs[1][...] = part[block:]

    ga2_t, gm2_t = assembled(
        late_text_parts,
        [two, one],
        [],
        [c_le, c_l],
        [images_early + images_late],
        12 * block_flops,
    )

    def add_late(_, refs):
        total = refs[0][...].astype(FULL) + refs[1][...].astype(FULL)
        return [total[:block], total[block:]]

    ga2_i, gm2_i, ga2_t, gm2_t = local(
        add_late, [two, one], [], [gi_late, gi_late_back], [ga2_t, gm2_t]
    )
    p_in_i = both_ways(ga2_i, "x", -1)
    p_in_t = both_ways(ga2_t, "z", -1)
    m_in_i = y_partner(gm2_i, False)
    m_in_t = y_partner(gm2_t, True)

    def image_part(couplings, texts, first, count):
        cols = pl.ds(first, count)
        part = dot(couplings[0][:, cols], texts[:n_te, :], (0, 0))
        return (part + dot(couplings[1][:, cols], texts[n_te:, :], (0, 0))).astype(HALF)

    def text_part(couplings, images, first, count):
        at = pl.ds(first, count)
        part = dot(couplings[0][at, :], images[:n_ie, :], (1, 0))
        return (part + dot(couplings[2][at, :], images[n_ie:, :], (1, 0))).astype(HALF)

    def parts_first(_, couplings, stacks, outs):
        images, texts = stacks
        outs[0][...] = image_part(couplings, texts, block, block)
        part = image_part(couplings, texts, 4 * block, block)
        outs[1][...] = part[:rows]
        outs[2][...] = part[rows:]
        outs[3][...] = text_part(couplings, images, 0, block)
        outs[4][...] = text_part(couplings, images, 2 * block, rows)

    gp_i, gm_i, gt_i, ge_t, gm_t = assembled(
        parts_first,
        [two, one, one, two, one],
        [],
        [c_ee, c_le, c_l],
        [images_early + images_late, texts_early + texts_late],
        20 * block_flops,
    )
    gt_back = other_core(gt_i)

    def round_one(scalars, refs):
        p_in_i, p_in_t, m_in_i, m_in_t, gp_i, gm_i, gt_back, ge_t, gm_t = [
            ref[...].astype(FULL) for ref in refs
        ]
        p_i = p_in_i + gp_i
        p_t = p_in_t + ge_t * (1.0 - scalars[0][0])
        return [
            p_i[:rows],
            p_i[rows:],
            p_t[:rows],
            p_t[rows:],
            gm_i + gt_back + m_in_i,
            gm_t + m_in_t,
        ]

    p_i, p_i_there, p_t, p_t_there, m_i, m_t = local(
        round_one,
        [one_full, one, one_full, one, one, one],
        [is_first],
        [p_in_i, p_in_t, m_in_i, m_in_t, gp_i, gm_i, gt_back, ge_t, gm_t],
    )
    a_in_i = both_ways(m_i, "x", -1)
    a_in_t = both_ways(m_t, "z", -1)
    p_back_i = other_core(p_i_there)
    p_back_t = other_core(p_t_there)

    def parts_second(_, couplings, stacks, outs):
        images, texts = stacks
        outs[0][...] = image_part(couplings, texts, 3 * block, block)
        outs[1][...] = image_part(couplings, texts, 2 * block, block)
        outs[2][...] = image_part(couplings, texts, 0, block)
        outs[3][...] = text_part(couplings, images, block, block)

    gb_i, ga_i, go_i, ga_t = assembled(
        parts_second,
        [two, two, two, two],
        [],
        [c_ee, c_le, c_l],
        [images_early + images_late, texts_early + texts_late],
        24 * block_flops,
    )
    gb_back = other_core(gb_i)

    def round_two(_, refs):
        p_i, p_back_i, p_t, p_back_t, a_in_i, a_in_t, ga_i, gb_back, ga_t = [
            ref[...].astype(FULL) for ref in refs
        ]
        a_i = ga_i + gb_back
        return [
            p_i + p_back_i,
            p_t + p_back_t,
            jnp.concatenate([a_i[:rows] + a_in_i, a_i[rows:]], 0),
            jnp.concatenate([ga_t[:rows] + a_in_t, ga_t[rows:]], 0),
        ]

    p_i, p_t, a_i, a_t = local(
        round_two,
        [one, one, two, two],
        [],
        [p_i, p_back_i, p_t, p_back_t, a_in_i, a_in_t, ga_i, gb_back, ga_t],
    )
    o_in_i = both_ways(a_i, "x", -1)
    o_in_t = both_ways(a_t, "z", -1)
    y_in_i = y_partner(p_i, False)
    y_in_t = y_partner(p_t, True)

    def round_three(scalars, refs):
        o_in_i, o_in_t, y_in_i, y_in_t, go_i, ge_t = [ref[...].astype(FULL) for ref in refs]
        o_i = o_in_i + go_i
        o_t = o_in_t + ge_t * scalars[0][0]
        return [o_i[:rows] + y_in_i, o_i[rows:], o_t[:rows] + y_in_t, o_t[rows:]]

    o_i, o_i_there, o_t, o_t_there = local(
        round_three,
        [one_full, one, one_full, one],
        [is_first],
        [o_in_i, o_in_t, y_in_i, y_in_t, go_i, ge_t],
    )
    o_back_i = other_core(o_i_there)
    o_back_t = other_core(o_t_there)

    def finish(scalars, refs):
        multiplier = scalars[0][0]
        results = []
        for raw, mine, back in (refs[:3], refs[3:]):
            unit, scale = unit_rows(raw[...])
            grad = multiplier * (mine[...] + back[...].astype(FULL))
            results.append(scale * (grad - unit * jnp.sum(unit * grad, axis=1, keepdims=True)))
        return results

    return tuple(
        local(
            finish,
            [one_full, one_full],
            [derivative_multiplier],
            [picture_vectors_raw, o_i, o_back_i, caption_vectors_raw, o_t, o_back_t],
        )
    )


def solution(mesh):
    fine = Mesh(mesh.devices.reshape(FINE_SIZES), FINE_AXES)
    rows = P(FINE_AXES, None)
    return jax.shard_map(
        on_device,
        mesh=fine,
        in_specs=(rows, rows, P(), P(), P()),
        out_specs=(rows, rows),
        check_vma=False,
    )
```

```python
import functools
import math

import jax
import jax.numpy as jnp
import numpy as np
from jax import lax
from jax.experimental import pallas as pl
from jax.experimental.pallas import tpu as pltpu
from jax.sharding import Mesh
from jax.sharding import PartitionSpec as P

FINE_AXES = ("y_lo", "core", "x", "z", "y_hi")
FINE_SIZES = (2, 2, 4, 4, 2)
RING = 4
VMEM_BYTES = 32 * 1024 * 1024
HALF = jnp.bfloat16
FULL = jnp.float32

VMEM = pl.BlockSpec(memory_space=pltpu.VMEM)
SMEM = pl.BlockSpec(memory_space=pltpu.SMEM)
ANY = pl.BlockSpec(memory_space=pl.ANY)
PARAMS = pltpu.CompilerParams(vmem_limit_bytes=VMEM_BYTES)

WAYS = ((2, 1), (1, 1), (3, 1), (2, 0), (1, 0), (3, 0), (0, 1))


def place(core, x, y, z):
    return int(np.ravel_multi_index((y % 2, core, x, z, y // 2), FINE_SIZES))


def mate(core, y):
    if core == 0:
        return y ^ 1
    return (y + 1) % RING if y % 2 else (y - 1) % RING


def ring_gather(shard):
    groups = []
    for y in range(RING):
        for k in range(RING):
            groups.append([place(0, x, y, k) for x in range(RING)])
            groups.append([place(1, k, y, z) for z in range(RING)])
    return lax.all_gather(shard, FINE_AXES, axis=0, tiled=True, axis_index_groups=groups)


def sent(value, steps, across):
    pairs = []
    for x, y, z in np.ndindex(RING, RING, RING):
        for core in range(2):
            to_y = mate(core, y) if across else y
            to_x = (x + steps) % RING if core == 0 else x
            to_z = (z + steps) % RING if core == 1 else z
            pairs.append((place(core, x, y, z), place(core, to_x, to_y, to_z)))
    return lax.ppermute(value, FINE_AXES, pairs)


def other_core(value):
    return lax.ppermute(value, "core", [(0, 1), (1, 0)])


def dot(a, b, contract):
    return lax.dot_general(a, b, ((contract[:1], contract[1:]), ((), ())), preferred_element_type=FULL)


def unit_rows(raw):
    values = raw.astype(FULL)
    scale = lax.rsqrt(jnp.mean(values * values, axis=1, keepdims=True) + 1e-06) / math.sqrt(
        values.shape[1]
    )
    return values * scale, scale


def normalize_kernel(info, images, texts, there, raw, first, second, both):
    rows = images.shape[0]
    is_first = info[0] == 0
    here = jnp.where(is_first, images[...].astype(FULL), texts[...].astype(FULL)).astype(HALF)
    raw[pl.ds(info[0] * rows, rows), :] = here
    raw[pl.ds((1 - info[0]) * rows, rows), :] = there[...]
    unit = unit_rows(raw[...])[0].astype(HALF)
    first[...] = unit[:rows]
    second[...] = unit[rows:]
    both[...] = unit


def part_kernel(steps, own, n_after, info, affine, mine_a, mine_b, *refs):
    theirs, refs = refs[:4], refs[4 + n_after :]
    part, coupling = refs
    count = mine_a.shape[0]
    rows = count // RING
    at = pl.ds(pl.multiple_of(lax.rem(info[1] + steps, RING) * rows, rows), rows)
    mine = jnp.concatenate([mine_a[at, :], mine_b[at, :]], 0)
    for k, piece in enumerate(theirs):
        energies = dot(mine, piece[...], (1, 1))
        tile = 0.5 * jnp.tanh(affine[0] * energies + affine[1]) + 0.5
        if own and k < 2:
            row = lax.broadcasted_iota(jnp.int32, tile.shape, 0)
            column = lax.broadcasted_iota(jnp.int32, tile.shape, 1)
            same = (row - k * rows == column - info[2] * rows) & (row // rows == k)
            tile = tile - jnp.where(same, 1.0, 0.0)
        coupling[:, pl.ds(k * count, count)] = tile.astype(HALF)
    total = None
    for k, piece in enumerate(theirs):
        term = dot(coupling[:, pl.ds(k * count, count)], piece[...], (1, 0))
        total = term if total is None else total + term
    part[...] = total.astype(HALF)


def part_of(steps, own, info, affine, mine, theirs, after):
    count, width = theirs[0].shape
    unit = 2 * count // RING
    return pl.pallas_call(
        functools.partial(part_kernel, steps, own, len(after)),
        out_shape=jax.ShapeDtypeStruct((unit, width), HALF),
        in_specs=[SMEM, SMEM] + [VMEM] * 6 + [ANY] * len(after),
        out_specs=VMEM,
        scratch_shapes=[pltpu.VMEM((unit, 4 * count), HALF)],
        cost_estimate=pl.CostEstimate(
            flops=16 * unit * count * width,
            bytes_accessed=2 * unit * width,
            transcendentals=4 * unit * count,
        ),
        compiler_params=PARAMS,
    )(info, affine, *mine, *theirs, *after)


def finish_kernel(info, multiplier, raw, *refs):
    parts, (here, there, grads) = refs[:-3], refs[-3:]
    rows = here.shape[0]
    total = parts[0][...].astype(FULL)
    for part in parts[1:]:
        total = total + part[...].astype(FULL)
    unit, scale = unit_rows(raw[...])
    grad = multiplier[0] * total
    grads[...] = scale * (grad - unit * jnp.sum(unit * grad, axis=1, keepdims=True))
    here[...] = grads[pl.ds(info[0] * rows, rows), :]
    there[...] = grads[pl.ds((1 - info[0]) * rows, rows), :]


def on_device(
    picture_vectors_raw, caption_vectors_raw, logit_multiplier, offset_term, incoming_adjoint
):
    rows, width = picture_vectors_raw.shape
    pairs = rows * math.prod(FINE_SIZES)
    core, x, z = (lax.axis_index(name) for name in ("core", "x", "z"))
    is_first = core == 0
    info = jnp.stack([core, jnp.where(is_first, x, z), jnp.where(is_first, z, x)]).astype(jnp.int32)
    affine = jnp.concatenate([0.5 * logit_multiplier, 0.5 * offset_term])
    multiplier = incoming_adjoint * logit_multiplier / pairs
    shard = jax.ShapeDtypeStruct((rows, width), HALF)
    unit = jax.ShapeDtypeStruct((2 * rows, width), HALF)
    shard_full = jax.ShapeDtypeStruct((rows, width), FULL)

    raw_there = other_core(jnp.where(is_first, caption_vectors_raw, picture_vectors_raw))
    raw, own_a, own_b, own = pl.pallas_call(
        normalize_kernel,
        out_shape=[unit, shard, shard, unit],
        in_specs=[SMEM] + [VMEM] * 3,
        out_specs=[VMEM] * 4,
        compiler_params=PARAMS,
    )(info, picture_vectors_raw, caption_vectors_raw, raw_there)

    partner = sent(own, 0, True)
    near = [ring_gather(own_a), ring_gather(own_b)]
    near_there = [other_core(piece) for piece in near]
    far = [ring_gather(partner[:rows]), ring_gather(partner[rows:])]
    far_there = [other_core(piece) for piece in far]
    theirs = near_there + far_there

    arrived = []
    for k, (steps, across) in enumerate(WAYS):
        after = arrived[k - 4 : k - 3] if k >= 4 else []
        mine = far if across else near
        part = part_of(steps, False, info, affine, mine, theirs, after)
        arrived.append(sent(part, steps, across))
    own_part = part_of(0, True, info, affine, near, theirs, arrived[3:4])

    here, there = pl.pallas_call(
        finish_kernel,
        out_shape=[shard_full, shard_full],
        in_specs=[SMEM, SMEM] + [VMEM] * (2 + len(arrived)),
        out_specs=[VMEM] * 2,
        scratch_shapes=[pltpu.VMEM((2 * rows, width), FULL)],
        compiler_params=PARAMS,
    )(info, multiplier, raw, own_part, *arrived)
    back = other_core(there)
    return (jnp.where(is_first, here, back), jnp.where(is_first, back, here))


def solution(mesh):
    fine = Mesh(mesh.devices.reshape(FINE_SIZES), FINE_AXES)
    rows = P(FINE_AXES, None)
    return jax.shard_map(
        on_device,
        mesh=fine,
        in_specs=(rows, rows, P(), P(), P()),
        out_specs=(rows, rows),
        check_vma=False,
    )
```

```python
import functools
import math

import jax
import jax.numpy as jnp
import numpy as np
from jax import lax
from jax.experimental import pallas as pl
from jax.experimental.pallas import tpu as pltpu
from jax.sharding import Mesh
from jax.sharding import PartitionSpec as P

FINE_AXES = ("y_lo", "core", "x", "z", "y_hi")
FINE_SIZES = (2, 2, 4, 4, 2)
RING = 4
VMEM_BYTES = 16 * 1024 * 1024
HALF = jnp.bfloat16
FULL = jnp.float32

VMEM = pl.BlockSpec(memory_space=pltpu.VMEM)
SMEM = pl.BlockSpec(memory_space=pltpu.SMEM)
ANY = pl.BlockSpec(memory_space=pl.ANY)
PARAMS = pltpu.CompilerParams(vmem_limit_bytes=VMEM_BYTES)

WAYS = ((2, 1), (1, 1), (3, 1), (2, 0), (1, 0), (3, 0), (0, 1))
EARLY = ((0, 1), (1, 0), (3, 0))


def place(core, x, y, z):
    return int(np.ravel_multi_index((y % 2, core, x, z, y // 2), FINE_SIZES))


def mate(core, y):
    if core == 0:
        return y ^ 1
    return (y + 1) % RING if y % 2 else (y - 1) % RING


def sent(value, steps, across):
    pairs = []
    for x, y, z in np.ndindex(RING, RING, RING):
        for core in range(2):
            to_y = mate(core, y) if across else y
            to_x = (x + steps) % RING if core == 0 else x
            to_z = (z + steps) % RING if core == 1 else z
            pairs.append((place(core, x, y, z), place(core, to_x, to_y, to_z)))
    return lax.ppermute(value, FINE_AXES, pairs)


def other_core(value):
    return lax.ppermute(value, "core", [(0, 1), (1, 0)])


def dot(a, b, contract):
    return lax.dot_general(a, b, ((contract[:1], contract[1:]), ((), ())), preferred_element_type=FULL)


def unit_rows(raw):
    values = raw.astype(FULL)
    scale = lax.rsqrt(jnp.mean(values * values, axis=1, keepdims=True) + 1e-06) / math.sqrt(
        values.shape[1]
    )
    return values * scale, scale


def normalize_kernel(is_first, image, text, image_there, text_there, raw, mine, theirs):
    rows = image.shape[0]
    first = is_first[0] > 0
    images = (image[...].astype(FULL), image_there[...].astype(FULL))
    texts = (text[...].astype(FULL), text_there[...].astype(FULL))
    for k in range(2):
        at = pl.ds(k * rows, rows)
        of_image = jnp.where(first, images[k], images[1 - k])
        of_text = jnp.where(first, texts[k], texts[1 - k])
        here = jnp.where(first, of_image, of_text)
        raw[at, :] = here.astype(HALF)
        mine[at, :] = unit_rows(here)[0].astype(HALF)
        theirs[at, :] = unit_rows(jnp.where(first, of_text, of_image))[0].astype(HALF)


def accumulate(affine, mine, theirs, coupling, start, diagonal):
    unit = mine.shape[0]
    for k, other in enumerate(theirs):
        energies = dot(mine, other[...], (1, 1))
        tile = 0.5 * jnp.tanh(affine[0] * energies + affine[1]) + 0.5
        if diagonal and k == 0:
            row = lax.broadcasted_iota(jnp.int32, tile.shape, 0)
            column = lax.broadcasted_iota(jnp.int32, tile.shape, 1)
            tile = tile - jnp.where(row == column, 1.0, 0.0)
        coupling[:, pl.ds(k * unit, unit)] = tile.astype(HALF)
    total = start
    for k, other in enumerate(theirs):
        term = dot(coupling[:, pl.ds(k * unit, unit)], other[...], (1, 0))
        total = term if total is None else total + term
    return total


def early_kernel(count, affine, *refs):
    mine, theirs, sums, coupling = refs[:count], refs[count : 2 * count], refs[2 * count : -1], refs[-1]
    for k in range(count):
        sums[k][...] = accumulate(affine, mine[k][...], theirs, coupling, None, k == 0)


def early_sums(affine, mine, theirs):
    count = len(mine)
    unit, width = mine[0].shape
    return pl.pallas_call(
        functools.partial(early_kernel, count),
        out_shape=[jax.ShapeDtypeStruct((unit, width), FULL)] * count,
        in_specs=[SMEM] + [VMEM] * (2 * count),
        out_specs=[VMEM] * count,
        scratch_shapes=[pltpu.VMEM((unit, count * unit), HALF)],
        cost_estimate=pl.CostEstimate(
            flops=4 * (count * unit) ** 2 * width,
            bytes_accessed=8 * count * unit * width,
            transcendentals=(count * unit) ** 2,
        ),
        compiler_params=PARAMS,
    )(affine, *mine, *theirs)


def part_kernel(count, summed, n_after, affine, mine, *refs):
    theirs, refs = refs[:count], refs[count:]
    start = refs[0][...] if summed else None
    part, coupling = refs[-2:]
    part[...] = accumulate(affine, mine[...], theirs, coupling, start, False).astype(HALF)


def part_of(affine, mine, theirs, start, after):
    unit, width = mine.shape
    count = len(theirs)
    starts = [] if start is None else [start]
    return pl.pallas_call(
        functools.partial(part_kernel, count, len(starts), len(after)),
        out_shape=jax.ShapeDtypeStruct((unit, width), HALF),
        in_specs=[SMEM] + [VMEM] * (1 + count + len(starts)) + [ANY] * len(after),
        out_specs=VMEM,
        scratch_shapes=[pltpu.VMEM((unit, count * unit), HALF)],
        cost_estimate=pl.CostEstimate(
            flops=4 * count * unit**2 * width,
            bytes_accessed=2 * unit * width,
            transcendentals=count * unit**2,
        ),
        compiler_params=PARAMS,
    )(affine, mine, *theirs, *starts, *after)


def finish_kernel(core, multiplier, raw, *refs):
    parts, (here, there, grads) = refs[:-3], refs[-3:]
    rows = here.shape[0]
    total = parts[0][...].astype(FULL)
    for part in parts[1:]:
        total = total + part[...].astype(FULL)
    unit, scale = unit_rows(raw[...])
    grad = multiplier[0] * total
    grads[...] = scale * (grad - unit * jnp.sum(unit * grad, axis=1, keepdims=True))
    here[...] = grads[pl.ds(core[0] * rows, rows), :]
    there[...] = grads[pl.ds((1 - core[0]) * rows, rows), :]


def on_device(
    picture_vectors_raw, caption_vectors_raw, logit_multiplier, offset_term, incoming_adjoint
):
    rows, width = picture_vectors_raw.shape
    pairs = rows * math.prod(FINE_SIZES)
    core = lax.axis_index("core").astype(jnp.int32)
    is_first = core == 0
    affine = jnp.concatenate([0.5 * logit_multiplier, 0.5 * offset_term])
    multiplier = incoming_adjoint * logit_multiplier / pairs
    unit = jax.ShapeDtypeStruct((2 * rows, width), HALF)
    shard_full = jax.ShapeDtypeStruct((rows, width), FULL)

    raw, own, own_theirs = pl.pallas_call(
        normalize_kernel,
        out_shape=[unit] * 3,
        in_specs=[SMEM] + [VMEM] * 4,
        out_specs=[VMEM] * 3,
        compiler_params=PARAMS,
    )(
        is_first.astype(FULL).reshape(1),
        picture_vectors_raw,
        caption_vectors_raw,
        other_core(picture_vectors_raw),
        other_core(caption_vectors_raw),
    )

    mine, theirs = {(0, 0): own}, {(0, 0): own_theirs}
    for steps, across in reversed(WAYS):
        mine[steps, across] = sent(own, -steps, across)
        theirs[steps, across] = other_core(mine[steps, across])
    first = [(0, 0), *EARLY]
    second = [way for way in mine if way not in first]
    sums = early_sums(affine, [mine[w] for w in first], [theirs[w] for w in first])
    sums = dict(zip(first, sums, strict=True))

    arrived = []
    for k, way in enumerate((*WAYS, (0, 0))):
        after = arrived[k - 4 : k - 3] if k >= 4 else []
        if way in sums:
            part = part_of(affine, mine[way], [theirs[w] for w in second], sums[way], after)
        else:
            part = part_of(affine, mine[way], [theirs[w] for w in (*first, *second)], None, after)
        if way != (0, 0):
            arrived.append(sent(part, *way))

    here, there = pl.pallas_call(
        finish_kernel,
        out_shape=[shard_full, shard_full],
        in_specs=[SMEM, SMEM] + [VMEM] * (2 + len(arrived)),
        out_specs=[VMEM] * 2,
        scratch_shapes=[pltpu.VMEM((2 * rows, width), FULL)],
        compiler_params=PARAMS,
    )(core.reshape(1), multiplier, raw, part, *arrived)
    back = other_core(there)
    return (jnp.where(is_first, here, back), jnp.where(is_first, back, here))


def solution(mesh):
    fine = Mesh(mesh.devices.reshape(FINE_SIZES), FINE_AXES)
    rows = P(FINE_AXES, None)
    return jax.shard_map(
        on_device,
        mesh=fine,
        in_specs=(rows, rows, P(), P(), P()),
        out_specs=(rows, rows),
        check_vma=False,
    )
```

```python
import functools
import math

import jax
import jax.numpy as jnp
import numpy as np
from jax import lax
from jax.experimental import pallas as pl
from jax.experimental.pallas import tpu as pltpu
from jax.sharding import Mesh
from jax.sharding import PartitionSpec as P

FINE_AXES = ("y_lo", "core", "x", "z", "y_hi")
FINE_SIZES = (2, 2, 4, 4, 2)
RING = 4
VMEM_BYTES = 16 * 1024 * 1024
HALF = jnp.bfloat16
FULL = jnp.float32

VMEM = pl.BlockSpec(memory_space=pltpu.VMEM)
SMEM = pl.BlockSpec(memory_space=pltpu.SMEM)
ANY = pl.BlockSpec(memory_space=pl.ANY)
PARAMS = pltpu.CompilerParams(vmem_limit_bytes=VMEM_BYTES)

OWN, RIGHT, LEFT, FAR = (0, 0), (1, 0), (3, 0), (2, 0)
PARTNER, RIGHT_ACROSS, LEFT_ACROSS, FAR_ACROSS = (0, 1), (1, 1), (3, 1), (2, 1)


def place(core, x, y, z):
    return int(np.ravel_multi_index((y % 2, core, x, z, y // 2), FINE_SIZES))


def mate(core, y):
    if core == 0:
        return y ^ 1
    return (y + 1) % RING if y % 2 else (y - 1) % RING


def sent(value, steps, across):
    pairs = []
    for x, y, z in np.ndindex(RING, RING, RING):
        for core in range(2):
            to_y = mate(core, y) if across else y
            to_x = (x + steps) % RING if core == 0 else x
            to_z = (z + steps) % RING if core == 1 else z
            pairs.append((place(core, x, y, z), place(core, to_x, to_y, to_z)))
    return lax.ppermute(value, FINE_AXES, pairs)


def other_core(value):
    return lax.ppermute(value, "core", [(0, 1), (1, 0)])


def dot(a, b, contract):
    return lax.dot_general(a, b, ((contract[:1], contract[1:]), ((), ())), preferred_element_type=FULL)


def unit_rows(raw):
    values = raw.astype(FULL)
    scale = lax.rsqrt(jnp.mean(values * values, axis=1, keepdims=True) + 1e-06) / math.sqrt(
        values.shape[1]
    )
    return values * scale, scale


def normalize_kernel(is_first, *refs):
    sources, (raw, mine, theirs, held, sems) = refs[:4], refs[4:]
    rows = sources[0].shape[0]
    cut = rows // 4
    copies = []
    for k, source in enumerate(sources):
        for n in range(4):
            at = pl.ds(n * cut, cut)
            copies.append(pltpu.make_async_copy(source.at[at], held.at[k, at], sems.at[4 * k + n]))
    for copy in copies:
        copy.start()
    for copy in copies:
        copy.wait()
    first = is_first[0] > 0
    image, text, image_there, text_there = [held[k].astype(FULL) for k in range(4)]
    images, texts = (image, image_there), (text, text_there)
    for k in range(2):
        at = pl.ds(k * rows, rows)
        of_image = jnp.where(first, images[k], images[1 - k])
        of_text = jnp.where(first, texts[k], texts[1 - k])
        here = jnp.where(first, of_image, of_text)
        raw[at, :] = here.astype(HALF)
        mine[at, :] = unit_rows(here)[0].astype(HALF)
        theirs[at, :] = unit_rows(jnp.where(first, of_text, of_image))[0].astype(HALF)


def accumulate(affine, mine, theirs, coupling, start, diagonal):
    unit = mine.shape[0]
    for k, other in enumerate(theirs):
        energies = dot(mine, other[...], (1, 1))
        tile = 0.5 * jnp.tanh(affine[0] * energies + affine[1]) + 0.5
        if diagonal and k == 0:
            row = lax.broadcasted_iota(jnp.int32, tile.shape, 0)
            column = lax.broadcasted_iota(jnp.int32, tile.shape, 1)
            tile = tile - jnp.where(row == column, 1.0, 0.0)
        coupling[:, pl.ds(k * unit, unit)] = tile.astype(HALF)
    total = start
    for k, other in enumerate(theirs):
        term = dot(coupling[:, pl.ds(k * unit, unit)], other[...], (1, 0))
        total = term if total is None else total + term
    return total


def sums_kernel(count, n_theirs, summed, n_unread, diagonal, affine, *refs):
    mine, refs = refs[:count], refs[count:]
    theirs, refs = refs[:n_theirs], refs[n_theirs:]
    starts, refs = refs[: count * summed], refs[count * summed + n_unread :]
    sums, coupling = refs[:count], refs[-1]
    for k in range(count):
        start = starts[k][...] if summed else None
        sums[k][...] = accumulate(affine, mine[k][...], theirs, coupling, start, diagonal and k == 0)


def sums_of(affine, mine, theirs, starts=(), passed=(), after=(), diagonal=False):
    count, n_theirs = len(mine), len(theirs)
    before = 1 + count + n_theirs + len(starts)
    unit, width = mine[0].shape
    return pl.pallas_call(
        functools.partial(
            sums_kernel, count, n_theirs, bool(starts), len(passed) + len(after), diagonal
        ),
        out_shape=[jax.ShapeDtypeStruct((unit, width), FULL)] * count
        + [jax.ShapeDtypeStruct(array.shape, array.dtype) for array in passed],
        in_specs=[SMEM] + [VMEM] * (before - 1) + [ANY] * (len(passed) + len(after)),
        out_specs=[VMEM] * count + [ANY] * len(passed),
        input_output_aliases={before + k: count + k for k in range(len(passed))},
        scratch_shapes=[pltpu.VMEM((unit, n_theirs * unit), HALF)],
        cost_estimate=pl.CostEstimate(
            flops=4 * count * n_theirs * unit**2 * width,
            bytes_accessed=8 * count * unit * width,
            transcendentals=count * n_theirs * unit**2,
        ),
        compiler_params=PARAMS,
    )(affine, *mine, *theirs, *starts, *passed, *after)


def part_kernel(count, n_added, n_after, affine, mine, *refs):
    theirs, refs = refs[:count], refs[count:]
    start = None
    for ref in refs[:n_added]:
        start = ref[...].astype(FULL) if start is None else start + ref[...].astype(FULL)
    part, coupling = refs[-2:]
    part[...] = accumulate(affine, mine[...], theirs, coupling, start, False).astype(HALF)


def part_of(affine, mine, theirs, added=(), after=()):
    unit, width = mine.shape
    count = len(theirs)
    return pl.pallas_call(
        functools.partial(part_kernel, count, len(added), len(after)),
        out_shape=jax.ShapeDtypeStruct((unit, width), HALF),
        in_specs=[SMEM] + [VMEM] * (1 + count + len(added)) + [ANY] * len(after),
        out_specs=VMEM,
        scratch_shapes=[pltpu.VMEM((unit, count * unit), HALF)],
        cost_estimate=pl.CostEstimate(
            flops=4 * count * unit**2 * width,
            bytes_accessed=2 * unit * width,
            transcendentals=count * unit**2,
        ),
        compiler_params=PARAMS,
    )(affine, mine, *theirs, *added, *after)


def finish_kernel(core, multiplier, raw, *refs):
    parts, (here, there, grads) = refs[:-3], refs[-3:]
    rows = here.shape[0]
    total = parts[0][...].astype(FULL)
    for part in parts[1:]:
        total = total + part[...].astype(FULL)
    unit, scale = unit_rows(raw[...])
    grad = multiplier[0] * total
    grads[...] = scale * (grad - unit * jnp.sum(unit * grad, axis=1, keepdims=True))
    here[...] = grads[pl.ds(core[0] * rows, rows), :]
    there[...] = grads[pl.ds((1 - core[0]) * rows, rows), :]


def on_device(
    picture_vectors_raw, caption_vectors_raw, logit_multiplier, offset_term, incoming_adjoint
):
    rows, width = picture_vectors_raw.shape
    pairs = rows * math.prod(FINE_SIZES)
    core = lax.axis_index("core").astype(jnp.int32)
    is_first = core == 0
    affine = jnp.concatenate([0.5 * logit_multiplier, 0.5 * offset_term])
    multiplier = incoming_adjoint * logit_multiplier / pairs
    unit = jax.ShapeDtypeStruct((2 * rows, width), HALF)
    shard_full = jax.ShapeDtypeStruct((rows, width), FULL)

    raw, own, own_theirs = pl.pallas_call(
        normalize_kernel,
        out_shape=[unit] * 3,
        in_specs=[SMEM] + [ANY] * 4,
        out_specs=[VMEM] * 3,
        scratch_shapes=[
            pltpu.VMEM((4, rows, width), HALF),
            pltpu.SemaphoreType.DMA((16,)),
        ],
        compiler_params=PARAMS,
    )(
        is_first.astype(FULL).reshape(1),
        picture_vectors_raw,
        caption_vectors_raw,
        other_core(picture_vectors_raw),
        other_core(caption_vectors_raw),
    )

    mine = {OWN: own}
    for way in (RIGHT, LEFT, PARTNER, RIGHT_ACROSS, LEFT_ACROSS):
        mine[way] = sent(own, -way[0], way[1])
    mine[FAR] = sent(mine[RIGHT], -1, 0)
    mine[FAR_ACROSS] = sent(mine[LEFT_ACROSS], 1, 0)
    theirs = {OWN: own_theirs}
    for way in (RIGHT, LEFT, PARTNER, RIGHT_ACROSS, LEFT_ACROSS):
        theirs[way] = other_core(mine[way])

    def pick(units, ways):
        return [units[way] for way in ways]

    one, two, three = (OWN, RIGHT, LEFT), (PARTNER, RIGHT_ACROSS, LEFT_ACROSS), (FAR, FAR_ACROSS)
    sums = sums_of(affine, pick(mine, one), pick(theirs, one), diagonal=True)
    sums = sums_of(affine, pick(mine, one), pick(theirs, two), sums)
    sums += sums_of(affine, pick(mine, two[:1]), pick(theirs, one + two))
    *more, mine[FAR], mine[FAR_ACROSS] = sums_of(
        affine,
        pick(mine, two[1:]),
        pick(theirs, one + two),
        passed=pick(mine, three),
        after=[sums[0], sums[3]],
    )
    for way in three:
        theirs[way] = other_core(mine[way])
    sums = dict(zip(one + two, [*sums, *more], strict=True))

    def part(way, added=(), after=()):
        if way in three:
            return part_of(affine, mine[way], pick(theirs, one + two + three), added, after)
        return part_of(affine, mine[way], pick(theirs, three), [sums[way], *added], after)

    far = sent(part(FAR), 1, 0)
    far_across = sent(part(FAR_ACROSS), -1, 0)
    arrived = [sent(part(way), *way) for way in (RIGHT_ACROSS, PARTNER, LEFT)]
    arrived.append(sent(part(LEFT_ACROSS, [far_across]), *LEFT_ACROSS))
    arrived.append(sent(part(RIGHT, [far], arrived[:1]), *RIGHT))
    own_part = part(OWN, after=arrived[1:2])

    here, there = pl.pallas_call(
        finish_kernel,
        out_shape=[shard_full, shard_full],
        in_specs=[SMEM, SMEM] + [VMEM] * (2 + len(arrived)),
        out_specs=[VMEM] * 2,
        scratch_shapes=[pltpu.VMEM((2 * rows, width), FULL)],
        compiler_params=PARAMS,
    )(core.reshape(1), multiplier, raw, own_part, *arrived)
    back = other_core(there)
    return (jnp.where(is_first, here, back), jnp.where(is_first, back, here))


def solution(mesh):
    fine = Mesh(mesh.devices.reshape(FINE_SIZES), FINE_AXES)
    rows = P(FINE_AXES, None)
    return jax.shard_map(
        on_device,
        mesh=fine,
        in_specs=(rows, rows, P(), P(), P()),
        out_specs=(rows, rows),
        check_vma=False,
    )
```

```python
import functools
import math

import jax
import jax.numpy as jnp
import numpy as np
from jax import lax
from jax.experimental import pallas as pl
from jax.experimental.pallas import tpu as pltpu
from jax.sharding import Mesh
from jax.sharding import PartitionSpec as P

FINE_AXES = ("y_lo", "core", "x", "z", "y_hi")
FINE_SIZES = (2, 2, 4, 4, 2)
RING = 4
VMEM_BYTES = 16 * 1024 * 1024
HALF = jnp.bfloat16
FULL = jnp.float32

VMEM = pl.BlockSpec(memory_space=pltpu.VMEM)
SMEM = pl.BlockSpec(memory_space=pltpu.SMEM)
ANY = pl.BlockSpec(memory_space=pl.ANY)
PARAMS = pltpu.CompilerParams(vmem_limit_bytes=VMEM_BYTES)

ONE = ("x", "y", "z")
TWO = ("xyz", "xy", "yz", "zx")


def place(core, x, y, z):
    return int(np.ravel_multi_index((y % 2, core, x, z, y // 2), FINE_SIZES))


def mate(core, k):
    if core == 0:
        return k ^ 1
    return (k + 1) % RING if k % 2 else (k - 1) % RING


def sent(value, way):
    pairs = []
    for at in np.ndindex(RING, RING, RING):
        for core in range(2):
            to = [mate(core, k) if axis in way else k for axis, k in zip("xyz", at, strict=True)]
            pairs.append((place(core, *at), place(core, *to)))
    return lax.ppermute(value, FINE_AXES, pairs)


def other_core(value):
    return lax.ppermute(value, "core", [(0, 1), (1, 0)])


def dot(a, b, contract):
    return lax.dot_general(a, b, ((contract[:1], contract[1:]), ((), ())), preferred_element_type=FULL)


def unit_rows(raw):
    values = raw.astype(FULL)
    scale = lax.rsqrt(jnp.mean(values * values, axis=1, keepdims=True) + 1e-06) / math.sqrt(
        values.shape[1]
    )
    return values * scale, scale


def local(body, outs, scalars, arrays, after=()):
    n_scalars, n_arrays = len(scalars), len(arrays)

    def kernel(*refs):
        given = refs[: n_scalars + n_arrays]
        results = refs[n_scalars + n_arrays + len(after) :]
        for ref, value in zip(results, body(given[:n_scalars], given[n_scalars:]), strict=True):
            ref[...] = value.astype(ref.dtype)

    return pl.pallas_call(
        kernel,
        out_shape=[jax.ShapeDtypeStruct(s, d) for s, d in outs],
        in_specs=[SMEM] * n_scalars + [VMEM] * n_arrays + [ANY] * len(after),
        out_specs=[VMEM] * len(outs),
        compiler_params=PARAMS,
    )(*scalars, *arrays, *after)


def accumulate(affine, mine, theirs, coupling, start, diagonal):
    unit = mine.shape[0]
    pieces = [(ref, k) for ref in theirs for k in range(0, ref.shape[0], unit)]
    for n, (ref, k) in enumerate(pieces):
        energies = dot(mine, ref[pl.ds(k, unit), :], (1, 1))
        tile = 0.5 * jnp.tanh(affine[0] * energies + affine[1]) + 0.5
        if diagonal and n == 0:
            row = lax.broadcasted_iota(jnp.int32, tile.shape, 0)
            column = lax.broadcasted_iota(jnp.int32, tile.shape, 1)
            tile = tile - jnp.where(row == column, 1.0, 0.0)
        coupling[:, pl.ds(n * unit, unit)] = tile.astype(HALF)
    total, first = start, 0
    for ref in theirs:
        count = ref.shape[0]
        term = dot(coupling[:, pl.ds(first, count)], ref[...], (1, 0))
        total = term if total is None else total + term
        first += count
    return total


def sums_kernel(count, n_theirs, n_after, diagonal, affine, *refs):
    mine, theirs = refs[:count], refs[count : count + n_theirs]
    sums, coupling = refs[count + n_theirs + n_after : -1], refs[-1]
    for k in range(count):
        total = accumulate(affine, mine[k][...], theirs, coupling, None, diagonal and k == 0)
        sums[k][...] = total


def sums_of(affine, mine, theirs, after=(), diagonal=False):
    count, n_theirs, n_after = len(mine), len(theirs), len(after)
    unit, width = mine[0].shape
    against = sum(array.shape[0] for array in theirs)
    return pl.pallas_call(
        functools.partial(sums_kernel, count, n_theirs, n_after, diagonal),
        out_shape=[jax.ShapeDtypeStruct((unit, width), FULL)] * count,
        in_specs=[SMEM] + [VMEM] * (count + n_theirs) + [ANY] * n_after,
        out_specs=[VMEM] * count,
        scratch_shapes=[pltpu.VMEM((unit, against), HALF)],
        cost_estimate=pl.CostEstimate(
            flops=4 * count * unit * against * width,
            bytes_accessed=8 * count * unit * width,
            transcendentals=count * unit * against,
        ),
        compiler_params=PARAMS,
    )(affine, *mine, *theirs, *after)


def part_kernel(n_added, affine, mine, theirs, *refs):
    start = refs[0][...]
    for ref in refs[1:n_added]:
        start = start + ref[...].astype(FULL)
    part, coupling = refs[-2:]
    part[...] = accumulate(affine, mine[...], [theirs], coupling, start, False).astype(HALF)


def part_of(affine, mine, theirs, added):
    unit, width = mine.shape
    against = theirs.shape[0]
    return pl.pallas_call(
        functools.partial(part_kernel, len(added)),
        out_shape=jax.ShapeDtypeStruct((unit, width), HALF),
        in_specs=[SMEM] + [VMEM] * (2 + len(added)),
        out_specs=VMEM,
        scratch_shapes=[pltpu.VMEM((unit, against), HALF)],
        cost_estimate=pl.CostEstimate(
            flops=4 * unit * against * width,
            bytes_accessed=2 * unit * width,
            transcendentals=unit * against,
        ),
        compiler_params=PARAMS,
    )(affine, mine, theirs, *added)


def finish_kernel(core, multiplier, raw, *refs):
    parts, (here, there, grads) = refs[:-3], refs[-3:]
    rows = here.shape[0]
    total = parts[0][...].astype(FULL)
    for part in parts[1:]:
        total = total + part[...].astype(FULL)
    unit, scale = unit_rows(raw[...])
    grad = multiplier[0] * total
    grads[...] = scale * (grad - unit * jnp.sum(unit * grad, axis=1, keepdims=True))
    here[...] = grads[pl.ds(core[0] * rows, rows), :]
    there[...] = grads[pl.ds((1 - core[0]) * rows, rows), :]


def on_device(
    picture_vectors_raw, caption_vectors_raw, logit_multiplier, offset_term, incoming_adjoint
):
    rows, width = picture_vectors_raw.shape
    pairs = rows * math.prod(FINE_SIZES)
    core = lax.axis_index("core").astype(jnp.int32)
    is_first = core == 0
    first_flag = is_first.astype(FULL).reshape(1)
    affine = jnp.concatenate([0.5 * logit_multiplier, 0.5 * offset_term])
    multiplier = incoming_adjoint * logit_multiplier / pairs
    shard, unit = ((rows, width), HALF), ((2 * rows, width), HALF)
    shard_full = jax.ShapeDtypeStruct((rows, width), FULL)

    image_there = other_core(picture_vectors_raw)
    text_there = other_core(caption_vectors_raw)
    image, text, raw_here = local(
        lambda scalars, refs: [
            unit_rows(refs[0][...])[0],
            unit_rows(refs[1][...])[0],
            jnp.where(scalars[0][0] > 0, refs[0][...].astype(FULL), refs[1][...].astype(FULL)),
        ],
        [shard] * 3,
        [first_flag],
        [picture_vectors_raw, caption_vectors_raw],
    )

    def own_units(scalars, refs):
        first = scalars[0][0] > 0
        image_there, text_there, image, text, raw_here = [ref[...].astype(FULL) for ref in refs]
        raw_there = jnp.where(first, image_there, text_there)
        images, texts = (image, unit_rows(image_there)[0]), (text, unit_rows(text_there)[0])
        results = [[], [], []]
        for k in range(2):
            of_image = jnp.where(first, images[k], images[1 - k])
            of_text = jnp.where(first, texts[k], texts[1 - k])
            results[0].append(jnp.where(first, of_image, of_text))
            results[1].append(jnp.where(first, of_text, of_image))
            raws = (raw_here, raw_there)
            results[2].append(jnp.where(first, raws[k], raws[1 - k]))
        return [jnp.concatenate(halves, 0) for halves in results]

    own, own_theirs, raw = local(
        own_units, [unit] * 3, [first_flag], [image_there, text_there, image, text, raw_here]
    )

    def stacked(ways, after=()):
        (stack,) = local(
            lambda _, refs: [jnp.concatenate([ref[...] for ref in refs], 0)],
            [((2 * rows * len(ways), width), HALF)],
            [],
            [mine[way] for way in ways],
            after,
        )
        return other_core(stack)

    mine = {"": own}
    for way in ONE:
        mine[way] = sent(own, way)
    mine["xyz"] = sent(mine["x"], "yz")
    mine["xy"] = sent(mine["x"], "y")
    mine["yz"] = sent(mine["y"], "z")
    mine["zx"] = sent(mine["z"], "x")
    theirs_one = [own_theirs, stacked(ONE)]
    sums = sums_of(affine, [mine[way] for way in ("", *ONE)], theirs_one, diagonal=True)
    theirs_two = stacked(TWO, sums[:1])
    sums += sums_of(affine, [mine[way] for way in TWO], theirs_one)
    sums = dict(zip(("", *ONE, *TWO), sums, strict=True))

    def part(way, *added):
        return part_of(affine, mine[way], theirs_two, [sums[way], *added])

    for_x = [sent(part("xyz"), "yz"), sent(part("xy"), "y")]
    for_y = sent(part("yz"), "z")
    for_z = sent(part("zx"), "x")
    arrived = [
        sent(part("x", *for_x), "x"),
        sent(part("y", for_y), "y"),
        sent(part("z", for_z), "z"),
    ]
    own_part = part("")

    here, there = pl.pallas_call(
        finish_kernel,
        out_shape=[shard_full, shard_full],
        in_specs=[SMEM, SMEM] + [VMEM] * (2 + len(arrived)),
        out_specs=[VMEM] * 2,
        scratch_shapes=[pltpu.VMEM((2 * rows, width), FULL)],
        compiler_params=PARAMS,
    )(core.reshape(1), multiplier, raw, own_part, *arrived)
    back = other_core(there)
    return (jnp.where(is_first, here, back), jnp.where(is_first, back, here))


def solution(mesh):
    fine = Mesh(mesh.devices.reshape(FINE_SIZES), FINE_AXES)
    rows = P(FINE_AXES, None)
    return jax.shard_map(
        on_device,
        mesh=fine,
        in_specs=(rows, rows, P(), P(), P()),
        out_specs=(rows, rows),
        check_vma=False,
    )
```

```python
import functools
import math

import jax
import jax.numpy as jnp
import numpy as np
from jax import lax
from jax.experimental import pallas as pl
from jax.experimental.pallas import tpu as pltpu
from jax.sharding import Mesh
from jax.sharding import PartitionSpec as P

FINE_AXES = ("y_lo", "core", "x", "z", "y_hi")
FINE_SIZES = (2, 2, 4, 4, 2)
RING = 4
VMEM_BYTES = 16 * 1024 * 1024
HALF = jnp.bfloat16
FULL = jnp.float32

VMEM = pl.BlockSpec(memory_space=pltpu.VMEM)
SMEM = pl.BlockSpec(memory_space=pltpu.SMEM)
ANY = pl.BlockSpec(memory_space=pl.ANY)
PARAMS = pltpu.CompilerParams(vmem_limit_bytes=VMEM_BYTES)

ONE = ("x", "y", "z")
TWO = ("xyz", "xy", "yz", "zx")


def place(core, x, y, z):
    return int(np.ravel_multi_index((y % 2, core, x, z, y // 2), FINE_SIZES))


def mate(core, axis, k):
    if (core == 0) != (axis == "z"):
        return k ^ 1
    return (k + 1) % RING if k % 2 else (k - 1) % RING


def sent(value, way):
    pairs = []
    for at in np.ndindex(RING, RING, RING):
        for core in range(2):
            to = [mate(core, axis, k) if axis in way else k for axis, k in zip("xyz", at, strict=True)]
            pairs.append((place(core, *at), place(core, *to)))
    return lax.ppermute(value, FINE_AXES, pairs)


def other_core(value):
    return lax.ppermute(value, "core", [(0, 1), (1, 0)])


def dot(a, b, contract):
    return lax.dot_general(a, b, ((contract[:1], contract[1:]), ((), ())), preferred_element_type=FULL)


def unit_rows(raw):
    values = raw.astype(FULL)
    scale = lax.rsqrt(jnp.mean(values * values, axis=1, keepdims=True) + 1e-06) / math.sqrt(
        values.shape[1]
    )
    return values * scale, scale


def local(body, outs, scalars, arrays, after=()):
    n_scalars, n_arrays = len(scalars), len(arrays)

    def kernel(*refs):
        given = refs[: n_scalars + n_arrays]
        results = refs[n_scalars + n_arrays + len(after) :]
        for ref, value in zip(results, body(given[:n_scalars], given[n_scalars:]), strict=True):
            ref[...] = value.astype(ref.dtype)

    return pl.pallas_call(
        kernel,
        out_shape=[jax.ShapeDtypeStruct(s, d) for s, d in outs],
        in_specs=[SMEM] * n_scalars + [VMEM] * n_arrays + [ANY] * len(after),
        out_specs=[VMEM] * len(outs),
        compiler_params=PARAMS,
    )(*scalars, *arrays, *after)


def accumulate(affine, mine, theirs, coupling, start, diagonal):
    unit = mine.shape[0]
    pieces = [(ref, k) for ref in theirs for k in range(0, ref.shape[0], unit)]
    for n, (ref, k) in enumerate(pieces):
        energies = dot(mine, ref[pl.ds(k, unit), :], (1, 1))
        tile = 0.5 * jnp.tanh(affine[0] * energies + affine[1]) + 0.5
        if diagonal and n == 0:
            row = lax.broadcasted_iota(jnp.int32, tile.shape, 0)
            column = lax.broadcasted_iota(jnp.int32, tile.shape, 1)
            tile = tile - jnp.where(row == column, 1.0, 0.0)
        coupling[:, pl.ds(n * unit, unit)] = tile.astype(HALF)
    total, first = start, 0
    for ref in theirs:
        count = ref.shape[0]
        term = dot(coupling[:, pl.ds(first, count)], ref[...], (1, 0))
        total = term if total is None else total + term
        first += count
    return total


def sums_kernel(count, n_theirs, n_starts, n_after, diagonal, affine, *refs):
    mine, refs = refs[:count], refs[count:]
    theirs, refs = refs[:n_theirs], refs[n_theirs:]
    starts, refs = refs[:n_starts], refs[n_starts + n_after :]
    sums, coupling = refs[:-1], refs[-1]
    for k in range(count):
        start = starts[k][...] if starts else None
        total = accumulate(affine, mine[k][...], theirs, coupling, start, diagonal and k == 0)
        sums[k][...] = total.astype(sums[k].dtype)


def sums_of(affine, mine, theirs, starts=(), after=(), kinds=None, diagonal=False, hides=True):
    count, n_theirs, n_starts, n_after = len(mine), len(theirs), len(starts), len(after)
    unit, width = mine[0].shape
    against = sum(array.shape[0] for array in theirs)
    kinds = kinds or [FULL] * count
    return pl.pallas_call(
        functools.partial(sums_kernel, count, n_theirs, n_starts, n_after, diagonal),
        out_shape=[jax.ShapeDtypeStruct((unit, width), kind) for kind in kinds],
        in_specs=[SMEM] + [VMEM] * (count + n_theirs + n_starts) + [ANY] * n_after,
        out_specs=[VMEM] * count,
        scratch_shapes=[pltpu.VMEM((unit, against), HALF)],
        cost_estimate=pl.CostEstimate(
            flops=4 * count * unit * against * width if hides else 0,
            bytes_accessed=8 * count * unit * width if hides else 0,
            transcendentals=count * unit * against if hides else 0,
        ),
        compiler_params=PARAMS,
    )(affine, *mine, *theirs, *starts, *after)


def finish_kernel(core, multiplier, raw, *refs):
    parts, (here, there, grads) = refs[:-3], refs[-3:]
    rows = here.shape[0]
    total = parts[0][...].astype(FULL)
    for part in parts[1:]:
        total = total + part[...].astype(FULL)
    unit, scale = unit_rows(raw[...])
    grad = multiplier[0] * total
    grads[...] = scale * (grad - unit * jnp.sum(unit * grad, axis=1, keepdims=True))
    here[...] = grads[pl.ds(core[0] * rows, rows), :]
    there[...] = grads[pl.ds((1 - core[0]) * rows, rows), :]


def on_device(
    picture_vectors_raw, caption_vectors_raw, logit_multiplier, offset_term, incoming_adjoint
):
    rows, width = picture_vectors_raw.shape
    pairs = rows * math.prod(FINE_SIZES)
    core = lax.axis_index("core").astype(jnp.int32)
    is_first = core == 0
    first_flag = is_first.astype(FULL).reshape(1)
    affine = jnp.concatenate([0.5 * logit_multiplier, 0.5 * offset_term])
    multiplier = incoming_adjoint * logit_multiplier / pairs
    shard, unit = ((rows, width), HALF), ((2 * rows, width), HALF)
    shard_full = jax.ShapeDtypeStruct((rows, width), FULL)

    image_there = other_core(picture_vectors_raw)
    text_there = other_core(caption_vectors_raw)
    image, text, raw_here = local(
        lambda scalars, refs: [
            unit_rows(refs[0][...])[0],
            unit_rows(refs[1][...])[0],
            jnp.where(scalars[0][0] > 0, refs[0][...].astype(FULL), refs[1][...].astype(FULL)),
        ],
        [shard] * 3,
        [first_flag],
        [picture_vectors_raw, caption_vectors_raw],
    )

    def own_units(scalars, refs):
        first = scalars[0][0] > 0
        image_there, text_there, image, text, raw_here = [ref[...].astype(FULL) for ref in refs]
        raw_there = jnp.where(first, image_there, text_there)
        images, texts = (image, unit_rows(image_there)[0]), (text, unit_rows(text_there)[0])
        results = [[], [], []]
        for k in range(2):
            of_image = jnp.where(first, images[k], images[1 - k])
            of_text = jnp.where(first, texts[k], texts[1 - k])
            results[0].append(jnp.where(first, of_image, of_text))
            results[1].append(jnp.where(first, of_text, of_image))
            raws = (raw_here, raw_there)
            results[2].append(jnp.where(first, raws[k], raws[1 - k]))
        return [jnp.concatenate(halves, 0) for halves in results]

    own, own_theirs, raw = local(
        own_units, [unit] * 3, [first_flag], [image_there, text_there, image, text, raw_here]
    )

    def stacked(ways, after=()):
        (stack,) = local(
            lambda _, refs: [jnp.concatenate([ref[...] for ref in refs], 0)],
            [((2 * rows * len(ways), width), HALF)],
            [],
            [mine[way] for way in ways],
            after,
        )
        return other_core(stack)

    mine = {"": own}
    for way in ONE:
        mine[way] = sent(own, way)
    mine["xyz"] = sent(mine["x"], "yz")
    mine["xy"] = sent(mine["x"], "y")
    mine["yz"] = sent(mine["y"], "z")
    mine["zx"] = sent(mine["z"], "x")
    def pick(units, ways):
        return [units[way] for way in ways]

    theirs_one = [own_theirs, stacked(ONE)]
    near = ("", *ONE)
    sums = sums_of(affine, pick(mine, near), theirs_one, diagonal=True, hides=False)
    theirs_two = [stacked(TWO, sums[:1])]
    sums += sums_of(affine, pick(mine, TWO), theirs_one)
    sums = dict(zip((*near, *TWO), sums, strict=True))

    def parts_of(ways, kinds, after=()):
        return sums_of(affine, pick(mine, ways), theirs_two, pick(sums, ways), after, kinds)

    part_xyz, part_xy = parts_of(("xyz", "xy"), [HALF, HALF])
    for_x = [sent(part_xyz, "yz"), sent(part_xy, "y")]
    part_yz, part_zx = parts_of(("yz", "zx"), [HALF, HALF], [part_xy])
    for_y = [sent(part_yz, "z")]
    for_z = [sent(part_zx, "x")]
    own_part, part_x, part_y, part_z = parts_of(near, [FULL] * 4, [part_zx])

    def with_added(part, added, way):
        (total,) = local(
            lambda _, refs: [sum([ref[...].astype(FULL) for ref in refs[1:]], refs[0][...])],
            [unit],
            [],
            [part, *added],
        )
        return sent(total, way)

    arrived = [
        with_added(part_x, for_x, "x"),
        with_added(part_y, for_y, "y"),
        with_added(part_z, for_z, "z"),
    ]

    here, there = pl.pallas_call(
        finish_kernel,
        out_shape=[shard_full, shard_full],
        in_specs=[SMEM, SMEM] + [VMEM] * (2 + len(arrived)),
        out_specs=[VMEM] * 2,
        scratch_shapes=[pltpu.VMEM((2 * rows, width), FULL)],
        compiler_params=PARAMS,
    )(core.reshape(1), multiplier, raw, own_part, *arrived)
    back = other_core(there)
    return (jnp.where(is_first, here, back), jnp.where(is_first, back, here))


def solution(mesh):
    fine = Mesh(mesh.devices.reshape(FINE_SIZES), FINE_AXES)
    rows = P(FINE_AXES, None)
    return jax.shard_map(
        on_device,
        mesh=fine,
        in_specs=(rows, rows, P(), P(), P()),
        out_specs=(rows, rows),
        check_vma=False,
    )
```

```python
import functools
import math

import jax
import jax.numpy as jnp
import numpy as np
from jax import lax
from jax.experimental import pallas as pl
from jax.experimental.pallas import tpu as pltpu
from jax.sharding import Mesh
from jax.sharding import PartitionSpec as P

FINE_AXES = ("y_lo", "core", "x", "z", "y_hi")
FINE_SIZES = (2, 2, 4, 4, 2)
RING = 4
VMEM_BYTES = 16 * 1024 * 1024
WIDE_VMEM_BYTES = 56 * 1024 * 1024
CUTS = 4
HALF = jnp.bfloat16
FULL = jnp.float32

VMEM = pl.BlockSpec(memory_space=pltpu.VMEM)
SMEM = pl.BlockSpec(memory_space=pltpu.SMEM)
ANY = pl.BlockSpec(memory_space=pl.ANY)
PARAMS = pltpu.CompilerParams(vmem_limit_bytes=VMEM_BYTES)

ONE = ("x", "y", "z")
TWO = ("xy", "yz", "zx")
CORNER = "xyz"


def place(core, x, y, z):
    return int(np.ravel_multi_index((y % 2, core, x, z, y // 2), FINE_SIZES))


def mate(core, axis, k):
    if (core == 0) != (axis == "z"):
        return k ^ 1
    return (k + 1) % RING if k % 2 else (k - 1) % RING


def sent(value, way):
    pairs = []
    for at in np.ndindex(RING, RING, RING):
        for core in range(2):
            to = [mate(core, axis, k) if axis in way else k for axis, k in zip("xyz", at, strict=True)]
            pairs.append((place(core, *at), place(core, *to)))
    return lax.ppermute(value, FINE_AXES, pairs)


def other_core(value):
    return lax.ppermute(value, "core", [(0, 1), (1, 0)])


def dot(a, b, contract):
    return lax.dot_general(a, b, ((contract[:1], contract[1:]), ((), ())), preferred_element_type=FULL)


def unit_rows(raw):
    values = raw.astype(FULL)
    scale = lax.rsqrt(jnp.mean(values * values, axis=1, keepdims=True) + 1e-06) / math.sqrt(
        values.shape[1]
    )
    return values * scale, scale


def local(body, outs, scalars, arrays, after=()):
    n_scalars, n_arrays = len(scalars), len(arrays)

    def kernel(*refs):
        given = refs[: n_scalars + n_arrays]
        results = refs[n_scalars + n_arrays + len(after) :]
        for ref, value in zip(results, body(given[:n_scalars], given[n_scalars:]), strict=True):
            ref[...] = value.astype(ref.dtype)

    return pl.pallas_call(
        kernel,
        out_shape=[jax.ShapeDtypeStruct(s, d) for s, d in outs],
        in_specs=[SMEM] * n_scalars + [VMEM] * n_arrays + [ANY] * len(after),
        out_specs=[VMEM] * len(outs),
        compiler_params=PARAMS,
    )(*scalars, *arrays, *after)


def accumulate(affine, mine, theirs, coupling, start, diagonal):
    unit = mine.shape[0]
    pieces = [(ref, k) for ref in theirs for k in range(0, ref.shape[0], unit)]
    for n, (ref, k) in enumerate(pieces):
        energies = dot(mine, ref[pl.ds(k, unit), :], (1, 1))
        tile = 0.5 * jnp.tanh(affine[0] * energies + affine[1]) + 0.5
        if diagonal and n == 0:
            row = lax.broadcasted_iota(jnp.int32, tile.shape, 0)
            column = lax.broadcasted_iota(jnp.int32, tile.shape, 1)
            tile = tile - jnp.where(row == column, 1.0, 0.0)
        coupling[:, pl.ds(n * unit, unit)] = tile.astype(HALF)
    total, first = start, 0
    for ref in theirs:
        count = ref.shape[0]
        term = dot(coupling[:, pl.ds(first, count)], ref[...], (1, 0))
        total = term if total is None else total + term
        first += count
    return total


def sums_kernel(count, n_theirs, n_starts, n_after, diagonal, affine, *refs):
    mine, refs = refs[:count], refs[count:]
    theirs, refs = refs[:n_theirs], refs[n_theirs:]
    starts, refs = refs[:n_starts], refs[n_starts + n_after :]
    sums, coupling = refs[:-1], refs[-1]
    for k in range(count):
        start = starts[k][...] if starts else None
        total = accumulate(affine, mine[k][...], theirs, coupling, start, diagonal and k == 0)
        sums[k][...] = total.astype(sums[k].dtype)


def sums_of(affine, mine, theirs, starts=(), after=(), kinds=None, diagonal=False, hides=True):
    count, n_theirs, n_starts, n_after = len(mine), len(theirs), len(starts), len(after)
    unit, width = mine[0].shape
    against = sum(array.shape[0] for array in theirs)
    kinds = kinds or [FULL] * count
    return pl.pallas_call(
        functools.partial(sums_kernel, count, n_theirs, n_starts, n_after, diagonal),
        out_shape=[jax.ShapeDtypeStruct((unit, width), kind) for kind in kinds],
        in_specs=[SMEM] + [VMEM] * (count + n_theirs + n_starts) + [ANY] * n_after,
        out_specs=[VMEM] * count,
        scratch_shapes=[pltpu.VMEM((unit, against), HALF)],
        cost_estimate=pl.CostEstimate(
            flops=4 * count * unit * against * width if hides else 0,
            bytes_accessed=8 * count * unit * width if hides else 0,
            transcendentals=count * unit * against if hides else 0,
        ),
        compiler_params=PARAMS,
    )(affine, *mine, *theirs, *starts, *after)


def cut_copies(pairs, sems):
    copies = []
    for source, target in pairs:
        rows = source.shape[0] // CUTS
        for k in range(CUTS):
            at = pl.ds(k * rows, rows)
            copies.append(pltpu.make_async_copy(source.at[at], target.at[at], sems.at[len(copies)]))
    return copies


def first_kernel(is_first, image_raw, text_raw, image, text, raw_here, held, sems):
    copies = cut_copies([(image_raw, held.at[0]), (text_raw, held.at[1])], sems)
    for copy in copies:
        copy.start()
    for copy in copies:
        copy.wait()
    images, texts = held[0].astype(FULL), held[1].astype(FULL)
    image[...] = unit_rows(images)[0].astype(HALF)
    text[...] = unit_rows(texts)[0].astype(HALF)
    raw_here[...] = jnp.where(is_first[0] > 0, images, texts).astype(HALF)


def last_kernel(core, here, back, image_grad, text_grad, sems):
    for mine, theirs, which in ((image_grad, text_grad, 0), (text_grad, image_grad, 1)):

        @pl.when(core[0] == which)
        def _(mine=mine, theirs=theirs):
            copies = cut_copies([(here, mine), (back, theirs)], sems)
            for copy in copies:
                copy.start()
            for copy in copies:
                copy.wait()


def finish_kernel(core, multiplier, raw, *refs):
    parts, (here, there, grads) = refs[:-3], refs[-3:]
    rows = here.shape[0]
    total = parts[0][...].astype(FULL)
    for part in parts[1:]:
        total = total + part[...].astype(FULL)
    unit, scale = unit_rows(raw[...])
    grad = multiplier[0] * total
    grads[...] = scale * (grad - unit * jnp.sum(unit * grad, axis=1, keepdims=True))
    here[...] = grads[pl.ds(core[0] * rows, rows), :]
    there[...] = grads[pl.ds((1 - core[0]) * rows, rows), :]


def on_device(
    picture_vectors_raw, caption_vectors_raw, logit_multiplier, offset_term, incoming_adjoint
):
    rows, width = picture_vectors_raw.shape
    pairs = rows * math.prod(FINE_SIZES)
    core = lax.axis_index("core").astype(jnp.int32)
    is_first = core == 0
    first_flag = is_first.astype(FULL).reshape(1)
    affine = jnp.concatenate([0.5 * logit_multiplier, 0.5 * offset_term])
    multiplier = incoming_adjoint * logit_multiplier / pairs
    shard, unit = ((rows, width), HALF), ((2 * rows, width), HALF)
    shard_full = jax.ShapeDtypeStruct((rows, width), FULL)

    image_there = other_core(picture_vectors_raw)
    text_there = other_core(caption_vectors_raw)
    image, text, raw_here = pl.pallas_call(
        first_kernel,
        out_shape=[jax.ShapeDtypeStruct(*shard)] * 3,
        in_specs=[SMEM, ANY, ANY],
        out_specs=[VMEM] * 3,
        scratch_shapes=[pltpu.VMEM((2, rows, width), HALF), pltpu.SemaphoreType.DMA((2 * CUTS,))],
        compiler_params=pltpu.CompilerParams(vmem_limit_bytes=WIDE_VMEM_BYTES),
    )(first_flag, picture_vectors_raw, caption_vectors_raw)

    def own_units(scalars, refs):
        first = scalars[0][0] > 0
        image_there, text_there, image, text, raw_here = [ref[...].astype(FULL) for ref in refs]
        raw_there = jnp.where(first, image_there, text_there)
        images, texts = (image, unit_rows(image_there)[0]), (text, unit_rows(text_there)[0])
        results = [[], [], []]
        for k in range(2):
            of_image = jnp.where(first, images[k], images[1 - k])
            of_text = jnp.where(first, texts[k], texts[1 - k])
            results[0].append(jnp.where(first, of_image, of_text))
            results[1].append(jnp.where(first, of_text, of_image))
            raws = (raw_here, raw_there)
            results[2].append(jnp.where(first, raws[k], raws[1 - k]))
        return [jnp.concatenate(halves, 0) for halves in results]

    own, own_theirs, raw = local(
        own_units, [unit] * 3, [first_flag], [image_there, text_there, image, text, raw_here]
    )

    def stacked(ways, after=()):
        (stack,) = local(
            lambda _, refs: [jnp.concatenate([ref[...] for ref in refs], 0)],
            [((2 * rows * len(ways), width), HALF)],
            [],
            [mine[way] for way in ways],
            after,
        )
        return other_core(stack)

    mine = {"": own}
    for way in ONE:
        mine[way] = sent(own, way)
    mine["xy"] = sent(mine["x"], "y")
    mine["yz"] = sent(mine["y"], "z")
    mine["zx"] = sent(mine["z"], "x")
    def pick(units, ways):
        return [units[way] for way in ways]

    mine[CORNER] = sent(mine["xy"], "z")

    def pick(units, ways):
        return [units[way] for way in ways]

    theirs_one = [own_theirs, stacked(ONE)]
    near = ("", *ONE)
    sums_near = sums_of(affine, pick(mine, near), theirs_one, diagonal=True, hides=False)
    theirs_two = [stacked(TWO, sums_near[:1])]
    sums_two = sums_of(affine, pick(mine, TWO), theirs_one)
    sums_two = sums_of(affine, pick(mine, TWO), theirs_two, sums_two)
    theirs_corner = [stacked([CORNER], sums_two[:1])]
    sums_corner = sums_of(affine, [mine[CORNER]], theirs_one + theirs_two, after=sums_two[:1])

    far = (CORNER, *TWO)
    part_xyz, part_xy, part_yz, part_zx = sums_of(
        affine, pick(mine, far), theirs_corner, [*sums_corner, *sums_two], kinds=[HALF] * 4
    )
    for_x = [sent(part_xyz, "yz"), sent(part_xy, "y")]
    for_y = [sent(part_yz, "z")]
    for_z = [sent(part_zx, "x")]
    own_part, part_x, part_y, part_z = sums_of(
        affine, pick(mine, near), theirs_two + theirs_corner, sums_near, after=[part_xyz]
    )

    def with_added(part, added, way):
        (total,) = local(
            lambda _, refs: [sum([ref[...].astype(FULL) for ref in refs[1:]], refs[0][...])],
            [unit],
            [],
            [part, *added],
        )
        return sent(total, way)

    arrived = [
        with_added(part_x, for_x, "x"),
        with_added(part_y, for_y, "y"),
        with_added(part_z, for_z, "z"),
    ]

    here, there = pl.pallas_call(
        finish_kernel,
        out_shape=[shard_full, shard_full],
        in_specs=[SMEM, SMEM] + [VMEM] * (2 + len(arrived)),
        out_specs=[VMEM] * 2,
        scratch_shapes=[pltpu.VMEM((2 * rows, width), FULL)],
        compiler_params=PARAMS,
    )(core.reshape(1), multiplier, raw, own_part, *arrived)
    back = other_core(there)
    return tuple(
        pl.pallas_call(
            last_kernel,
            out_shape=[shard_full] * 2,
            in_specs=[SMEM, VMEM, VMEM],
            out_specs=[ANY] * 2,
            scratch_shapes=[pltpu.SemaphoreType.DMA((2 * CUTS,))],
            compiler_params=PARAMS,
        )(core.reshape(1), here, back)
    )


def solution(mesh):
    fine = Mesh(mesh.devices.reshape(FINE_SIZES), FINE_AXES)
    rows = P(FINE_AXES, None)
    return jax.shard_map(
        on_device,
        mesh=fine,
        in_specs=(rows, rows, P(), P(), P()),
        out_specs=(rows, rows),
        check_vma=False,
    )
```

```python
import functools
import math

import jax
import jax.numpy as jnp
import numpy as np
from jax import lax
from jax.experimental import pallas as pl
from jax.experimental.pallas import tpu as pltpu
from jax.sharding import Mesh
from jax.sharding import PartitionSpec as P

FINE_AXES = ("y_lo", "core", "x", "z", "y_hi")
FINE_SIZES = (2, 2, 4, 4, 2)
RING = 4
VMEM_BYTES = 16 * 1024 * 1024
HALF = jnp.bfloat16
FULL = jnp.float32

VMEM = pl.BlockSpec(memory_space=pltpu.VMEM)
SMEM = pl.BlockSpec(memory_space=pltpu.SMEM)
ANY = pl.BlockSpec(memory_space=pl.ANY)
PARAMS = pltpu.CompilerParams(vmem_limit_bytes=VMEM_BYTES)

ONE = ("x", "y", "z")
TWO = ("xy", "yz", "zx")
CORNER = "xyz"


def place(core, x, y, z):
    return int(np.ravel_multi_index((y % 2, core, x, z, y // 2), FINE_SIZES))


def mate(core, axis, k):
    if (core == 0) != (axis == "z"):
        return k ^ 1
    return (k + 1) % RING if k % 2 else (k - 1) % RING


def sent(value, way):
    pairs = []
    for at in np.ndindex(RING, RING, RING):
        for core in range(2):
            to = [mate(core, axis, k) if axis in way else k for axis, k in zip("xyz", at, strict=True)]
            pairs.append((place(core, *at), place(core, *to)))
    return lax.ppermute(value, FINE_AXES, pairs)


def other_core(value):
    return lax.ppermute(value, "core", [(0, 1), (1, 0)])


def dot(a, b, contract):
    return lax.dot_general(a, b, ((contract[:1], contract[1:]), ((), ())), preferred_element_type=FULL)


def unit_rows(raw):
    values = raw.astype(FULL)
    scale = lax.rsqrt(jnp.mean(values * values, axis=1, keepdims=True) + 1e-06) / math.sqrt(
        values.shape[1]
    )
    return values * scale, scale


def local(body, outs, scalars, arrays, after=()):
    n_scalars, n_arrays = len(scalars), len(arrays)

    def kernel(*refs):
        given = refs[: n_scalars + n_arrays]
        results = refs[n_scalars + n_arrays + len(after) :]
        for ref, value in zip(results, body(given[:n_scalars], given[n_scalars:]), strict=True):
            ref[...] = value.astype(ref.dtype)

    return pl.pallas_call(
        kernel,
        out_shape=[jax.ShapeDtypeStruct(s, d) for s, d in outs],
        in_specs=[SMEM] * n_scalars + [VMEM] * n_arrays + [ANY] * len(after),
        out_specs=[VMEM] * len(outs),
        compiler_params=PARAMS,
    )(*scalars, *arrays, *after)


def accumulate(affine, mine, theirs, coupling, start, diagonal):
    unit = mine.shape[0]
    pieces = [(ref, k) for ref in theirs for k in range(0, ref.shape[0], unit)]
    for n, (ref, k) in enumerate(pieces):
        energies = dot(mine, ref[pl.ds(k, unit), :], (1, 1))
        tile = 0.5 * jnp.tanh(affine[0] * energies + affine[1]) + 0.5
        if diagonal and n == 0:
            row = lax.broadcasted_iota(jnp.int32, tile.shape, 0)
            column = lax.broadcasted_iota(jnp.int32, tile.shape, 1)
            tile = tile - jnp.where(row == column, 1.0, 0.0)
        coupling[:, pl.ds(n * unit, unit)] = tile.astype(HALF)
    total, first = start, 0
    for ref in theirs:
        count = ref.shape[0]
        term = dot(coupling[:, pl.ds(first, count)], ref[...], (1, 0))
        total = term if total is None else total + term
        first += count
    return total


def sums_kernel(count, n_theirs, n_starts, n_after, diagonal, affine, *refs):
    mine, refs = refs[:count], refs[count:]
    theirs, refs = refs[:n_theirs], refs[n_theirs:]
    starts, refs = refs[:n_starts], refs[n_starts + n_after :]
    sums, coupling = refs[:-1], refs[-1]
    for k in range(count):
        start = starts[k][...] if starts else None
        total = accumulate(affine, mine[k][...], theirs, coupling, start, diagonal and k == 0)
        sums[k][...] = total.astype(sums[k].dtype)


def sums_of(affine, mine, theirs, starts=(), after=(), kinds=None, diagonal=False, hides=True):
    count, n_theirs, n_starts, n_after = len(mine), len(theirs), len(starts), len(after)
    unit, width = mine[0].shape
    against = sum(array.shape[0] for array in theirs)
    kinds = kinds or [FULL] * count
    return pl.pallas_call(
        functools.partial(sums_kernel, count, n_theirs, n_starts, n_after, diagonal),
        out_shape=[jax.ShapeDtypeStruct((unit, width), kind) for kind in kinds],
        in_specs=[SMEM] + [VMEM] * (count + n_theirs + n_starts) + [ANY] * n_after,
        out_specs=[VMEM] * count,
        scratch_shapes=[pltpu.VMEM((unit, against), HALF)],
        cost_estimate=pl.CostEstimate(
            flops=4 * count * unit * against * width if hides else 0,
            bytes_accessed=8 * count * unit * width if hides else 0,
            transcendentals=count * unit * against if hides else 0,
        ),
        compiler_params=PARAMS,
    )(affine, *mine, *theirs, *starts, *after)


def finish_kernel(core, multiplier, raw, *refs):
    parts, (here, there, grads) = refs[:-3], refs[-3:]
    rows = here.shape[0]
    total = parts[0][...].astype(FULL)
    for part in parts[1:]:
        total = total + part[...].astype(FULL)
    unit, scale = unit_rows(raw[...])
    grad = multiplier[0] * total
    grads[...] = scale * (grad - unit * jnp.sum(unit * grad, axis=1, keepdims=True))
    here[...] = grads[pl.ds(core[0] * rows, rows), :]
    there[...] = grads[pl.ds((1 - core[0]) * rows, rows), :]


def on_device(
    picture_vectors_raw, caption_vectors_raw, logit_multiplier, offset_term, incoming_adjoint
):
    rows, width = picture_vectors_raw.shape
    pairs = rows * math.prod(FINE_SIZES)
    core = lax.axis_index("core").astype(jnp.int32)
    is_first = core == 0
    first_flag = is_first.astype(FULL).reshape(1)
    affine = jnp.concatenate([0.5 * logit_multiplier, 0.5 * offset_term])
    multiplier = incoming_adjoint * logit_multiplier / pairs
    shard, unit = ((rows, width), HALF), ((2 * rows, width), HALF)
    shard_full = jax.ShapeDtypeStruct((rows, width), FULL)

    image_there = other_core(picture_vectors_raw)
    text_there = other_core(caption_vectors_raw)
    image, text, raw_here = local(
        lambda scalars, refs: [
            unit_rows(refs[0][...])[0],
            unit_rows(refs[1][...])[0],
            jnp.where(scalars[0][0] > 0, refs[0][...].astype(FULL), refs[1][...].astype(FULL)),
        ],
        [shard] * 3,
        [first_flag],
        [picture_vectors_raw, caption_vectors_raw],
    )

    def own_units(scalars, refs):
        first = scalars[0][0] > 0
        image_there, text_there, image, text, raw_here = [ref[...].astype(FULL) for ref in refs]
        raw_there = jnp.where(first, image_there, text_there)
        images, texts = (image, unit_rows(image_there)[0]), (text, unit_rows(text_there)[0])
        results = [[], [], []]
        for k in range(2):
            of_image = jnp.where(first, images[k], images[1 - k])
            of_text = jnp.where(first, texts[k], texts[1 - k])
            results[0].append(jnp.where(first, of_image, of_text))
            results[1].append(jnp.where(first, of_text, of_image))
            raws = (raw_here, raw_there)
            results[2].append(jnp.where(first, raws[k], raws[1 - k]))
        return [jnp.concatenate(halves, 0) for halves in results]

    own, own_theirs, raw = local(
        own_units, [unit] * 3, [first_flag], [image_there, text_there, image, text, raw_here]
    )

    def stacked(ways, after=()):
        (stack,) = local(
            lambda _, refs: [jnp.concatenate([ref[...] for ref in refs], 0)],
            [((2 * rows * len(ways), width), HALF)],
            [],
            [mine[way] for way in ways],
            after,
        )
        return other_core(stack)

    mine = {"": own}
    for way in ONE:
        mine[way] = sent(own, way)
    mine[CORNER] = sent(own, CORNER)
    mine["xy"] = sent(mine["x"], "y")
    mine["yz"] = sent(mine["y"], "z")
    mine["zx"] = sent(mine["z"], "x")
    def pick(units, ways):
        return [units[way] for way in ways]

    first = (*ONE, CORNER)
    theirs_one = [own_theirs, stacked(first)]
    *sums_near, sum_corner = sums_of(
        affine, pick(mine, ("", *first)), theirs_one, diagonal=True, hides=False
    )
    theirs_two = [stacked(TWO, sums_near[:1])]
    sums_two = sums_of(affine, pick(mine, TWO), theirs_one)

    part_xy, part_yz, part_zx = sums_of(
        affine, pick(mine, TWO), theirs_two, sums_two, kinds=[HALF] * 3
    )
    for_x, for_y, for_z = sent(part_xy, "y"), sent(part_yz, "z"), sent(part_zx, "x")
    (part_xyz,) = sums_of(
        affine, [mine[CORNER]], theirs_two, [sum_corner], after=[part_xy], kinds=[HALF]
    )
    arrived = [sent(part_xyz, CORNER)]
    part_x, part_y, part_z = sums_of(
        affine, pick(mine, ONE), theirs_two, sums_near[1:], after=[part_xyz]
    )

    def with_added(part, added, way):
        (total,) = local(
            lambda _, refs: [sum([ref[...].astype(FULL) for ref in refs[1:]], refs[0][...])],
            [unit],
            [],
            [part, *added],
        )
        return sent(total, way)

    arrived.append(with_added(part_x, [for_x], "x"))
    arrived.append(with_added(part_y, [for_y], "y"))
    arrived.append(with_added(part_z, [for_z], "z"))
    (own_part,) = sums_of(affine, [own], theirs_two, sums_near[:1], after=[part_z])

    here, there = pl.pallas_call(
        finish_kernel,
        out_shape=[shard_full, shard_full],
        in_specs=[SMEM, SMEM] + [VMEM] * (2 + len(arrived)),
        out_specs=[VMEM] * 2,
        scratch_shapes=[pltpu.VMEM((2 * rows, width), FULL)],
        compiler_params=PARAMS,
    )(core.reshape(1), multiplier, raw, own_part, *arrived)
    back = other_core(there)
    return (jnp.where(is_first, here, back), jnp.where(is_first, back, here))


def solution(mesh):
    fine = Mesh(mesh.devices.reshape(FINE_SIZES), FINE_AXES)
    rows = P(FINE_AXES, None)
    return jax.shard_map(
        on_device,
        mesh=fine,
        in_specs=(rows, rows, P(), P(), P()),
        out_specs=(rows, rows),
        check_vma=False,
    )
```

```python
import functools
import math

import jax
import jax.numpy as jnp
import numpy as np
from jax import lax
from jax.experimental import pallas as pl
from jax.experimental.pallas import tpu as pltpu
from jax.sharding import Mesh
from jax.sharding import PartitionSpec as P

FINE_AXES = ("y_lo", "core", "x", "z", "y_hi")
FINE_SIZES = (2, 2, 4, 4, 2)
RING = 4
VMEM_BYTES = 16 * 1024 * 1024
HALF = jnp.bfloat16
FULL = jnp.float32

VMEM = pl.BlockSpec(memory_space=pltpu.VMEM)
SMEM = pl.BlockSpec(memory_space=pltpu.SMEM)
ANY = pl.BlockSpec(memory_space=pl.ANY)
PARAMS = pltpu.CompilerParams(vmem_limit_bytes=VMEM_BYTES)

ONE = ("x", "y", "z")
TWO = ("xy", "yz", "zx")
CORNER = "xyz"


def place(core, x, y, z):
    return int(np.ravel_multi_index((y % 2, core, x, z, y // 2), FINE_SIZES))


def mate(core, axis, k):
    if (core == 0) != (axis == "z"):
        return k ^ 1
    return (k + 1) % RING if k % 2 else (k - 1) % RING


def sent(value, way):
    pairs = []
    for at in np.ndindex(RING, RING, RING):
        for core in range(2):
            to = [mate(core, axis, k) if axis in way else k for axis, k in zip("xyz", at, strict=True)]
            pairs.append((place(core, *at), place(core, *to)))
    return lax.ppermute(value, FINE_AXES, pairs)


def other_core(value):
    return lax.ppermute(value, "core", [(0, 1), (1, 0)])


def dot(a, b, contract):
    return lax.dot_general(a, b, ((contract[:1], contract[1:]), ((), ())), preferred_element_type=FULL)


def unit_rows(raw):
    values = raw.astype(FULL)
    scale = lax.rsqrt(jnp.mean(values * values, axis=1, keepdims=True) + 1e-06) / math.sqrt(
        values.shape[1]
    )
    return values * scale, scale


def local(body, outs, scalars, arrays, after=()):
    n_scalars, n_arrays = len(scalars), len(arrays)

    def kernel(*refs):
        given = refs[: n_scalars + n_arrays]
        results = refs[n_scalars + n_arrays + len(after) :]
        for ref, value in zip(results, body(given[:n_scalars], given[n_scalars:]), strict=True):
            ref[...] = value.astype(ref.dtype)

    return pl.pallas_call(
        kernel,
        out_shape=[jax.ShapeDtypeStruct(s, d) for s, d in outs],
        in_specs=[SMEM] * n_scalars + [VMEM] * n_arrays + [ANY] * len(after),
        out_specs=[VMEM] * len(outs),
        compiler_params=PARAMS,
    )(*scalars, *arrays, *after)


def accumulate(affine, mine, theirs, coupling, start, diagonal):
    unit = mine.shape[0]
    pieces = [(ref, k) for ref in theirs for k in range(0, ref.shape[0], unit)]
    for n, (ref, k) in enumerate(pieces):
        energies = dot(mine, ref[pl.ds(k, unit), :], (1, 1))
        tile = 0.5 * jnp.tanh(affine[0] * energies + affine[1]) + 0.5
        if diagonal and n == 0:
            row = lax.broadcasted_iota(jnp.int32, tile.shape, 0)
            column = lax.broadcasted_iota(jnp.int32, tile.shape, 1)
            tile = tile - jnp.where(row == column, 1.0, 0.0)
        coupling[:, pl.ds(n * unit, unit)] = tile.astype(HALF)
    total, first = start, 0
    for ref in theirs:
        count = ref.shape[0]
        term = dot(coupling[:, pl.ds(first, count)], ref[...], (1, 0))
        total = term if total is None else total + term
        first += count
    return total


def sums_kernel(count, n_theirs, n_starts, n_after, diagonal, affine, *refs):
    mine, refs = refs[:count], refs[count:]
    theirs, refs = refs[:n_theirs], refs[n_theirs:]
    starts, refs = refs[:n_starts], refs[n_starts + n_after :]
    sums, coupling = refs[:-1], refs[-1]
    for k in range(count):
        start = starts[k][...] if starts else None
        total = accumulate(affine, mine[k][...], theirs, coupling, start, diagonal and k == 0)
        sums[k][...] = total.astype(sums[k].dtype)


def sums_of(affine, mine, theirs, starts=(), after=(), kinds=None, diagonal=False, hides=True):
    count, n_theirs, n_starts, n_after = len(mine), len(theirs), len(starts), len(after)
    unit, width = mine[0].shape
    against = sum(array.shape[0] for array in theirs)
    kinds = kinds or [FULL] * count
    return pl.pallas_call(
        functools.partial(sums_kernel, count, n_theirs, n_starts, n_after, diagonal),
        out_shape=[jax.ShapeDtypeStruct((unit, width), kind) for kind in kinds],
        in_specs=[SMEM] + [VMEM] * (count + n_theirs + n_starts) + [ANY] * n_after,
        out_specs=[VMEM] * count,
        scratch_shapes=[pltpu.VMEM((unit, against), HALF)],
        cost_estimate=pl.CostEstimate(
            flops=4 * count * unit * against * width if hides else 0,
            bytes_accessed=8 * count * unit * width if hides else 0,
            transcendentals=count * unit * against if hides else 0,
        ),
        compiler_params=PARAMS,
    )(affine, *mine, *theirs, *starts, *after)


def finish_kernel(core, multiplier, raw, *refs):
    parts, (here, there, grads) = refs[:-3], refs[-3:]
    rows = here.shape[0]
    total = parts[0][...].astype(FULL)
    for part in parts[1:]:
        total = total + part[...].astype(FULL)
    unit, scale = unit_rows(raw[...])
    grad = multiplier[0] * total
    grads[...] = scale * (grad - unit * jnp.sum(unit * grad, axis=1, keepdims=True))
    here[...] = grads[pl.ds(core[0] * rows, rows), :]
    there[...] = grads[pl.ds((1 - core[0]) * rows, rows), :]


def on_device(
    picture_vectors_raw, caption_vectors_raw, logit_multiplier, offset_term, incoming_adjoint
):
    rows, width = picture_vectors_raw.shape
    pairs = rows * math.prod(FINE_SIZES)
    core = lax.axis_index("core").astype(jnp.int32)
    is_first = core == 0
    first_flag = is_first.astype(FULL).reshape(1)
    affine = jnp.concatenate([0.5 * logit_multiplier, 0.5 * offset_term])
    multiplier = incoming_adjoint * logit_multiplier / pairs
    shard, unit = ((rows, width), HALF), ((2 * rows, width), HALF)
    shard_full = jax.ShapeDtypeStruct((rows, width), FULL)

    image_there = other_core(picture_vectors_raw)
    text_there = other_core(caption_vectors_raw)
    image, text, raw_here = local(
        lambda scalars, refs: [
            unit_rows(refs[0][...])[0],
            unit_rows(refs[1][...])[0],
            jnp.where(scalars[0][0] > 0, refs[0][...].astype(FULL), refs[1][...].astype(FULL)),
        ],
        [shard] * 3,
        [first_flag],
        [picture_vectors_raw, caption_vectors_raw],
    )

    def own_units(scalars, refs):
        first = scalars[0][0] > 0
        image_there, text_there, image, text, raw_here = [ref[...].astype(FULL) for ref in refs]
        raw_there = jnp.where(first, image_there, text_there)
        images, texts = (image, unit_rows(image_there)[0]), (text, unit_rows(text_there)[0])
        results = [[], [], []]
        for k in range(2):
            of_image = jnp.where(first, images[k], images[1 - k])
            of_text = jnp.where(first, texts[k], texts[1 - k])
            results[0].append(jnp.where(first, of_image, of_text))
            results[1].append(jnp.where(first, of_text, of_image))
            raws = (raw_here, raw_there)
            results[2].append(jnp.where(first, raws[k], raws[1 - k]))
        return [jnp.concatenate(halves, 0) for halves in results]

    own, own_theirs, raw = local(
        own_units, [unit] * 3, [first_flag], [image_there, text_there, image, text, raw_here]
    )

    def stacked(ways, after=()):
        (stack,) = local(
            lambda _, refs: [jnp.concatenate([ref[...] for ref in refs], 0)],
            [((2 * rows * len(ways), width), HALF)],
            [],
            [mine[way] for way in ways],
            after,
        )
        return other_core(stack)

    mine = {"": own}
    for way in ONE:
        mine[way] = sent(own, way)
    mine["xy"] = sent(mine["x"], "y")
    mine["yz"] = sent(mine["y"], "z")
    mine["zx"] = sent(mine["z"], "x")
    def pick(units, ways):
        return [units[way] for way in ways]

    mine[CORNER] = sent(mine["xy"], "z")
    near = ("", *ONE)
    theirs = [own_theirs, stacked(ONE)]
    sums_near = sums_of(affine, pick(mine, near), theirs, diagonal=True, hides=False)
    theirs_two = stacked(TWO, sums_near[:1])
    sums_two = sums_of(affine, pick(mine, TWO), theirs)
    sums_two = sums_of(affine, pick(mine, TWO), [theirs_two], sums_two)
    theirs_corner = stacked([CORNER], sums_two[:1])
    sum_corner = sums_of(affine, [mine[CORNER]], [*theirs, theirs_two], after=sums_two[:1])

    part_xy, part_yz, part_zx = sums_of(
        affine, pick(mine, TWO), [theirs_corner], sums_two, sum_corner, [HALF] * 3
    )
    for_x, for_y, for_z = sent(part_xy, "y"), sent(part_yz, "z"), sent(part_zx, "x")
    (part_xyz,) = sums_of(
        affine, [mine[CORNER]], [theirs_corner], sum_corner, [part_xy], [HALF]
    )
    arrived = [sent(part_xyz, CORNER)]
    theirs = [theirs_two, theirs_corner]
    part_x, part_y, part_z = sums_of(
        affine, pick(mine, ONE), theirs, sums_near[1:], [part_xyz]
    )

    def with_added(part, added, way):
        (total,) = local(
            lambda _, refs: [sum([ref[...].astype(FULL) for ref in refs[1:]], refs[0][...])],
            [unit],
            [],
            [part, *added],
        )
        return sent(total, way)

    arrived.append(with_added(part_x, [for_x], "x"))
    arrived.append(with_added(part_y, [for_y], "y"))
    arrived.append(with_added(part_z, [for_z], "z"))
    (own_part,) = sums_of(affine, [own], theirs, sums_near[:1], [part_z])

    here, there = pl.pallas_call(
        finish_kernel,
        out_shape=[shard_full, shard_full],
        in_specs=[SMEM, SMEM] + [VMEM] * (2 + len(arrived)),
        out_specs=[VMEM] * 2,
        scratch_shapes=[pltpu.VMEM((2 * rows, width), FULL)],
        compiler_params=PARAMS,
    )(core.reshape(1), multiplier, raw, own_part, *arrived)
    back = other_core(there)
    return (jnp.where(is_first, here, back), jnp.where(is_first, back, here))


def solution(mesh):
    fine = Mesh(mesh.devices.reshape(FINE_SIZES), FINE_AXES)
    rows = P(FINE_AXES, None)
    return jax.shard_map(
        on_device,
        mesh=fine,
        in_specs=(rows, rows, P(), P(), P()),
        out_specs=(rows, rows),
        check_vma=False,
    )
```

```python
import functools
import math

import jax
import jax.numpy as jnp
import numpy as np
from jax import lax
from jax.experimental import pallas as pl
from jax.experimental.pallas import tpu as pltpu
from jax.sharding import Mesh
from jax.sharding import PartitionSpec as P

FINE_AXES = ("y_lo", "core", "x", "z", "y_hi")
FINE_SIZES = (2, 2, 4, 4, 2)
RING = 4
VMEM_BYTES = 16 * 1024 * 1024
HALF = jnp.bfloat16
FULL = jnp.float32

VMEM = pl.BlockSpec(memory_space=pltpu.VMEM)
SMEM = pl.BlockSpec(memory_space=pltpu.SMEM)
ANY = pl.BlockSpec(memory_space=pl.ANY)
PARAMS = pltpu.CompilerParams(vmem_limit_bytes=VMEM_BYTES)

ONE = ("x", "y", "z")
TWO = ("xyz", "xy", "yz", "zx")


def place(core, x, y, z):
    return int(np.ravel_multi_index((y % 2, core, x, z, y // 2), FINE_SIZES))


def mate(core, axis, k):
    if (core == 0) != (axis == "z"):
        return k ^ 1
    return (k + 1) % RING if k % 2 else (k - 1) % RING


def sent(value, way, crossing=False):
    pairs = []
    for at in np.ndindex(RING, RING, RING):
        for core in range(2):
            to = [mate(core, axis, k) if axis in way else k for axis, k in zip("xyz", at, strict=True)]
            pairs.append((place(core, *at), place(1 - core if crossing else core, *to)))
    return lax.ppermute(value, FINE_AXES, pairs)


def other_core(value):
    return lax.ppermute(value, "core", [(0, 1), (1, 0)])


def dot(a, b, contract):
    return lax.dot_general(a, b, ((contract[:1], contract[1:]), ((), ())), preferred_element_type=FULL)


def unit_rows(raw):
    values = raw.astype(FULL)
    scale = lax.rsqrt(jnp.mean(values * values, axis=1, keepdims=True) + 1e-06) / math.sqrt(
        values.shape[1]
    )
    return values * scale, scale


def local(body, outs, scalars, arrays, after=()):
    n_scalars, n_arrays = len(scalars), len(arrays)

    def kernel(*refs):
        given = refs[: n_scalars + n_arrays]
        results = refs[n_scalars + n_arrays + len(after) :]
        for ref, value in zip(results, body(given[:n_scalars], given[n_scalars:]), strict=True):
            ref[...] = value.astype(ref.dtype)

    return pl.pallas_call(
        kernel,
        out_shape=[jax.ShapeDtypeStruct(s, d) for s, d in outs],
        in_specs=[SMEM] * n_scalars + [VMEM] * n_arrays + [ANY] * len(after),
        out_specs=[VMEM] * len(outs),
        compiler_params=PARAMS,
    )(*scalars, *arrays, *after)


def accumulate(affine, mine, theirs, coupling, start, diagonal):
    unit = mine.shape[0]
    pieces = [(ref, k) for ref in theirs for k in range(0, ref.shape[0], unit)]
    for n, (ref, k) in enumerate(pieces):
        energies = dot(mine, ref[pl.ds(k, unit), :], (1, 1))
        tile = 0.5 * jnp.tanh(affine[0] * energies + affine[1]) + 0.5
        if diagonal and n == 0:
            row = lax.broadcasted_iota(jnp.int32, tile.shape, 0)
            column = lax.broadcasted_iota(jnp.int32, tile.shape, 1)
            tile = tile - jnp.where(row == column, 1.0, 0.0)
        coupling[:, pl.ds(n * unit, unit)] = tile.astype(HALF)
    total, first = start, 0
    for ref in theirs:
        count = ref.shape[0]
        term = dot(coupling[:, pl.ds(first, count)], ref[...], (1, 0))
        total = term if total is None else total + term
        first += count
    return total


def sums_kernel(count, n_theirs, n_starts, n_after, diagonal, affine, *refs):
    mine, refs = refs[:count], refs[count:]
    theirs, refs = refs[:n_theirs], refs[n_theirs:]
    starts, refs = refs[:n_starts], refs[n_starts + n_after :]
    sums, coupling = refs[:-1], refs[-1]
    for k in range(count):
        start = starts[k][...] if starts else None
        total = accumulate(affine, mine[k][...], theirs, coupling, start, diagonal and k == 0)
        sums[k][...] = total.astype(sums[k].dtype)


def sums_of(affine, mine, theirs, starts=(), after=(), kinds=None, diagonal=False, hides=True):
    count, n_theirs, n_starts, n_after = len(mine), len(theirs), len(starts), len(after)
    unit, width = mine[0].shape
    against = sum(array.shape[0] for array in theirs)
    kinds = kinds or [FULL] * count
    return pl.pallas_call(
        functools.partial(sums_kernel, count, n_theirs, n_starts, n_after, diagonal),
        out_shape=[jax.ShapeDtypeStruct((unit, width), kind) for kind in kinds],
        in_specs=[SMEM] + [VMEM] * (count + n_theirs + n_starts) + [ANY] * n_after,
        out_specs=[VMEM] * count,
        scratch_shapes=[pltpu.VMEM((unit, against), HALF)],
        cost_estimate=pl.CostEstimate(
            flops=4 * count * unit * against * width if hides else 0,
            bytes_accessed=8 * count * unit * width if hides else 0,
            transcendentals=count * unit * against if hides else 0,
        ),
        compiler_params=PARAMS,
    )(affine, *mine, *theirs, *starts, *after)


def on_device(
    picture_vectors_raw, caption_vectors_raw, logit_multiplier, offset_term, incoming_adjoint
):
    rows, width = picture_vectors_raw.shape
    pairs = rows * math.prod(FINE_SIZES)
    core = lax.axis_index("core").astype(jnp.int32)
    is_first = core == 0
    first_flag = is_first.astype(FULL).reshape(1)
    affine = jnp.concatenate([0.5 * logit_multiplier, 0.5 * offset_term])
    multiplier = incoming_adjoint * logit_multiplier / pairs
    shard, unit = ((rows, width), HALF), ((2 * rows, width), HALF)
    shard_full = ((rows, width), FULL)

    image_there = other_core(picture_vectors_raw)
    text_there = other_core(caption_vectors_raw)
    image, text = local(
        lambda _, refs: [unit_rows(ref[...])[0] for ref in refs],
        [shard] * 2,
        [],
        [picture_vectors_raw, caption_vectors_raw],
    )

    def own_units(scalars, refs):
        first = scalars[0][0] > 0
        image_there, text_there, image, text = [ref[...].astype(FULL) for ref in refs]
        images, texts = (image, unit_rows(image_there)[0]), (text, unit_rows(text_there)[0])
        results = [[], []]
        for k in range(2):
            of_image = jnp.where(first, images[k], images[1 - k])
            of_text = jnp.where(first, texts[k], texts[1 - k])
            results[0].append(jnp.where(first, of_image, of_text))
            results[1].append(jnp.where(first, of_text, of_image))
        return [jnp.concatenate(halves, 0) for halves in results]

    own, own_theirs = local(
        own_units, [unit] * 2, [first_flag], [image_there, text_there, image, text]
    )

    def stacked(ways, after=()):
        (stack,) = local(
            lambda _, refs: [jnp.concatenate([ref[...] for ref in refs], 0)],
            [((2 * rows * len(ways), width), HALF)],
            [],
            [mine[way] for way in ways],
            after,
        )
        return other_core(stack)

    mine = {"": own}
    for way in ONE:
        mine[way] = sent(own, way)
    mine["xyz"] = sent(mine["x"], "yz")
    mine["xy"] = sent(mine["x"], "y")
    mine["yz"] = sent(mine["y"], "z")
    mine["zx"] = sent(mine["z"], "x")
    def pick(units, ways):
        return [units[way] for way in ways]

    theirs_one = [own_theirs, stacked(ONE)]
    near = ("", *ONE)
    sums = sums_of(affine, pick(mine, near), theirs_one, diagonal=True, hides=False)
    theirs_two = [stacked(TWO, sums[:1])]
    sums += sums_of(affine, pick(mine, TWO), theirs_one)
    sums = dict(zip((*near, *TWO), sums, strict=True))

    def parts_of(ways, kinds, after=()):
        return sums_of(affine, pick(mine, ways), theirs_two, pick(sums, ways), after, kinds)

    part_xyz, part_xy = parts_of(("xyz", "xy"), [HALF, HALF])
    for_x = [sent(part_xy, "y")]
    part_yz, part_zx = parts_of(("yz", "zx"), [HALF, HALF], [part_xy])
    for_y = [sent(part_xyz, "zx"), sent(part_yz, "z")]
    for_z = [sent(part_zx, "x")]
    own_part, part_x, part_y, part_z = parts_of(near, [FULL] * 4, [part_zx])

    def halves(scalars, refs):
        core, total = scalars[0][0], refs[0]
        found = []
        for which in (core, 1 - core):
            at = pl.ds(pl.multiple_of(which * rows, rows), rows)
            half = total[at, :]
            for ref in refs[1:]:
                half = half + ref[at, :].astype(FULL)
            found.append(half)
        return found

    which = core.reshape(1)
    own_here, own_there = local(halves, [shard_full, shard], [which], [own_part])
    here, there = [own_here], [other_core(own_there)]
    for way, part, added in (("x", part_x, for_x), ("y", part_y, for_y), ("z", part_z, for_z)):
        mine_half, other_half = local(halves, [shard] * 2, [which], [part, *added])
        here.append(sent(mine_half, way))
        there.append(sent(other_half, way, True))

    def finish(scalars, refs):
        first, multiplier = scalars[0][0] > 0, scalars[1][0]
        raws, refs = refs[:2], refs[2:]
        totals = []
        for parts in (refs[: len(here)], refs[len(here) :]):
            totals.append(sum([ref[...].astype(FULL) for ref in parts[1:]], parts[0][...].astype(FULL)))
        results = []
        for k, raw in enumerate(raws):
            unit, scale = unit_rows(raw[...])
            grad = multiplier * jnp.where(first, totals[k], totals[1 - k])
            results.append(scale * (grad - unit * jnp.sum(unit * grad, axis=1, keepdims=True)))
        return results

    return tuple(
        local(
            finish,
            [shard_full] * 2,
            [first_flag, multiplier],
            [picture_vectors_raw, caption_vectors_raw, *here, *there],
        )
    )


def solution(mesh):
    fine = Mesh(mesh.devices.reshape(FINE_SIZES), FINE_AXES)
    rows = P(FINE_AXES, None)
    return jax.shard_map(
        on_device,
        mesh=fine,
        in_specs=(rows, rows, P(), P(), P()),
        out_specs=(rows, rows),
        check_vma=False,
    )
```

```python
import functools
import math

import jax
import jax.numpy as jnp
import numpy as np
from jax import lax
from jax.experimental import pallas as pl
from jax.experimental.pallas import tpu as pltpu
from jax.sharding import Mesh
from jax.sharding import PartitionSpec as P

FINE_AXES = ("y_lo", "core", "x", "z", "y_hi")
FINE_SIZES = (2, 2, 4, 4, 2)
RING = 4
VMEM_BYTES = 16 * 1024 * 1024
HALF = jnp.bfloat16
FULL = jnp.float32

VMEM = pl.BlockSpec(memory_space=pltpu.VMEM)
SMEM = pl.BlockSpec(memory_space=pltpu.SMEM)
ANY = pl.BlockSpec(memory_space=pl.ANY)
PARAMS = pltpu.CompilerParams(vmem_limit_bytes=VMEM_BYTES)

ONE = ("x", "y", "z")
TWO = ("xyz", "xy", "yz", "zx")


def place(core, x, y, z):
    return int(np.ravel_multi_index((y % 2, core, x, z, y // 2), FINE_SIZES))


def mate(core, axis, k):
    if (core == 0) != (axis == "z"):
        return k ^ 1
    return (k + 1) % RING if k % 2 else (k - 1) % RING


def sent(value, way, crossing=False):
    pairs = []
    for at in np.ndindex(RING, RING, RING):
        for core in range(2):
            to = [mate(core, axis, k) if axis in way else k for axis, k in zip("xyz", at, strict=True)]
            pairs.append((place(core, *at), place(1 - core if crossing else core, *to)))
    return lax.ppermute(value, FINE_AXES, pairs)


def other_core(value):
    return lax.ppermute(value, "core", [(0, 1), (1, 0)])


def dot(a, b, contract):
    return lax.dot_general(a, b, ((contract[:1], contract[1:]), ((), ())), preferred_element_type=FULL)


def unit_rows(raw):
    values = raw.astype(FULL)
    scale = lax.rsqrt(jnp.mean(values * values, axis=1, keepdims=True) + 1e-06) / math.sqrt(
        values.shape[1]
    )
    return values * scale, scale


def local(body, outs, scalars, arrays, after=()):
    n_scalars, n_arrays = len(scalars), len(arrays)

    def kernel(*refs):
        given = refs[: n_scalars + n_arrays]
        results = refs[n_scalars + n_arrays + len(after) :]
        for ref, value in zip(results, body(given[:n_scalars], given[n_scalars:]), strict=True):
            ref[...] = value.astype(ref.dtype)

    return pl.pallas_call(
        kernel,
        out_shape=[jax.ShapeDtypeStruct(s, d) for s, d in outs],
        in_specs=[SMEM] * n_scalars + [VMEM] * n_arrays + [ANY] * len(after),
        out_specs=[VMEM] * len(outs),
        compiler_params=PARAMS,
    )(*scalars, *arrays, *after)


def accumulate(affine, mine, theirs, coupling, start, diagonal):
    unit = mine.shape[0]
    pieces = [(ref, k) for ref in theirs for k in range(0, ref.shape[0], unit)]
    for n, (ref, k) in enumerate(pieces):
        energies = dot(mine, ref[pl.ds(k, unit), :], (1, 1))
        tile = 0.5 * jnp.tanh(affine[0] * energies + affine[1]) + 0.5
        if diagonal and n == 0:
            row = lax.broadcasted_iota(jnp.int32, tile.shape, 0)
            column = lax.broadcasted_iota(jnp.int32, tile.shape, 1)
            tile = tile - jnp.where(row == column, 1.0, 0.0)
        coupling[:, pl.ds(n * unit, unit)] = tile.astype(HALF)
    total, first = start, 0
    for ref in theirs:
        count = ref.shape[0]
        term = dot(coupling[:, pl.ds(first, count)], ref[...], (1, 0))
        total = term if total is None else total + term
        first += count
    return total


def sums_kernel(plan, n_inputs, n_after, diagonal, affine, *refs):
    inputs, results, coupling = refs[:n_inputs], refs[n_inputs + n_after : -1], refs[-1]
    for k, (mine, theirs, start) in enumerate(plan):
        begin = None if start is None else inputs[start][...]
        total = accumulate(
            affine, inputs[mine][...], [inputs[n] for n in theirs], coupling, begin, diagonal and k == 0
        )
        results[k][...] = total.astype(results[k].dtype)


def sums_of(affine, jobs, after=(), kind=FULL, diagonal=False, hides=True):
    inputs, plan, tiles, widest = [], [], 0, 0

    def index(array):
        for n, known in enumerate(inputs):
            if known is array:
                return n
        inputs.append(array)
        return len(inputs) - 1

    unit, width = jobs[0][0].shape
    for mine, theirs, start in jobs:
        against = sum(array.shape[0] for array in theirs)
        tiles, widest = tiles + against // unit, max(widest, against)
        plan.append(
            (index(mine), [index(array) for array in theirs], None if start is None else index(start))
        )
    return pl.pallas_call(
        functools.partial(sums_kernel, plan, len(inputs), len(after), diagonal),
        out_shape=[jax.ShapeDtypeStruct((unit, width), kind)] * len(jobs),
        in_specs=[SMEM] + [VMEM] * len(inputs) + [ANY] * len(after),
        out_specs=[VMEM] * len(jobs),
        scratch_shapes=[pltpu.VMEM((unit, widest), HALF)],
        cost_estimate=pl.CostEstimate(
            flops=4 * tiles * unit**2 * width if hides else 0,
            bytes_accessed=8 * len(jobs) * unit * width if hides else 0,
            transcendentals=tiles * unit**2 if hides else 0,
        ),
        compiler_params=PARAMS,
    )(affine, *inputs, *after)


def on_device(
    picture_vectors_raw, caption_vectors_raw, logit_multiplier, offset_term, incoming_adjoint
):
    rows, width = picture_vectors_raw.shape
    pairs = rows * math.prod(FINE_SIZES)
    core = lax.axis_index("core").astype(jnp.int32)
    is_first = core == 0
    first_flag = is_first.astype(FULL).reshape(1)
    affine = jnp.concatenate([0.5 * logit_multiplier, 0.5 * offset_term])
    multiplier = incoming_adjoint * logit_multiplier / pairs
    shard, unit = ((rows, width), HALF), ((2 * rows, width), HALF)
    shard_full = ((rows, width), FULL)

    image_there = other_core(picture_vectors_raw)
    text_there = other_core(caption_vectors_raw)
    image, text = local(
        lambda _, refs: [unit_rows(ref[...])[0] for ref in refs],
        [shard] * 2,
        [],
        [picture_vectors_raw, caption_vectors_raw],
    )

    def own_units(scalars, refs):
        first = scalars[0][0] > 0
        image_there, text_there, image, text = [ref[...].astype(FULL) for ref in refs]
        images, texts = (image, unit_rows(image_there)[0]), (text, unit_rows(text_there)[0])
        results = [[], []]
        for k in range(2):
            of_image = jnp.where(first, images[k], images[1 - k])
            of_text = jnp.where(first, texts[k], texts[1 - k])
            results[0].append(jnp.where(first, of_image, of_text))
            results[1].append(jnp.where(first, of_text, of_image))
        return [jnp.concatenate(halves, 0) for halves in results]

    own, own_theirs = local(
        own_units, [unit] * 2, [first_flag], [image_there, text_there, image, text]
    )

    def stacked(ways, after=()):
        (stack,) = local(
            lambda _, refs: [jnp.concatenate([ref[...] for ref in refs], 0)],
            [((2 * rows * len(ways), width), HALF)],
            [],
            [mine[way] for way in ways],
            after,
        )
        return other_core(stack)

    mine = {"": own}
    for way in ONE:
        mine[way] = sent(own, way)
    mine["xyz"] = sent(mine["x"], "yz")
    mine["xy"] = sent(mine["x"], "y")
    mine["yz"] = sent(mine["y"], "z")
    mine["zx"] = sent(mine["z"], "x")
    near = ("", *ONE)
    one = [own_theirs, stacked(ONE)]
    sums = sums_of(affine, [(mine[way], one, None) for way in near], diagonal=True, hides=False)
    sums = dict(zip(near, sums, strict=True))
    two = [stacked(TWO, [sums[""]])]
    sums |= zip(TWO, sums_of(affine, [(mine[way], one, None) for way in TWO]), strict=True)

    def parts_of(ways, after, kind=FULL):
        return sums_of(affine, [(mine[way], two, sums[way]) for way in ways], after, kind)

    def added(part, other):
        (total,) = local(
            lambda _, refs: [refs[0][...] + refs[1][...].astype(FULL)], [unit], [], [part, other]
        )
        return total

    (part_xyz,) = parts_of(["xyz"], [], HALF)
    for_yz = sent(part_xyz, "x")
    part_xy, part_zx = parts_of(["xy", "zx"], [part_xyz], HALF)
    for_x, for_z = sent(part_xy, "y"), sent(part_zx, "x")
    (part_yz,) = parts_of(["yz"], [part_xy])
    part_yz = added(part_yz, for_yz)
    for_y = sent(part_yz, "z")
    part_x, part_y, part_z = parts_of(ONE, [part_yz])
    part_x, part_z = added(part_x, for_x), added(part_z, for_z)
    from_x, from_z = sent(part_x, "x"), sent(part_z, "z")

    def halves(scalars, refs):
        core, total = scalars[0][0], refs[0]
        found = []
        for which in (core, 1 - core):
            at = pl.ds(pl.multiple_of(which * rows, rows), rows)
            half = total[at, :]
            for ref in refs[1:]:
                half = half + ref[at, :].astype(FULL)
            found.append(half)
        return found

    which = core.reshape(1)
    y_here, y_there = local(halves, [shard] * 2, [which], [part_y, for_y], [part_x, part_z])
    (own_part,) = parts_of([""], [y_here])
    y_here, y_there = sent(y_here, "y"), sent(y_there, "y", True)
    here, there = local(
        halves, [shard_full, shard], [which], [own_part, from_x, from_z], [y_there]
    )
    there = other_core(there)

    def finish(scalars, refs):
        first, multiplier = scalars[0][0] > 0, scalars[1][0]
        here, there, y_here, y_there = [ref[...].astype(FULL) for ref in refs[2:]]
        totals = (here + y_here, there + y_there)
        results = []
        for k, raw in enumerate(refs[:2]):
            unit, scale = unit_rows(raw[...])
            grad = multiplier * jnp.where(first, totals[k], totals[1 - k])
            results.append(scale * (grad - unit * jnp.sum(unit * grad, axis=1, keepdims=True)))
        return results

    return tuple(
        local(
            finish,
            [shard_full] * 2,
            [first_flag, multiplier],
            [picture_vectors_raw, caption_vectors_raw, here, there, y_here, y_there],
        )
    )


def solution(mesh):
    fine = Mesh(mesh.devices.reshape(FINE_SIZES), FINE_AXES)
    rows = P(FINE_AXES, None)
    return jax.shard_map(
        on_device,
        mesh=fine,
        in_specs=(rows, rows, P(), P(), P()),
        out_specs=(rows, rows),
        check_vma=False,
    )
```

```python
import functools
import math

import jax
import jax.numpy as jnp
import numpy as np
from jax import lax
from jax.experimental import pallas as pl
from jax.experimental.pallas import tpu as pltpu
from jax.sharding import Mesh
from jax.sharding import PartitionSpec as P

FINE_AXES = ("y_lo", "core", "x", "z", "y_hi")
FINE_SIZES = (2, 2, 4, 4, 2)
RING = 4
VMEM_BYTES = 16 * 1024 * 1024
HALF = jnp.bfloat16
FULL = jnp.float32

VMEM = pl.BlockSpec(memory_space=pltpu.VMEM)
SMEM = pl.BlockSpec(memory_space=pltpu.SMEM)
ANY = pl.BlockSpec(memory_space=pl.ANY)
PARAMS = pltpu.CompilerParams(vmem_limit_bytes=VMEM_BYTES)

ONE = ("x", "z", "y")


def place(core, x, y, z):
    return int(np.ravel_multi_index((y % 2, core, x, z, y // 2), FINE_SIZES))


def mate(core, axis, k):
    if (core == 0) != (axis == "z"):
        return k ^ 1
    return (k + 1) % RING if k % 2 else (k - 1) % RING


def sent(value, way, crossing=False):
    pairs = []
    for at in np.ndindex(RING, RING, RING):
        for core in range(2):
            to = [mate(core, axis, k) if axis in way else k for axis, k in zip("xyz", at, strict=True)]
            pairs.append((place(core, *at), place(1 - core if crossing else core, *to)))
    return lax.ppermute(value, FINE_AXES, pairs)


def other_core(value):
    return lax.ppermute(value, "core", [(0, 1), (1, 0)])


def dot(a, b, contract):
    return lax.dot_general(a, b, ((contract[:1], contract[1:]), ((), ())), preferred_element_type=FULL)


def unit_rows(raw):
    values = raw.astype(FULL)
    scale = lax.rsqrt(jnp.mean(values * values, axis=1, keepdims=True) + 1e-06) / math.sqrt(
        values.shape[1]
    )
    return values * scale, scale


def local(body, outs, scalars, arrays, after=()):
    n_scalars, n_arrays = len(scalars), len(arrays)

    def kernel(*refs):
        given = refs[: n_scalars + n_arrays]
        results = refs[n_scalars + n_arrays + len(after) :]
        for ref, value in zip(results, body(given[:n_scalars], given[n_scalars:]), strict=True):
            ref[...] = value.astype(ref.dtype)

    return pl.pallas_call(
        kernel,
        out_shape=[jax.ShapeDtypeStruct(s, d) for s, d in outs],
        in_specs=[SMEM] * n_scalars + [VMEM] * n_arrays + [ANY] * len(after),
        out_specs=[VMEM] * len(outs),
        compiler_params=PARAMS,
    )(*scalars, *arrays, *after)


def accumulate(affine, mine, theirs, coupling, start, diagonal):
    unit = mine.shape[0]
    pieces = [(ref, k) for ref in theirs for k in range(0, ref.shape[0], unit)]
    for n, (ref, k) in enumerate(pieces):
        energies = dot(mine, ref[pl.ds(k, unit), :], (1, 1))
        tile = 0.5 * jnp.tanh(affine[0] * energies + affine[1]) + 0.5
        if diagonal and n == 0:
            row = lax.broadcasted_iota(jnp.int32, tile.shape, 0)
            column = lax.broadcasted_iota(jnp.int32, tile.shape, 1)
            tile = tile - jnp.where(row == column, 1.0, 0.0)
        coupling[:, pl.ds(n * unit, unit)] = tile.astype(HALF)
    total, first = start, 0
    for ref in theirs:
        count = ref.shape[0]
        term = dot(coupling[:, pl.ds(first, count)], ref[...], (1, 0))
        total = term if total is None else total + term
        first += count
    return total


def sums_kernel(plan, n_inputs, n_after, diagonal, affine, *refs):
    inputs, results, coupling = refs[:n_inputs], refs[n_inputs + n_after : -1], refs[-1]
    for k, (mine, theirs, start) in enumerate(plan):
        begin = None if start is None else inputs[start][...]
        total = accumulate(
            affine, inputs[mine][...], [inputs[n] for n in theirs], coupling, begin, diagonal and k == 0
        )
        results[k][...] = total.astype(results[k].dtype)


def sums_of(affine, jobs, after=(), kind=FULL, diagonal=False, hides=True):
    inputs, plan, tiles, widest = [], [], 0, 0

    def index(array):
        for n, known in enumerate(inputs):
            if known is array:
                return n
        inputs.append(array)
        return len(inputs) - 1

    unit, width = jobs[0][0].shape
    for mine, theirs, start in jobs:
        against = sum(array.shape[0] for array in theirs)
        tiles, widest = tiles + against // unit, max(widest, against)
        plan.append(
            (index(mine), [index(array) for array in theirs], None if start is None else index(start))
        )
    return pl.pallas_call(
        functools.partial(sums_kernel, plan, len(inputs), len(after), diagonal),
        out_shape=[jax.ShapeDtypeStruct((unit, width), kind)] * len(jobs),
        in_specs=[SMEM] + [VMEM] * len(inputs) + [ANY] * len(after),
        out_specs=[VMEM] * len(jobs),
        scratch_shapes=[pltpu.VMEM((unit, widest), HALF)],
        cost_estimate=pl.CostEstimate(
            flops=4 * tiles * unit**2 * width if hides else 0,
            bytes_accessed=8 * len(jobs) * unit * width if hides else 0,
            transcendentals=tiles * unit**2 if hides else 0,
        ),
        compiler_params=PARAMS,
    )(affine, *inputs, *after)


def on_device(
    picture_vectors_raw, caption_vectors_raw, logit_multiplier, offset_term, incoming_adjoint
):
    rows, width = picture_vectors_raw.shape
    pairs = rows * math.prod(FINE_SIZES)
    core = lax.axis_index("core").astype(jnp.int32)
    is_first = core == 0
    first_flag = is_first.astype(FULL).reshape(1)
    affine = jnp.concatenate([0.5 * logit_multiplier, 0.5 * offset_term])
    multiplier = incoming_adjoint * logit_multiplier / pairs
    shard, unit = ((rows, width), HALF), ((2 * rows, width), HALF)
    shard_full = ((rows, width), FULL)

    image_there = other_core(picture_vectors_raw)
    text_there = other_core(caption_vectors_raw)
    image, text = local(
        lambda _, refs: [unit_rows(ref[...])[0] for ref in refs],
        [shard] * 2,
        [],
        [picture_vectors_raw, caption_vectors_raw],
    )

    def own_units(scalars, refs):
        first = scalars[0][0] > 0
        image_there, text_there, image, text = [ref[...].astype(FULL) for ref in refs]
        images, texts = (image, unit_rows(image_there)[0]), (text, unit_rows(text_there)[0])
        results = [[], []]
        for k in range(2):
            of_image = jnp.where(first, images[k], images[1 - k])
            of_text = jnp.where(first, texts[k], texts[1 - k])
            results[0].append(jnp.where(first, of_image, of_text))
            results[1].append(jnp.where(first, of_text, of_image))
        return [jnp.concatenate(halves, 0) for halves in results]

    own, own_theirs = local(
        own_units, [unit] * 2, [first_flag], [image_there, text_there, image, text]
    )

    def stacked(ways, after=()):
        (stack,) = local(
            lambda _, refs: [jnp.concatenate([ref[...] for ref in refs], 0)],
            [((2 * rows * len(ways), width), HALF)],
            [],
            [mine[way] for way in ways],
            after,
        )
        return other_core(stack)

    mine = {"": own}
    for way in ONE:
        mine[way] = sent(own, way)
    mine["xyz"] = sent(mine["x"], "yz")
    mine["xy"] = sent(mine["x"], "y")
    mine["yz"] = sent(mine["y"], "z")
    mine["zx"] = sent(mine["z"], "x")
    near = ("", *ONE)
    one = [own_theirs, stacked(ONE)]
    sums = sums_of(affine, [(mine[way], one, None) for way in near], diagonal=True, hides=False)
    sums = dict(zip(near, sums, strict=True))
    zx_there = stacked(["zx"], [sums[""]])
    (sums["zx"],) = sums_of(affine, [(mine["zx"], one, None)], [sums[""]])
    two = [zx_there, stacked(("xyz", "xy", "yz"), [sums["zx"], zx_there])]
    jobs = [(mine["xyz"], one, None), (mine["xy"], one, None)]
    sums["xyz"], sums["xy"] = sums_of(affine, jobs, [sums["zx"]])

    def parts_of(ways, after, kind=FULL):
        return sums_of(affine, [(mine[way], two, sums[way]) for way in ways], after, kind)

    def added(part, other):
        (total,) = local(
            lambda _, refs: [refs[0][...] + refs[1][...].astype(FULL)], [unit], [], [part, other]
        )
        return total

    (part_xyz,) = parts_of(["xyz"], [], HALF)
    for_yz = sent(part_xyz, "x")
    part_xy, part_zx = parts_of(["xy", "zx"], [part_xyz], HALF)
    for_x, for_z = sent(part_xy, "y"), sent(part_zx, "x")
    (part_yz,) = sums_of(affine, [(mine["yz"], one + two, None)], [part_xy])
    part_yz = added(part_yz, for_yz)
    for_y = sent(part_yz, "z")
    part_x, part_z, part_y = parts_of(ONE, [part_yz])
    part_x, part_z = added(part_x, for_x), added(part_z, for_z)
    from_x, from_z = sent(part_x, "x"), sent(part_z, "z")

    def halves(scalars, refs):
        core, total = scalars[0][0], refs[0]
        found = []
        for which in (core, 1 - core):
            at = pl.ds(pl.multiple_of(which * rows, rows), rows)
            half = total[at, :]
            for ref in refs[1:]:
                half = half + ref[at, :].astype(FULL)
            found.append(half)
        return found

    which = core.reshape(1)
    y_here, y_there = local(halves, [shard] * 2, [which], [part_y, for_y], [part_x, part_z])
    (own_part,) = parts_of([""], [y_here])
    y_here, y_there = sent(y_here, "y"), sent(y_there, "y", True)
    here, there = local(
        halves, [shard_full, shard], [which], [own_part, from_x, from_z], [y_there]
    )
    there = other_core(there)

    def finish(scalars, refs):
        first, multiplier = scalars[0][0] > 0, scalars[1][0]
        here, there, y_here, y_there = [ref[...].astype(FULL) for ref in refs[2:]]
        totals = (here + y_here, there + y_there)
        results = []
        for k, raw in enumerate(refs[:2]):
            unit, scale = unit_rows(raw[...])
            grad = multiplier * jnp.where(first, totals[k], totals[1 - k])
            results.append(scale * (grad - unit * jnp.sum(unit * grad, axis=1, keepdims=True)))
        return results

    return tuple(
        local(
            finish,
            [shard_full] * 2,
            [first_flag, multiplier],
            [picture_vectors_raw, caption_vectors_raw, here, there, y_here, y_there],
        )
    )


def solution(mesh):
    fine = Mesh(mesh.devices.reshape(FINE_SIZES), FINE_AXES)
    rows = P(FINE_AXES, None)
    return jax.shard_map(
        on_device,
        mesh=fine,
        in_specs=(rows, rows, P(), P(), P()),
        out_specs=(rows, rows),
        check_vma=False,
    )
```

```python
import functools
import math

import jax
import jax.numpy as jnp
import numpy as np
from jax import lax
from jax.experimental import pallas as pl
from jax.experimental.pallas import tpu as pltpu
from jax.sharding import Mesh
from jax.sharding import PartitionSpec as P

FINE_AXES = ("y_lo", "core", "x", "z", "y_hi")
FINE_SIZES = (2, 2, 4, 4, 2)
RING = 4
VMEM_BYTES = 16 * 1024 * 1024
CUTS = 4
HALF = jnp.bfloat16
FULL = jnp.float32

VMEM = pl.BlockSpec(memory_space=pltpu.VMEM)
SMEM = pl.BlockSpec(memory_space=pltpu.SMEM)
ANY = pl.BlockSpec(memory_space=pl.ANY)
PARAMS = pltpu.CompilerParams(vmem_limit_bytes=VMEM_BYTES)

ONE = ("x", "y", "z")
TWO = ("xyz", "xy", "yz", "zx")


def place(core, x, y, z):
    return int(np.ravel_multi_index((y % 2, core, x, z, y // 2), FINE_SIZES))


def mate(core, axis, k):
    if (core == 0) != (axis == "z"):
        return k ^ 1
    return (k + 1) % RING if k % 2 else (k - 1) % RING


def sent(value, way, crossing=False):
    pairs = []
    for at in np.ndindex(RING, RING, RING):
        for core in range(2):
            to = [mate(core, axis, k) if axis in way else k for axis, k in zip("xyz", at, strict=True)]
            pairs.append((place(core, *at), place(1 - core if crossing else core, *to)))
    return lax.ppermute(value, FINE_AXES, pairs)


def other_core(value):
    return lax.ppermute(value, "core", [(0, 1), (1, 0)])


def dot(a, b, contract):
    return lax.dot_general(a, b, ((contract[:1], contract[1:]), ((), ())), preferred_element_type=FULL)


def unit_rows(raw):
    values = raw.astype(FULL)
    scale = lax.rsqrt(jnp.mean(values * values, axis=1, keepdims=True) + 1e-06) / math.sqrt(
        values.shape[1]
    )
    return values * scale, scale


def local(body, outs, scalars, arrays, after=()):
    n_scalars, n_arrays = len(scalars), len(arrays)

    def kernel(*refs):
        given = refs[: n_scalars + n_arrays]
        results = refs[n_scalars + n_arrays + len(after) :]
        for ref, value in zip(results, body(given[:n_scalars], given[n_scalars:]), strict=True):
            ref[...] = value.astype(ref.dtype)

    return pl.pallas_call(
        kernel,
        out_shape=[jax.ShapeDtypeStruct(s, d) for s, d in outs],
        in_specs=[SMEM] * n_scalars + [VMEM] * n_arrays + [ANY] * len(after),
        out_specs=[VMEM] * len(outs),
        compiler_params=PARAMS,
    )(*scalars, *arrays, *after)


def accumulate(affine, mine, theirs, coupling, start, diagonal):
    unit = mine.shape[0]
    pieces = [(ref, k) for ref in theirs for k in range(0, ref.shape[0], unit)]
    for n, (ref, k) in enumerate(pieces):
        energies = dot(mine, ref[pl.ds(k, unit), :], (1, 1))
        tile = 0.5 * jnp.tanh(affine[0] * energies + affine[1]) + 0.5
        if diagonal and n == 0:
            row = lax.broadcasted_iota(jnp.int32, tile.shape, 0)
            column = lax.broadcasted_iota(jnp.int32, tile.shape, 1)
            tile = tile - jnp.where(row == column, 1.0, 0.0)
        coupling[:, pl.ds(n * unit, unit)] = tile.astype(HALF)
    total, first = start, 0
    for ref in theirs:
        count = ref.shape[0]
        term = dot(coupling[:, pl.ds(first, count)], ref[...], (1, 0))
        total = term if total is None else total + term
        first += count
    return total


def sums_kernel(plan, n_inputs, n_after, diagonal, affine, *refs):
    inputs, results, coupling = refs[:n_inputs], refs[n_inputs + n_after : -1], refs[-1]
    for k, (mine, theirs, start) in enumerate(plan):
        begin = None if start is None else inputs[start][...]
        total = accumulate(
            affine, inputs[mine][...], [inputs[n] for n in theirs], coupling, begin, diagonal and k == 0
        )
        results[k][...] = total.astype(results[k].dtype)


def sums_of(affine, jobs, after=(), kind=FULL, diagonal=False, hides=True):
    inputs, plan, tiles, widest = [], [], 0, 0

    def index(array):
        for n, known in enumerate(inputs):
            if known is array:
                return n
        inputs.append(array)
        return len(inputs) - 1

    unit, width = jobs[0][0].shape
    for mine, theirs, start in jobs:
        against = sum(array.shape[0] for array in theirs)
        tiles, widest = tiles + against // unit, max(widest, against)
        plan.append(
            (index(mine), [index(array) for array in theirs], None if start is None else index(start))
        )
    return pl.pallas_call(
        functools.partial(sums_kernel, plan, len(inputs), len(after), diagonal),
        out_shape=[jax.ShapeDtypeStruct((unit, width), kind)] * len(jobs),
        in_specs=[SMEM] + [VMEM] * len(inputs) + [ANY] * len(after),
        out_specs=[VMEM] * len(jobs),
        scratch_shapes=[pltpu.VMEM((unit, widest), HALF)],
        cost_estimate=pl.CostEstimate(
            flops=4 * tiles * unit**2 * width if hides else 0,
            bytes_accessed=8 * len(jobs) * unit * width if hides else 0,
            transcendentals=tiles * unit**2 if hides else 0,
        ),
        compiler_params=PARAMS,
    )(affine, *inputs, *after)


def finish_kernel(is_first, multiplier, *refs):
    raws, (here, there, y_here, y_there), outs, (held, sems) = refs[:2], refs[2:6], refs[6:8], refs[8:]
    first = is_first[0] > 0
    cut = raws[0].shape[0] // CUTS
    copies = []
    for n in range(CUTS):
        at = pl.ds(n * cut, cut)
        totals = (here[at, :] + y_here[at, :].astype(FULL), there[at, :].astype(FULL) + y_there[at, :].astype(FULL))
        for k, raw in enumerate(raws):
            unit, scale = unit_rows(raw[at, :])
            grad = multiplier[0] * jnp.where(first, totals[k], totals[1 - k])
            held[k, at, :] = scale * (grad - unit * jnp.sum(unit * grad, axis=1, keepdims=True))
            copies.append(pltpu.make_async_copy(held.at[k, at], outs[k].at[at], sems.at[len(copies)]))
            copies[-1].start()
    for copy in copies:
        copy.wait()


def on_device(
    picture_vectors_raw, caption_vectors_raw, logit_multiplier, offset_term, incoming_adjoint
):
    rows, width = picture_vectors_raw.shape
    pairs = rows * math.prod(FINE_SIZES)
    core = lax.axis_index("core").astype(jnp.int32)
    is_first = core == 0
    first_flag = is_first.astype(FULL).reshape(1)
    affine = jnp.concatenate([0.5 * logit_multiplier, 0.5 * offset_term])
    multiplier = incoming_adjoint * logit_multiplier / pairs
    shard, unit = ((rows, width), HALF), ((2 * rows, width), HALF)
    shard_full = ((rows, width), FULL)

    image_there = other_core(picture_vectors_raw)
    text_there = other_core(caption_vectors_raw)
    image, text = local(
        lambda _, refs: [unit_rows(ref[...])[0] for ref in refs],
        [shard] * 2,
        [],
        [picture_vectors_raw, caption_vectors_raw],
    )

    def own_units(scalars, refs):
        first = scalars[0][0] > 0
        image_there, text_there, image, text = [ref[...].astype(FULL) for ref in refs]
        images, texts = (image, unit_rows(image_there)[0]), (text, unit_rows(text_there)[0])
        results = [[], []]
        for k in range(2):
            of_image = jnp.where(first, images[k], images[1 - k])
            of_text = jnp.where(first, texts[k], texts[1 - k])
            results[0].append(jnp.where(first, of_image, of_text))
            results[1].append(jnp.where(first, of_text, of_image))
        return [jnp.concatenate(halves, 0) for halves in results]

    own, own_theirs = local(
        own_units, [unit] * 2, [first_flag], [image_there, text_there, image, text]
    )

    def stacked(ways, after=()):
        (stack,) = local(
            lambda _, refs: [jnp.concatenate([ref[...] for ref in refs], 0)],
            [((2 * rows * len(ways), width), HALF)],
            [],
            [mine[way] for way in ways],
            after,
        )
        return other_core(stack)

    mine = {"": own}
    for way in ONE:
        mine[way] = sent(own, way)
    mine["xyz"] = sent(mine["x"], "yz")
    mine["xy"] = sent(mine["x"], "y")
    mine["yz"] = sent(mine["y"], "z")
    mine["zx"] = sent(mine["z"], "x")
    near = ("", *ONE)
    one = [own_theirs, stacked(ONE)]
    sums = sums_of(affine, [(mine[way], one, None) for way in near], diagonal=True, hides=False)
    sums = dict(zip(near, sums, strict=True))
    two = [stacked(TWO, [sums[""]])]
    ways = ("xyz", "xy", "zx")
    sums |= zip(ways, sums_of(affine, [(mine[way], one, None) for way in ways]), strict=True)

    def parts_of(ways, after, kind=FULL):
        return sums_of(affine, [(mine[way], two, sums[way]) for way in ways], after, kind)

    def added(part, other):
        (total,) = local(
            lambda _, refs: [refs[0][...] + refs[1][...].astype(FULL)], [unit], [], [part, other]
        )
        return total

    (part_xyz,) = parts_of(["xyz"], [], HALF)
    for_yz = sent(part_xyz, "x")
    part_xy, part_zx = parts_of(["xy", "zx"], [part_xyz], HALF)
    for_x, for_z = sent(part_xy, "y"), sent(part_zx, "x")
    (part_yz,) = sums_of(affine, [(mine["yz"], one + two, None)], [part_xy])
    part_yz = added(part_yz, for_yz)
    for_y = sent(part_yz, "z")
    part_x, part_y, part_z = parts_of(ONE, [part_yz])
    part_x, part_z = added(part_x, for_x), added(part_z, for_z)
    from_x, from_z = sent(part_x, "x"), sent(part_z, "z")

    def halves(scalars, refs):
        core, total = scalars[0][0], refs[0]
        found = []
        for which in (core, 1 - core):
            at = pl.ds(pl.multiple_of(which * rows, rows), rows)
            half = total[at, :]
            for ref in refs[1:]:
                half = half + ref[at, :].astype(FULL)
            found.append(half)
        return found

    which = core.reshape(1)
    y_here, y_there = local(halves, [shard] * 2, [which], [part_y, for_y], [part_x, part_z])
    (own_part,) = parts_of([""], [y_here])
    y_here, y_there = sent(y_here, "y"), sent(y_there, "y", True)
    here, there = local(
        halves, [shard_full, shard], [which], [own_part, from_x, from_z], [y_there]
    )
    there = other_core(there)

    return tuple(
        pl.pallas_call(
            finish_kernel,
            out_shape=[jax.ShapeDtypeStruct(*shard_full)] * 2,
            in_specs=[SMEM] * 2 + [VMEM] * 6,
            out_specs=[ANY] * 2,
            scratch_shapes=[
                pltpu.VMEM((2, rows, width), FULL),
                pltpu.SemaphoreType.DMA((2 * CUTS,)),
            ],
            compiler_params=PARAMS,
        )(
            first_flag,
            multiplier,
            picture_vectors_raw,
            caption_vectors_raw,
            here,
            there,
            y_here,
            y_there,
        )
    )


def solution(mesh):
    fine = Mesh(mesh.devices.reshape(FINE_SIZES), FINE_AXES)
    rows = P(FINE_AXES, None)
    return jax.shard_map(
        on_device,
        mesh=fine,
        in_specs=(rows, rows, P(), P(), P()),
        out_specs=(rows, rows),
        check_vma=False,
    )
```

```python
import functools
import math

import jax
import jax.numpy as jnp
import numpy as np
from jax import lax
from jax.experimental import pallas as pl
from jax.experimental.pallas import tpu as pltpu
from jax.sharding import Mesh
from jax.sharding import PartitionSpec as P

FINE_AXES = ("y_lo", "core", "x", "z", "y_hi")
FINE_SIZES = (2, 2, 4, 4, 2)
RING = 4
VMEM_BYTES = 16 * 1024 * 1024
CUTS = 4
HALF = jnp.bfloat16
FULL = jnp.float32

VMEM = pl.BlockSpec(memory_space=pltpu.VMEM)
SMEM = pl.BlockSpec(memory_space=pltpu.SMEM)
ANY = pl.BlockSpec(memory_space=pl.ANY)
PARAMS = pltpu.CompilerParams(vmem_limit_bytes=VMEM_BYTES)

ONE = ("x", "y", "z")
TWO = ("xy", "yz", "zx")


def place(core, x, y, z):
    return int(np.ravel_multi_index((y % 2, core, x, z, y // 2), FINE_SIZES))


def mate(core, axis, k):
    if (core == 0) != (axis == "z"):
        return k ^ 1
    return (k + 1) % RING if k % 2 else (k - 1) % RING


def sent(value, way, crossing=False):
    pairs = []
    for at in np.ndindex(RING, RING, RING):
        for core in range(2):
            to = [mate(core, axis, k) if axis in way else k for axis, k in zip("xyz", at, strict=True)]
            pairs.append((place(core, *at), place(1 - core if crossing else core, *to)))
    return lax.ppermute(value, FINE_AXES, pairs)


def other_core(value):
    return lax.ppermute(value, "core", [(0, 1), (1, 0)])


def dot(a, b, contract):
    return lax.dot_general(a, b, ((contract[:1], contract[1:]), ((), ())), preferred_element_type=FULL)


def unit_rows(raw):
    values = raw.astype(FULL)
    scale = lax.rsqrt(jnp.mean(values * values, axis=1, keepdims=True) + 1e-06) / math.sqrt(
        values.shape[1]
    )
    return values * scale, scale


def local(body, outs, scalars, arrays, after=()):
    n_scalars, n_arrays = len(scalars), len(arrays)

    def kernel(*refs):
        given = refs[: n_scalars + n_arrays]
        results = refs[n_scalars + n_arrays + len(after) :]
        for ref, value in zip(results, body(given[:n_scalars], given[n_scalars:]), strict=True):
            ref[...] = value.astype(ref.dtype)

    return pl.pallas_call(
        kernel,
        out_shape=[jax.ShapeDtypeStruct(s, d) for s, d in outs],
        in_specs=[SMEM] * n_scalars + [VMEM] * n_arrays + [ANY] * len(after),
        out_specs=[VMEM] * len(outs),
        compiler_params=PARAMS,
    )(*scalars, *arrays, *after)


def accumulate(affine, mine, theirs, coupling, start, diagonal):
    unit = mine.shape[0]
    pieces = [(ref, k) for ref in theirs for k in range(0, ref.shape[0], unit)]
    for n, (ref, k) in enumerate(pieces):
        energies = dot(mine, ref[pl.ds(k, unit), :], (1, 1))
        tile = 0.5 * jnp.tanh(affine[0] * energies + affine[1]) + 0.5
        if diagonal and n == 0:
            row = lax.broadcasted_iota(jnp.int32, tile.shape, 0)
            column = lax.broadcasted_iota(jnp.int32, tile.shape, 1)
            tile = tile - jnp.where(row == column, 1.0, 0.0)
        coupling[:, pl.ds(n * unit, unit)] = tile.astype(HALF)
    total, first = start, 0
    for ref in theirs:
        count = ref.shape[0]
        term = dot(coupling[:, pl.ds(first, count)], ref[...], (1, 0))
        total = term if total is None else total + term
        first += count
    return total


def sums_kernel(plan, n_inputs, n_after, diagonal, affine, *refs):
    inputs, results, coupling = refs[:n_inputs], refs[n_inputs + n_after : -1], refs[-1]
    for k, (mine, theirs, start) in enumerate(plan):
        begin = None if start is None else inputs[start][...]
        total = accumulate(
            affine, inputs[mine][...], [inputs[n] for n in theirs], coupling, begin, diagonal and k == 0
        )
        results[k][...] = total.astype(results[k].dtype)


def sums_of(affine, jobs, after=(), kind=FULL, diagonal=False, hides=True):
    inputs, plan, tiles, widest = [], [], 0, 0

    def index(array):
        for n, known in enumerate(inputs):
            if known is array:
                return n
        inputs.append(array)
        return len(inputs) - 1

    unit, width = jobs[0][0].shape
    for mine, theirs, start in jobs:
        against = sum(array.shape[0] for array in theirs)
        tiles, widest = tiles + against // unit, max(widest, against)
        plan.append(
            (index(mine), [index(array) for array in theirs], None if start is None else index(start))
        )
    return pl.pallas_call(
        functools.partial(sums_kernel, plan, len(inputs), len(after), diagonal),
        out_shape=[jax.ShapeDtypeStruct((unit, width), kind)] * len(jobs),
        in_specs=[SMEM] + [VMEM] * len(inputs) + [ANY] * len(after),
        out_specs=[VMEM] * len(jobs),
        scratch_shapes=[pltpu.VMEM((unit, widest), HALF)],
        cost_estimate=pl.CostEstimate(
            flops=4 * tiles * unit**2 * width if hides else 0,
            bytes_accessed=8 * len(jobs) * unit * width if hides else 0,
            transcendentals=tiles * unit**2 if hides else 0,
        ),
        compiler_params=PARAMS,
    )(affine, *inputs, *after)


def finish_kernel(is_first, multiplier, *refs):
    raws, (here, there, y_here, y_there), outs, (held, sems) = refs[:2], refs[2:6], refs[6:8], refs[8:]
    first = is_first[0] > 0
    cut = raws[0].shape[0] // CUTS
    copies = []
    for n in range(CUTS):
        at = pl.ds(n * cut, cut)
        totals = (here[at, :] + y_here[at, :].astype(FULL), there[at, :].astype(FULL) + y_there[at, :].astype(FULL))
        for k, raw in enumerate(raws):
            unit, scale = unit_rows(raw[at, :])
            grad = multiplier[0] * jnp.where(first, totals[k], totals[1 - k])
            held[k, at, :] = scale * (grad - unit * jnp.sum(unit * grad, axis=1, keepdims=True))
            copies.append(pltpu.make_async_copy(held.at[k, at], outs[k].at[at], sems.at[len(copies)]))
            copies[-1].start()
    for copy in copies:
        copy.wait()


def on_device(
    picture_vectors_raw, caption_vectors_raw, logit_multiplier, offset_term, incoming_adjoint
):
    rows, width = picture_vectors_raw.shape
    pairs = rows * math.prod(FINE_SIZES)
    core = lax.axis_index("core").astype(jnp.int32)
    is_first = core == 0
    first_flag = is_first.astype(FULL).reshape(1)
    affine = jnp.concatenate([0.5 * logit_multiplier, 0.5 * offset_term])
    multiplier = incoming_adjoint * logit_multiplier / pairs
    shard, unit = ((rows, width), HALF), ((2 * rows, width), HALF)
    shard_full = ((rows, width), FULL)

    image_there = other_core(picture_vectors_raw)
    text_there = other_core(caption_vectors_raw)
    image, text = local(
        lambda _, refs: [unit_rows(ref[...])[0] for ref in refs],
        [shard] * 2,
        [],
        [picture_vectors_raw, caption_vectors_raw],
    )

    def own_units(scalars, refs):
        first = scalars[0][0] > 0
        image_there, text_there, image, text = [ref[...].astype(FULL) for ref in refs]
        images, texts = (image, unit_rows(image_there)[0]), (text, unit_rows(text_there)[0])
        results = [[], []]
        for k in range(2):
            of_image = jnp.where(first, images[k], images[1 - k])
            of_text = jnp.where(first, texts[k], texts[1 - k])
            results[0].append(jnp.where(first, of_image, of_text))
            results[1].append(jnp.where(first, of_text, of_image))
        return [jnp.concatenate(halves, 0) for halves in results]

    own, own_theirs = local(
        own_units, [unit] * 2, [first_flag], [image_there, text_there, image, text]
    )

    def stacked(ways, after=()):
        (stack,) = local(
            lambda _, refs: [jnp.concatenate([ref[...] for ref in refs], 0)],
            [((2 * rows * len(ways), width), HALF)],
            [],
            [mine[way] for way in ways],
            after,
        )
        return other_core(stack)

    mine = {"": own}
    for way in ONE:
        mine[way] = sent(own, way)
    mine["xyz"] = sent(mine["x"], "yz")
    mine["xy"] = sent(mine["x"], "y")
    mine["yz"] = sent(mine["y"], "z")
    mine["zx"] = sent(mine["z"], "x")
    near = ("", *ONE)
    one = [own_theirs, stacked(ONE)]
    sums = sums_of(affine, [(mine[way], one, None) for way in near], diagonal=True, hides=False)
    sums = dict(zip(near, sums, strict=True))
    corner_there = stacked(["xyz"], [sums[""]])
    (sums["xyz"],) = sums_of(affine, [(mine["xyz"], one, None)], [sums[""]])
    two = [corner_there, stacked(TWO, [sums["xyz"], corner_there])]
    jobs = [(mine["xy"], one, None), (mine["zx"], one, None)]
    sums["xy"], sums["zx"] = sums_of(affine, jobs, [sums["xyz"]])

    def parts_of(ways, after, kind=FULL):
        return sums_of(affine, [(mine[way], two, sums[way]) for way in ways], after, kind)

    def added(part, other):
        (total,) = local(
            lambda _, refs: [refs[0][...] + refs[1][...].astype(FULL)], [unit], [], [part, other]
        )
        return total

    (part_xyz,) = parts_of(["xyz"], [sums["xy"]], HALF)
    for_yz = sent(part_xyz, "x")
    part_xy, part_zx = parts_of(["xy", "zx"], [part_xyz], HALF)
    for_x, for_z = sent(part_xy, "y"), sent(part_zx, "x")
    (part_yz,) = sums_of(affine, [(mine["yz"], one + two, None)], [part_xy])
    part_yz = added(part_yz, for_yz)
    for_y = sent(part_yz, "z")
    part_x, part_y, part_z = parts_of(ONE, [part_yz])
    part_x, part_z = added(part_x, for_x), added(part_z, for_z)
    from_x, from_z = sent(part_x, "x"), sent(part_z, "z")

    def halves(scalars, refs):
        core, total = scalars[0][0], refs[0]
        found = []
        for which in (core, 1 - core):
            at = pl.ds(pl.multiple_of(which * rows, rows), rows)
            half = total[at, :]
            for ref in refs[1:]:
                half = half + ref[at, :].astype(FULL)
            found.append(half)
        return found

    which = core.reshape(1)
    y_here, y_there = local(halves, [shard] * 2, [which], [part_y, for_y], [part_x, part_z])
    (own_part,) = parts_of([""], [y_here])
    y_here, y_there = sent(y_here, "y"), sent(y_there, "y", True)
    here, there = local(
        halves, [shard_full, shard], [which], [own_part, from_x, from_z], [y_there]
    )
    there = other_core(there)

    return tuple(
        pl.pallas_call(
            finish_kernel,
            out_shape=[jax.ShapeDtypeStruct(*shard_full)] * 2,
            in_specs=[SMEM] * 2 + [VMEM] * 6,
            out_specs=[ANY] * 2,
            scratch_shapes=[
                pltpu.VMEM((2, rows, width), FULL),
                pltpu.SemaphoreType.DMA((2 * CUTS,)),
            ],
            compiler_params=PARAMS,
        )(
            first_flag,
            multiplier,
            picture_vectors_raw,
            caption_vectors_raw,
            here,
            there,
            y_here,
            y_there,
        )
    )


def solution(mesh):
    fine = Mesh(mesh.devices.reshape(FINE_SIZES), FINE_AXES)
    rows = P(FINE_AXES, None)
    return jax.shard_map(
        on_device,
        mesh=fine,
        in_specs=(rows, rows, P(), P(), P()),
        out_specs=(rows, rows),
        check_vma=False,
    )
```

```python
import functools
import math

import jax
import jax.numpy as jnp
import numpy as np
from jax import lax
from jax.experimental import pallas as pl
from jax.experimental.pallas import tpu as pltpu
from jax.sharding import Mesh
from jax.sharding import PartitionSpec as P

FINE_AXES = ("y_lo", "core", "x", "z", "y_hi")
FINE_SIZES = (2, 2, 4, 4, 2)
RING = 4
VMEM_BYTES = 16 * 1024 * 1024
CUTS = 4
HALF = jnp.bfloat16
FULL = jnp.float32

VMEM = pl.BlockSpec(memory_space=pltpu.VMEM)
SMEM = pl.BlockSpec(memory_space=pltpu.SMEM)
ANY = pl.BlockSpec(memory_space=pl.ANY)
PARAMS = pltpu.CompilerParams(vmem_limit_bytes=VMEM_BYTES)

ONE = ("x", "y", "z")
TWO = ("xy", "yz", "zx")


def place(core, x, y, z):
    return int(np.ravel_multi_index((y % 2, core, x, z, y // 2), FINE_SIZES))


def mate(core, axis, k):
    if (core == 0) != (axis == "z"):
        return k ^ 1
    return (k + 1) % RING if k % 2 else (k - 1) % RING


def sent(value, way, crossing=False):
    pairs = []
    for at in np.ndindex(RING, RING, RING):
        for core in range(2):
            to = [mate(core, axis, k) if axis in way else k for axis, k in zip("xyz", at, strict=True)]
            pairs.append((place(core, *at), place(1 - core if crossing else core, *to)))
    return lax.ppermute(value, FINE_AXES, pairs)


def other_core(value):
    return lax.ppermute(value, "core", [(0, 1), (1, 0)])


def dot(a, b, contract):
    return lax.dot_general(a, b, ((contract[:1], contract[1:]), ((), ())), preferred_element_type=FULL)


def unit_rows(raw):
    values = raw.astype(FULL)
    scale = lax.rsqrt(jnp.mean(values * values, axis=1, keepdims=True) + 1e-06) / math.sqrt(
        values.shape[1]
    )
    return values * scale, scale


def local(body, outs, scalars, arrays, after=()):
    n_scalars, n_arrays = len(scalars), len(arrays)

    def kernel(*refs):
        given = refs[: n_scalars + n_arrays]
        results = refs[n_scalars + n_arrays + len(after) :]
        for ref, value in zip(results, body(given[:n_scalars], given[n_scalars:]), strict=True):
            ref[...] = value.astype(ref.dtype)

    return pl.pallas_call(
        kernel,
        out_shape=[jax.ShapeDtypeStruct(s, d) for s, d in outs],
        in_specs=[SMEM] * n_scalars + [VMEM] * n_arrays + [ANY] * len(after),
        out_specs=[VMEM] * len(outs),
        compiler_params=PARAMS,
    )(*scalars, *arrays, *after)


def accumulate(affine, mine, theirs, coupling, start, diagonal):
    unit = mine.shape[0]
    slope, shift = 0.5 * affine[0][0], 0.5 * affine[1][0]
    pieces = [(ref, k) for ref in theirs for k in range(0, ref.shape[0], unit)]
    for n, (ref, k) in enumerate(pieces):
        energies = dot(mine, ref[pl.ds(k, unit), :], (1, 1))
        tile = 0.5 * jnp.tanh(slope * energies + shift) + 0.5
        if diagonal and n == 0:
            row = lax.broadcasted_iota(jnp.int32, tile.shape, 0)
            column = lax.broadcasted_iota(jnp.int32, tile.shape, 1)
            tile = tile - jnp.where(row == column, 1.0, 0.0)
        coupling[:, pl.ds(n * unit, unit)] = tile.astype(HALF)
    total, first = start, 0
    for ref in theirs:
        count = ref.shape[0]
        term = dot(coupling[:, pl.ds(first, count)], ref[...], (1, 0))
        total = term if total is None else total + term
        first += count
    return total


def sums_kernel(plan, n_inputs, n_after, diagonal, *refs):
    affine, refs = refs[:2], refs[2:]
    inputs, results, coupling = refs[:n_inputs], refs[n_inputs + n_after : -1], refs[-1]
    for k, (mine, theirs, start) in enumerate(plan):
        begin = None if start is None else inputs[start][...]
        total = accumulate(
            affine, inputs[mine][...], [inputs[n] for n in theirs], coupling, begin, diagonal and k == 0
        )
        results[k][...] = total.astype(results[k].dtype)


def sums_of(affine, jobs, after=(), kind=FULL, diagonal=False, hides=True):
    inputs, plan, tiles, widest = [], [], 0, 0

    def index(array):
        for n, known in enumerate(inputs):
            if known is array:
                return n
        inputs.append(array)
        return len(inputs) - 1

    unit, width = jobs[0][0].shape
    for mine, theirs, start in jobs:
        against = sum(array.shape[0] for array in theirs)
        tiles, widest = tiles + against // unit, max(widest, against)
        plan.append(
            (index(mine), [index(array) for array in theirs], None if start is None else index(start))
        )
    return pl.pallas_call(
        functools.partial(sums_kernel, plan, len(inputs), len(after), diagonal),
        out_shape=[jax.ShapeDtypeStruct((unit, width), kind)] * len(jobs),
        in_specs=[SMEM] * 2 + [VMEM] * len(inputs) + [ANY] * len(after),
        out_specs=[VMEM] * len(jobs),
        scratch_shapes=[pltpu.VMEM((unit, widest), HALF)],
        cost_estimate=pl.CostEstimate(
            flops=4 * tiles * unit**2 * width if hides else 0,
            bytes_accessed=8 * len(jobs) * unit * width if hides else 0,
            transcendentals=tiles * unit**2 if hides else 0,
        ),
        compiler_params=PARAMS,
    )(*affine, *inputs, *after)


def finish_kernel(is_first, multiplier, *refs):
    raws, (here, there, y_here, y_there), outs, (held, sems) = refs[:2], refs[2:6], refs[6:8], refs[8:]
    first = is_first[0] > 0
    cut = raws[0].shape[0] // CUTS
    copies = []
    for n in range(CUTS):
        at = pl.ds(n * cut, cut)
        totals = (here[at, :] + y_here[at, :].astype(FULL), there[at, :].astype(FULL) + y_there[at, :].astype(FULL))
        for k, raw in enumerate(raws):
            unit, scale = unit_rows(raw[at, :])
            grad = multiplier[0] * jnp.where(first, totals[k], totals[1 - k])
            held[k, at, :] = scale * (grad - unit * jnp.sum(unit * grad, axis=1, keepdims=True))
            copies.append(pltpu.make_async_copy(held.at[k, at], outs[k].at[at], sems.at[len(copies)]))
            copies[-1].start()
    for copy in copies:
        copy.wait()


def on_device(
    picture_vectors_raw, caption_vectors_raw, logit_multiplier, offset_term, incoming_adjoint
):
    rows, width = picture_vectors_raw.shape
    pairs = rows * math.prod(FINE_SIZES)
    core = lax.axis_index("core").astype(jnp.int32)
    is_first = core == 0
    first_flag = is_first.astype(FULL).reshape(1)
    affine = (logit_multiplier, offset_term)
    multiplier = incoming_adjoint * logit_multiplier / pairs
    shard, unit = ((rows, width), HALF), ((2 * rows, width), HALF)
    shard_full = ((rows, width), FULL)

    image_there = other_core(picture_vectors_raw)
    text_there = other_core(caption_vectors_raw)
    image, text = local(
        lambda _, refs: [unit_rows(ref[...])[0] for ref in refs],
        [shard] * 2,
        [],
        [picture_vectors_raw, caption_vectors_raw],
    )

    def own_units(scalars, refs):
        first = scalars[0][0] > 0
        image_there, text_there, image, text = [ref[...].astype(FULL) for ref in refs]
        images, texts = (image, unit_rows(image_there)[0]), (text, unit_rows(text_there)[0])
        results = [[], []]
        for k in range(2):
            of_image = jnp.where(first, images[k], images[1 - k])
            of_text = jnp.where(first, texts[k], texts[1 - k])
            results[0].append(jnp.where(first, of_image, of_text))
            results[1].append(jnp.where(first, of_text, of_image))
        return [jnp.concatenate(halves, 0) for halves in results]

    own, own_theirs = local(
        own_units, [unit] * 2, [first_flag], [image_there, text_there, image, text]
    )

    def stacked(ways, after=(), scalars=()):
        (stack,) = local(
            lambda _, refs: [jnp.concatenate([ref[...] for ref in refs], 0)],
            [((2 * rows * len(ways), width), HALF)],
            scalars,
            [mine[way] for way in ways],
            after,
        )
        return other_core(stack)

    mine = {"": own}
    for way in ONE:
        mine[way] = sent(own, way)
    mine["xyz"] = sent(mine["x"], "yz")
    mine["xy"] = sent(mine["x"], "y")
    mine["yz"] = sent(mine["y"], "z")
    mine["zx"] = sent(mine["z"], "x")
    near = ("", *ONE)
    one = [own_theirs, stacked(ONE, scalars=affine)]
    sums = sums_of(affine, [(mine[way], one, None) for way in near], diagonal=True, hides=False)
    sums = dict(zip(near, sums, strict=True))
    corner_there = stacked(["xyz"], [sums[""]])
    (sums["xyz"],) = sums_of(affine, [(mine["xyz"], one, None)], [sums[""]])
    two = [corner_there, stacked(TWO, [sums["xyz"], corner_there])]
    jobs = [(mine["xy"], one, None), (mine["zx"], one, None)]
    sums["xy"], sums["zx"] = sums_of(affine, jobs, [sums["xyz"]])

    def parts_of(ways, after, kind=FULL):
        return sums_of(affine, [(mine[way], two, sums[way]) for way in ways], after, kind)

    def added(part, other):
        (total,) = local(
            lambda _, refs: [refs[0][...] + refs[1][...].astype(FULL)], [unit], [], [part, other]
        )
        return total

    (part_xyz,) = parts_of(["xyz"], [sums["xy"]], HALF)
    for_yz = sent(part_xyz, "x")
    part_xy, part_zx = parts_of(["xy", "zx"], [part_xyz], HALF)
    for_x, for_z = sent(part_xy, "y"), sent(part_zx, "x")
    (part_yz,) = sums_of(affine, [(mine["yz"], one + two, None)], [part_xy])
    part_yz = added(part_yz, for_yz)
    for_y = sent(part_yz, "z")
    part_x, part_y, part_z = parts_of(ONE, [part_yz])
    part_x, part_z = added(part_x, for_x), added(part_z, for_z)
    from_x, from_z = sent(part_x, "x"), sent(part_z, "z")

    def halves(scalars, refs):
        core, total = scalars[0][0], refs[0]
        found = []
        for which in (core, 1 - core):
            at = pl.ds(pl.multiple_of(which * rows, rows), rows)
            half = total[at, :]
            for ref in refs[1:]:
                half = half + ref[at, :].astype(FULL)
            found.append(half)
        return found

    which = core.reshape(1)
    y_here, y_there = local(halves, [shard] * 2, [which], [part_y, for_y], [part_x, part_z])
    (own_part,) = parts_of([""], [y_here])
    y_here, y_there = sent(y_here, "y"), sent(y_there, "y", True)
    here, there = local(
        halves, [shard_full, shard], [which], [own_part, from_x, from_z], [y_there]
    )
    there = other_core(there)

    return tuple(
        pl.pallas_call(
            finish_kernel,
            out_shape=[jax.ShapeDtypeStruct(*shard_full)] * 2,
            in_specs=[SMEM] * 2 + [VMEM] * 6,
            out_specs=[ANY] * 2,
            scratch_shapes=[
                pltpu.VMEM((2, rows, width), FULL),
                pltpu.SemaphoreType.DMA((2 * CUTS,)),
            ],
            compiler_params=PARAMS,
        )(
            first_flag,
            multiplier,
            picture_vectors_raw,
            caption_vectors_raw,
            here,
            there,
            y_here,
            y_there,
        )
    )


def solution(mesh):
    fine = Mesh(mesh.devices.reshape(FINE_SIZES), FINE_AXES)
    rows = P(FINE_AXES, None)
    return jax.shard_map(
        on_device,
        mesh=fine,
        in_specs=(rows, rows, P(), P(), P()),
        out_specs=(rows, rows),
        check_vma=False,
    )
```

```python
import functools
import math

import jax
import jax.numpy as jnp
import numpy as np
from jax import lax
from jax.experimental import pallas as pl
from jax.experimental.pallas import tpu as pltpu
from jax.sharding import Mesh
from jax.sharding import PartitionSpec as P

FINE_AXES = ("y_lo", "core", "x", "z", "y_hi")
FINE_SIZES = (2, 2, 4, 4, 2)
RING = 4
VMEM_BYTES = 16 * 1024 * 1024
CUTS = 4
HALF = jnp.bfloat16
FULL = jnp.float32

VMEM = pl.BlockSpec(memory_space=pltpu.VMEM)
SMEM = pl.BlockSpec(memory_space=pltpu.SMEM)
ANY = pl.BlockSpec(memory_space=pl.ANY)
PARAMS = pltpu.CompilerParams(vmem_limit_bytes=VMEM_BYTES)

ONE = ("x", "y", "z")
TWO = ("xy", "yz", "zx")


def place(core, x, y, z):
    return int(np.ravel_multi_index((y % 2, core, x, z, y // 2), FINE_SIZES))


def mate(core, axis, k):
    if (core == 0) != (axis == "z"):
        return k ^ 1
    return (k + 1) % RING if k % 2 else (k - 1) % RING


def sent(value, way, crossing=False):
    pairs = []
    for at in np.ndindex(RING, RING, RING):
        for core in range(2):
            to = [mate(core, axis, k) if axis in way else k for axis, k in zip("xyz", at, strict=True)]
            pairs.append((place(core, *at), place(1 - core if crossing else core, *to)))
    return lax.ppermute(value, FINE_AXES, pairs)


def other_core(value):
    return lax.ppermute(value, "core", [(0, 1), (1, 0)])


def dot(a, b, contract):
    return lax.dot_general(a, b, ((contract[:1], contract[1:]), ((), ())), preferred_element_type=FULL)


def unit_rows(raw):
    values = raw.astype(FULL)
    scale = lax.rsqrt(jnp.mean(values * values, axis=1, keepdims=True) + 1e-06) / math.sqrt(
        values.shape[1]
    )
    return values * scale, scale


def local(body, outs, scalars, arrays, after=()):
    n_scalars, n_arrays = len(scalars), len(arrays)

    def kernel(*refs):
        given = refs[: n_scalars + n_arrays]
        results = refs[n_scalars + n_arrays + len(after) :]
        for ref, value in zip(results, body(given[:n_scalars], given[n_scalars:]), strict=True):
            ref[...] = value.astype(ref.dtype)

    return pl.pallas_call(
        kernel,
        out_shape=[jax.ShapeDtypeStruct(s, d) for s, d in outs],
        in_specs=[SMEM] * n_scalars + [VMEM] * n_arrays + [ANY] * len(after),
        out_specs=[VMEM] * len(outs),
        compiler_params=PARAMS,
    )(*scalars, *arrays, *after)


def accumulate(affine, mine, theirs, coupling, start, diagonal):
    unit = mine.shape[0]
    slope, shift = 0.5 * affine[0][0], 0.5 * affine[1][0]
    pieces = [(ref, k) for ref in theirs for k in range(0, ref.shape[0], unit)]
    for n, (ref, k) in enumerate(pieces):
        energies = dot(mine, ref[pl.ds(k, unit), :], (1, 1))
        tile = 0.5 * jnp.tanh(slope * energies + shift) + 0.5
        if diagonal and n == 0:
            row = lax.broadcasted_iota(jnp.int32, tile.shape, 0)
            column = lax.broadcasted_iota(jnp.int32, tile.shape, 1)
            tile = tile - jnp.where(row == column, 1.0, 0.0)
        coupling[:, pl.ds(n * unit, unit)] = tile.astype(HALF)
    total, first = start, 0
    for ref in theirs:
        count = ref.shape[0]
        term = dot(coupling[:, pl.ds(first, count)], ref[...], (1, 0))
        total = term if total is None else total + term
        first += count
    return total


def sums_kernel(plan, n_inputs, n_after, diagonal, *refs):
    affine, refs = refs[:2], refs[2:]
    inputs, results, coupling = refs[:n_inputs], refs[n_inputs + n_after : -1], refs[-1]
    for k, (mine, theirs, start) in enumerate(plan):
        begin = None if start is None else inputs[start][...]
        total = accumulate(
            affine, inputs[mine][...], [inputs[n] for n in theirs], coupling, begin, diagonal and k == 0
        )
        results[k][...] = total.astype(results[k].dtype)


def sums_of(affine, jobs, after=(), kind=FULL, diagonal=False, hides=True):
    inputs, plan, tiles, widest = [], [], 0, 0

    def index(array):
        for n, known in enumerate(inputs):
            if known is array:
                return n
        inputs.append(array)
        return len(inputs) - 1

    unit, width = jobs[0][0].shape
    for mine, theirs, start in jobs:
        against = sum(array.shape[0] for array in theirs)
        tiles, widest = tiles + against // unit, max(widest, against)
        plan.append(
            (index(mine), [index(array) for array in theirs], None if start is None else index(start))
        )
    return pl.pallas_call(
        functools.partial(sums_kernel, plan, len(inputs), len(after), diagonal),
        out_shape=[jax.ShapeDtypeStruct((unit, width), kind)] * len(jobs),
        in_specs=[SMEM] * 2 + [VMEM] * len(inputs) + [ANY] * len(after),
        out_specs=[VMEM] * len(jobs),
        scratch_shapes=[pltpu.VMEM((unit, widest), HALF)],
        cost_estimate=pl.CostEstimate(
            flops=4 * tiles * unit**2 * width if hides else 0,
            bytes_accessed=8 * len(jobs) * unit * width if hides else 0,
            transcendentals=tiles * unit**2 if hides else 0,
        ),
        compiler_params=PARAMS,
    )(*affine, *inputs, *after)


def finish_kernel(is_first, multiplier, *refs):
    raws, (here, there, y_here, y_there), outs, (held, sems) = refs[:2], refs[2:6], refs[6:8], refs[8:]
    first = is_first[0] > 0
    cut = raws[0].shape[0] // CUTS
    copies = []
    for n in range(CUTS):
        at = pl.ds(n * cut, cut)
        totals = (here[at, :] + y_here[at, :].astype(FULL), there[at, :].astype(FULL) + y_there[at, :].astype(FULL))
        for k, raw in enumerate(raws):
            unit, scale = unit_rows(raw[at, :])
            grad = multiplier[0] * jnp.where(first, totals[k], totals[1 - k])
            held[k, at, :] = scale * (grad - unit * jnp.sum(unit * grad, axis=1, keepdims=True))
            copies.append(pltpu.make_async_copy(held.at[k, at], outs[k].at[at], sems.at[len(copies)]))
            copies[-1].start()
    for copy in copies:
        copy.wait()


def on_device(
    picture_vectors_raw, caption_vectors_raw, logit_multiplier, offset_term, incoming_adjoint
):
    rows, width = picture_vectors_raw.shape
    pairs = rows * math.prod(FINE_SIZES)
    core = lax.axis_index("core").astype(jnp.int32)
    is_first = core == 0
    first_flag = is_first.astype(FULL).reshape(1)
    affine = (logit_multiplier, offset_term)
    multiplier = incoming_adjoint * logit_multiplier / pairs
    shard, unit = ((rows, width), HALF), ((2 * rows, width), HALF)
    shard_full = ((rows, width), FULL)

    image_there = other_core(picture_vectors_raw)
    text_there = other_core(caption_vectors_raw)
    def own_shards(_, refs):
        units = unit_rows(refs[0][...])[0]
        return [units[:rows], units[rows:]]

    both = jnp.concatenate([picture_vectors_raw, caption_vectors_raw], 0)
    image, text = local(own_shards, [shard] * 2, [], [both])

    def own_units(scalars, refs):
        first = scalars[0][0] > 0
        image_there, text_there, image, text = [ref[...].astype(FULL) for ref in refs]
        images, texts = (image, unit_rows(image_there)[0]), (text, unit_rows(text_there)[0])
        results = [[], []]
        for k in range(2):
            of_image = jnp.where(first, images[k], images[1 - k])
            of_text = jnp.where(first, texts[k], texts[1 - k])
            results[0].append(jnp.where(first, of_image, of_text))
            results[1].append(jnp.where(first, of_text, of_image))
        return [jnp.concatenate(halves, 0) for halves in results]

    own, own_theirs = local(
        own_units, [unit] * 2, [first_flag], [image_there, text_there, image, text]
    )

    def stacked(ways, after=(), scalars=()):
        (stack,) = local(
            lambda _, refs: [jnp.concatenate([ref[...] for ref in refs], 0)],
            [((2 * rows * len(ways), width), HALF)],
            scalars,
            [mine[way] for way in ways],
            after,
        )
        return other_core(stack)

    mine = {"": own}
    for way in ONE:
        mine[way] = sent(own, way)
    mine["xyz"] = sent(mine["x"], "yz")
    mine["xy"] = sent(mine["x"], "y")
    mine["yz"] = sent(mine["y"], "z")
    mine["zx"] = sent(mine["z"], "x")
    near = ("", *ONE)
    one = [own_theirs, stacked(ONE, scalars=affine)]
    sums = sums_of(affine, [(mine[way], one, None) for way in near], diagonal=True, hides=False)
    sums = dict(zip(near, sums, strict=True))
    corner_there = stacked(["xyz"], [sums[""]])
    (sums["xyz"],) = sums_of(affine, [(mine["xyz"], one, None)], [sums[""]])
    two = [corner_there, stacked(TWO, [sums["xyz"], corner_there])]
    jobs = [(mine["xy"], one, None), (mine["zx"], one, None)]
    sums["xy"], sums["zx"] = sums_of(affine, jobs, [sums["xyz"]])

    def parts_of(ways, after, kind=FULL):
        return sums_of(affine, [(mine[way], two, sums[way]) for way in ways], after, kind)

    def added(part, other):
        (total,) = local(
            lambda _, refs: [refs[0][...] + refs[1][...].astype(FULL)], [unit], [], [part, other]
        )
        return total

    (part_xyz,) = parts_of(["xyz"], [sums["xy"]], HALF)
    for_yz = sent(part_xyz, "x")
    part_xy, part_zx = parts_of(["xy", "zx"], [part_xyz], HALF)
    for_x, for_z = sent(part_xy, "y"), sent(part_zx, "x")
    (part_yz,) = sums_of(affine, [(mine["yz"], one + two, None)], [part_xy])
    part_yz = added(part_yz, for_yz)
    for_y = sent(part_yz, "z")
    part_x, part_y, part_z = parts_of(ONE, [part_yz])
    part_x, part_z = added(part_x, for_x), added(part_z, for_z)
    from_x, from_z = sent(part_x, "x"), sent(part_z, "z")

    def halves(scalars, refs):
        core, total = scalars[0][0], refs[0]
        found = []
        for which in (core, 1 - core):
            at = pl.ds(pl.multiple_of(which * rows, rows), rows)
            half = total[at, :]
            for ref in refs[1:]:
                half = half + ref[at, :].astype(FULL)
            found.append(half)
        return found

    which = core.reshape(1)
    y_here, y_there = local(halves, [shard] * 2, [which], [part_y, for_y], [part_x, part_z])
    (own_part,) = parts_of([""], [y_here])
    y_here, y_there = sent(y_here, "y"), sent(y_there, "y", True)
    here, there = local(
        halves, [shard_full, shard], [which], [own_part, from_x, from_z], [y_there]
    )
    there = other_core(there)

    return tuple(
        pl.pallas_call(
            finish_kernel,
            out_shape=[jax.ShapeDtypeStruct(*shard_full)] * 2,
            in_specs=[SMEM] * 2 + [VMEM] * 6,
            out_specs=[ANY] * 2,
            scratch_shapes=[
                pltpu.VMEM((2, rows, width), FULL),
                pltpu.SemaphoreType.DMA((2 * CUTS,)),
            ],
            compiler_params=PARAMS,
        )(
            first_flag,
            multiplier,
            picture_vectors_raw,
            caption_vectors_raw,
            here,
            there,
            y_here,
            y_there,
        )
    )


def solution(mesh):
    fine = Mesh(mesh.devices.reshape(FINE_SIZES), FINE_AXES)
    rows = P(FINE_AXES, None)
    return jax.shard_map(
        on_device,
        mesh=fine,
        in_specs=(rows, rows, P(), P(), P()),
        out_specs=(rows, rows),
        check_vma=False,
    )
```

```python
import functools
import math

import jax
import jax.numpy as jnp
import numpy as np
from jax import lax
from jax.experimental import pallas as pl
from jax.experimental.pallas import tpu as pltpu
from jax.sharding import Mesh
from jax.sharding import PartitionSpec as P

FINE_AXES = ("y_lo", "core", "x", "z", "y_hi")
FINE_SIZES = (2, 2, 4, 4, 2)
RING = 4
VMEM_BYTES = 16 * 1024 * 1024
CUTS = 4
HALF = jnp.bfloat16
FULL = jnp.float32

VMEM = pl.BlockSpec(memory_space=pltpu.VMEM)
SMEM = pl.BlockSpec(memory_space=pltpu.SMEM)
ANY = pl.BlockSpec(memory_space=pl.ANY)
PARAMS = pltpu.CompilerParams(vmem_limit_bytes=VMEM_BYTES)

ONE = ("x", "y", "z")
TWO = ("xy", "yz", "zx")


def place(core, x, y, z):
    return int(np.ravel_multi_index((y % 2, core, x, z, y // 2), FINE_SIZES))


def mate(core, axis, k):
    if (core == 0) != (axis == "z"):
        return k ^ 1
    return (k + 1) % RING if k % 2 else (k - 1) % RING


def sent(value, way, crossing=False):
    pairs = []
    for at in np.ndindex(RING, RING, RING):
        for core in range(2):
            to = [mate(core, axis, k) if axis in way else k for axis, k in zip("xyz", at, strict=True)]
            pairs.append((place(core, *at), place(1 - core if crossing else core, *to)))
    return lax.ppermute(value, FINE_AXES, pairs)


def other_core(value):
    return lax.ppermute(value, "core", [(0, 1), (1, 0)])


def dot(a, b, contract):
    return lax.dot_general(a, b, ((contract[:1], contract[1:]), ((), ())), preferred_element_type=FULL)


def unit_rows(raw):
    values = raw.astype(FULL)
    scale = lax.rsqrt(jnp.mean(values * values, axis=1, keepdims=True) + 1e-06) / math.sqrt(
        values.shape[1]
    )
    return values * scale, scale


def local(body, outs, scalars, arrays, after=()):
    n_scalars, n_arrays = len(scalars), len(arrays)

    def kernel(*refs):
        given = refs[: n_scalars + n_arrays]
        results = refs[n_scalars + n_arrays + len(after) :]
        for ref, value in zip(results, body(given[:n_scalars], given[n_scalars:]), strict=True):
            ref[...] = value.astype(ref.dtype)

    return pl.pallas_call(
        kernel,
        out_shape=[jax.ShapeDtypeStruct(s, d) for s, d in outs],
        in_specs=[SMEM] * n_scalars + [VMEM] * n_arrays + [ANY] * len(after),
        out_specs=[VMEM] * len(outs),
        compiler_params=PARAMS,
    )(*scalars, *arrays, *after)


def accumulate(affine, mine, theirs, coupling, start, diagonal):
    unit = mine.shape[0]
    slope, shift = 0.5 * affine[0][0], 0.5 * affine[1][0]
    pieces = [(ref, k) for ref in theirs for k in range(0, ref.shape[0], unit)]
    for n, (ref, k) in enumerate(pieces):
        energies = dot(mine, ref[pl.ds(k, unit), :], (1, 1))
        tile = 0.5 * jnp.tanh(slope * energies + shift) + 0.5
        if diagonal and n == 0:
            row = lax.broadcasted_iota(jnp.int32, tile.shape, 0)
            column = lax.broadcasted_iota(jnp.int32, tile.shape, 1)
            tile = tile - jnp.where(row == column, 1.0, 0.0)
        coupling[:, pl.ds(n * unit, unit)] = tile.astype(HALF)
    total, first = start, 0
    for ref in theirs:
        count = ref.shape[0]
        term = dot(coupling[:, pl.ds(first, count)], ref[...], (1, 0))
        total = term if total is None else total + term
        first += count
    return total


def sums_kernel(plan, n_inputs, n_after, diagonal, *refs):
    affine, refs = refs[:2], refs[2:]
    inputs, results, coupling = refs[:n_inputs], refs[n_inputs + n_after : -1], refs[-1]
    for k, (mine, theirs, start) in enumerate(plan):
        begin = None if start is None else inputs[start][...]
        total = accumulate(
            affine, inputs[mine][...], [inputs[n] for n in theirs], coupling, begin, diagonal and k == 0
        )
        results[k][...] = total.astype(results[k].dtype)


def sums_of(affine, jobs, after=(), kind=FULL, diagonal=False, hides=True):
    inputs, plan, tiles, widest = [], [], 0, 0

    def index(array):
        for n, known in enumerate(inputs):
            if known is array:
                return n
        inputs.append(array)
        return len(inputs) - 1

    unit, width = jobs[0][0].shape
    for mine, theirs, start in jobs:
        against = sum(array.shape[0] for array in theirs)
        tiles, widest = tiles + against // unit, max(widest, against)
        plan.append(
            (index(mine), [index(array) for array in theirs], None if start is None else index(start))
        )
    return pl.pallas_call(
        functools.partial(sums_kernel, plan, len(inputs), len(after), diagonal),
        out_shape=[jax.ShapeDtypeStruct((unit, width), kind)] * len(jobs),
        in_specs=[SMEM] * 2 + [VMEM] * len(inputs) + [ANY] * len(after),
        out_specs=[VMEM] * len(jobs),
        scratch_shapes=[pltpu.VMEM((unit, widest), HALF)],
        cost_estimate=pl.CostEstimate(
            flops=4 * tiles * unit**2 * width if hides else 0,
            bytes_accessed=8 * len(jobs) * unit * width if hides else 0,
            transcendentals=tiles * unit**2 if hides else 0,
        ),
        compiler_params=PARAMS,
    )(*affine, *inputs, *after)


def finish_kernel(is_first, multiplier, *refs):
    raws, (here, there, y_here, y_there), outs, (held, sems) = refs[:2], refs[2:6], refs[6:8], refs[8:]
    first = is_first[0] > 0
    cut = raws[0].shape[0] // CUTS
    copies = []
    for n in range(CUTS):
        at = pl.ds(n * cut, cut)
        totals = (here[at, :] + y_here[at, :].astype(FULL), there[at, :].astype(FULL) + y_there[at, :].astype(FULL))
        for k, raw in enumerate(raws):
            unit, scale = unit_rows(raw[at, :])
            grad = multiplier[0] * jnp.where(first, totals[k], totals[1 - k])
            held[k, at, :] = scale * (grad - unit * jnp.sum(unit * grad, axis=1, keepdims=True))
            copies.append(pltpu.make_async_copy(held.at[k, at], outs[k].at[at], sems.at[len(copies)]))
            copies[-1].start()
    for copy in copies:
        copy.wait()


def on_device(
    picture_vectors_raw, caption_vectors_raw, logit_multiplier, offset_term, incoming_adjoint
):
    rows, width = picture_vectors_raw.shape
    pairs = rows * math.prod(FINE_SIZES)
    core = lax.axis_index("core").astype(jnp.int32)
    is_first = core == 0
    first_flag = is_first.astype(FULL).reshape(1)
    affine = (logit_multiplier, offset_term)
    multiplier = incoming_adjoint * logit_multiplier / pairs
    shard, unit = ((rows, width), HALF), ((2 * rows, width), HALF)
    shard_full = ((rows, width), FULL)

    image_there = other_core(picture_vectors_raw)
    text_there = other_core(caption_vectors_raw)
    def own_shards(_, refs):
        units = unit_rows(refs[0][...])[0]
        return [units[:rows], units[rows:]]

    both = jnp.concatenate([picture_vectors_raw, caption_vectors_raw], 0)
    image, text = local(own_shards, [shard] * 2, [], [both])

    def own_units(scalars, refs):
        first = scalars[0][0] > 0
        image_there, text_there, image, text = [ref[...].astype(FULL) for ref in refs]
        images, texts = (image, unit_rows(image_there)[0]), (text, unit_rows(text_there)[0])
        results = [[], []]
        for k in range(2):
            of_image = jnp.where(first, images[k], images[1 - k])
            of_text = jnp.where(first, texts[k], texts[1 - k])
            results[0].append(jnp.where(first, of_image, of_text))
            results[1].append(jnp.where(first, of_text, of_image))
        return [jnp.concatenate(halves, 0) for halves in results]

    own, own_theirs = local(
        own_units, [unit] * 2, [first_flag], [image_there, text_there, image, text]
    )

    def stacked(ways, after=(), scalars=()):
        (stack,) = local(
            lambda _, refs: [jnp.concatenate([ref[...] for ref in refs], 0)],
            [((2 * rows * len(ways), width), HALF)],
            scalars,
            [mine[way] for way in ways],
            after,
        )
        return other_core(stack)

    mine = {"": own}
    for way in ONE:
        mine[way] = sent(own, way)
    mine["xyz"] = sent(mine["z"], "xy")
    mine["xy"] = sent(mine["x"], "y")
    mine["yz"] = sent(mine["y"], "z")
    mine["zx"] = sent(mine["z"], "x")
    near = ("", *ONE)
    one = [own_theirs, stacked(ONE, scalars=affine)]
    sums = sums_of(affine, [(mine[way], one, None) for way in near], diagonal=True, hides=False)
    sums = dict(zip(near, sums, strict=True))
    corner_there = stacked(["xyz"], [sums[""]])
    (sums["xyz"],) = sums_of(affine, [(mine["xyz"], one, None)], [sums[""]])
    two = [corner_there, stacked(TWO, [sums["xyz"], corner_there])]
    jobs = [(mine["xy"], one, None), (mine["zx"], one, None)]
    sums["xy"], sums["zx"] = sums_of(affine, jobs, [sums["xyz"]])

    def parts_of(ways, after, kind=FULL):
        return sums_of(affine, [(mine[way], two, sums[way]) for way in ways], after, kind)

    def added(part, other):
        (total,) = local(
            lambda _, refs: [refs[0][...] + refs[1][...].astype(FULL)], [unit], [], [part, other]
        )
        return total

    (part_xyz,) = parts_of(["xyz"], [sums["xy"]], HALF)
    for_yz = sent(part_xyz, "x")
    part_xy, part_zx = parts_of(["xy", "zx"], [part_xyz], HALF)
    for_x, for_z = sent(part_xy, "y"), sent(part_zx, "x")
    (part_yz,) = sums_of(affine, [(mine["yz"], one + two, None)], [part_xy])
    part_yz = added(part_yz, for_yz)
    for_y = sent(part_yz, "z")
    part_x, part_y, part_z = parts_of(ONE, [part_yz])
    part_x, part_z = added(part_x, for_x), added(part_z, for_z)
    from_x, from_z = sent(part_x, "x"), sent(part_z, "z")

    def halves(scalars, refs):
        core, total = scalars[0][0], refs[0]
        found = []
        for which in (core, 1 - core):
            at = pl.ds(pl.multiple_of(which * rows, rows), rows)
            half = total[at, :]
            for ref in refs[1:]:
                half = half + ref[at, :].astype(FULL)
            found.append(half)
        return found

    which = core.reshape(1)
    y_here, y_there = local(halves, [shard] * 2, [which], [part_y, for_y], [part_x, part_z])
    (own_part,) = parts_of([""], [y_here])
    y_here, y_there = sent(y_here, "y"), sent(y_there, "y", True)
    here, there = local(
        halves, [shard_full, shard], [which], [own_part, from_x, from_z], [y_there]
    )
    there = other_core(there)

    return tuple(
        pl.pallas_call(
            finish_kernel,
            out_shape=[jax.ShapeDtypeStruct(*shard_full)] * 2,
            in_specs=[SMEM] * 2 + [VMEM] * 6,
            out_specs=[ANY] * 2,
            scratch_shapes=[
                pltpu.VMEM((2, rows, width), FULL),
                pltpu.SemaphoreType.DMA((2 * CUTS,)),
            ],
            compiler_params=PARAMS,
        )(
            first_flag,
            multiplier,
            picture_vectors_raw,
            caption_vectors_raw,
            here,
            there,
            y_here,
            y_there,
        )
    )


def solution(mesh):
    fine = Mesh(mesh.devices.reshape(FINE_SIZES), FINE_AXES)
    rows = P(FINE_AXES, None)
    return jax.shard_map(
        on_device,
        mesh=fine,
        in_specs=(rows, rows, P(), P(), P()),
        out_specs=(rows, rows),
        check_vma=False,
    )
```

```python
import functools
import math

import jax
import jax.numpy as jnp
import numpy as np
from jax import lax
from jax.experimental import pallas as pl
from jax.experimental.pallas import tpu as pltpu
from jax.sharding import Mesh
from jax.sharding import PartitionSpec as P

FINE_AXES = ("y_lo", "core", "x", "z", "y_hi")
FINE_SIZES = (2, 2, 4, 4, 2)
RING = 4
VMEM_BYTES = 16 * 1024 * 1024
CUTS = 4
HALF = jnp.bfloat16
FULL = jnp.float32

VMEM = pl.BlockSpec(memory_space=pltpu.VMEM)
SMEM = pl.BlockSpec(memory_space=pltpu.SMEM)
ANY = pl.BlockSpec(memory_space=pl.ANY)
PARAMS = pltpu.CompilerParams(vmem_limit_bytes=VMEM_BYTES)

NAMES = ({"x": "x", "y": "y", "z": "z"}, {"x": "z", "y": "y", "z": "x"})
ONE = ("x", "y", "z")
TWO = ("xy", "yz", "zx")


def place(core, x, y, z):
    return int(np.ravel_multi_index((y % 2, core, x, z, y // 2), FINE_SIZES))


def mate(core, axis, k):
    if (core == 0) != (axis == "z"):
        return k ^ 1
    return (k + 1) % RING if k % 2 else (k - 1) % RING


def sent(value, way, crossing=False):
    pairs = []
    for at in np.ndindex(RING, RING, RING):
        for core in range(2):
            to = [
                mate(core, axis, k) if NAMES[core][axis] in way else k
                for axis, k in zip("xyz", at, strict=True)
            ]
            pairs.append((place(core, *at), place(1 - core if crossing else core, *to)))
    return lax.ppermute(value, FINE_AXES, pairs)


def other_core(value):
    return lax.ppermute(value, "core", [(0, 1), (1, 0)])


def dot(a, b, contract):
    return lax.dot_general(a, b, ((contract[:1], contract[1:]), ((), ())), preferred_element_type=FULL)


def unit_rows(raw):
    values = raw.astype(FULL)
    scale = lax.rsqrt(jnp.mean(values * values, axis=1, keepdims=True) + 1e-06) / math.sqrt(
        values.shape[1]
    )
    return values * scale, scale


def local(body, outs, scalars, arrays, after=()):
    n_scalars, n_arrays = len(scalars), len(arrays)

    def kernel(*refs):
        given = refs[: n_scalars + n_arrays]
        results = refs[n_scalars + n_arrays + len(after) :]
        for ref, value in zip(results, body(given[:n_scalars], given[n_scalars:]), strict=True):
            ref[...] = value.astype(ref.dtype)

    return pl.pallas_call(
        kernel,
        out_shape=[jax.ShapeDtypeStruct(s, d) for s, d in outs],
        in_specs=[SMEM] * n_scalars + [VMEM] * n_arrays + [ANY] * len(after),
        out_specs=[VMEM] * len(outs),
        compiler_params=PARAMS,
    )(*scalars, *arrays, *after)


def accumulate(affine, mine, theirs, coupling, start, diagonal):
    unit = mine.shape[0]
    slope, shift = 0.5 * affine[0][0], 0.5 * affine[1][0]
    pieces = [(ref, k) for ref in theirs for k in range(0, ref.shape[0], unit)]
    for n, (ref, k) in enumerate(pieces):
        energies = dot(mine, ref[pl.ds(k, unit), :], (1, 1))
        tile = 0.5 * jnp.tanh(slope * energies + shift) + 0.5
        if diagonal and n == 0:
            row = lax.broadcasted_iota(jnp.int32, tile.shape, 0)
            column = lax.broadcasted_iota(jnp.int32, tile.shape, 1)
            tile = tile - jnp.where(row == column, 1.0, 0.0)
        coupling[:, pl.ds(n * unit, unit)] = tile.astype(HALF)
    total, first = start, 0
    for ref in theirs:
        count = ref.shape[0]
        term = dot(coupling[:, pl.ds(first, count)], ref[...], (1, 0))
        total = term if total is None else total + term
        first += count
    return total


def sums_kernel(plan, n_inputs, n_after, diagonal, *refs):
    affine, refs = refs[:2], refs[2:]
    inputs, results, coupling = refs[:n_inputs], refs[n_inputs + n_after : -1], refs[-1]
    for k, (mine, theirs, start) in enumerate(plan):
        begin = None if start is None else inputs[start][...]
        total = accumulate(
            affine, inputs[mine][...], [inputs[n] for n in theirs], coupling, begin, diagonal and k == 0
        )
        results[k][...] = total.astype(results[k].dtype)


def sums_of(affine, jobs, after=(), kind=FULL, diagonal=False, hides=True):
    inputs, plan, tiles, widest = [], [], 0, 0

    def index(array):
        for n, known in enumerate(inputs):
            if known is array:
                return n
        inputs.append(array)
        return len(inputs) - 1

    unit, width = jobs[0][0].shape
    for mine, theirs, start in jobs:
        against = sum(array.shape[0] for array in theirs)
        tiles, widest = tiles + against // unit, max(widest, against)
        plan.append(
            (index(mine), [index(array) for array in theirs], None if start is None else index(start))
        )
    return pl.pallas_call(
        functools.partial(sums_kernel, plan, len(inputs), len(after), diagonal),
        out_shape=[jax.ShapeDtypeStruct((unit, width), kind)] * len(jobs),
        in_specs=[SMEM] * 2 + [VMEM] * len(inputs) + [ANY] * len(after),
        out_specs=[VMEM] * len(jobs),
        scratch_shapes=[pltpu.VMEM((unit, widest), HALF)],
        cost_estimate=pl.CostEstimate(
            flops=4 * tiles * unit**2 * width if hides else 0,
            bytes_accessed=8 * len(jobs) * unit * width if hides else 0,
            transcendentals=tiles * unit**2 if hides else 0,
        ),
        compiler_params=PARAMS,
    )(*affine, *inputs, *after)


def finish_kernel(is_first, multiplier, *refs):
    raws, (here, there, y_here, y_there), outs, (held, sems) = refs[:2], refs[2:6], refs[6:8], refs[8:]
    first = is_first[0] > 0
    cut = raws[0].shape[0] // CUTS
    copies = []
    for n in range(CUTS):
        at = pl.ds(n * cut, cut)
        totals = (here[at, :] + y_here[at, :].astype(FULL), there[at, :].astype(FULL) + y_there[at, :].astype(FULL))
        for k, raw in enumerate(raws):
            unit, scale = unit_rows(raw[at, :])
            grad = multiplier[0] * jnp.where(first, totals[k], totals[1 - k])
            held[k, at, :] = scale * (grad - unit * jnp.sum(unit * grad, axis=1, keepdims=True))
            copies.append(pltpu.make_async_copy(held.at[k, at], outs[k].at[at], sems.at[len(copies)]))
            copies[-1].start()
    for copy in copies:
        copy.wait()


def on_device(
    picture_vectors_raw, caption_vectors_raw, logit_multiplier, offset_term, incoming_adjoint
):
    rows, width = picture_vectors_raw.shape
    pairs = rows * math.prod(FINE_SIZES)
    core = lax.axis_index("core").astype(jnp.int32)
    is_first = core == 0
    first_flag = is_first.astype(FULL).reshape(1)
    affine = (logit_multiplier, offset_term)
    multiplier = incoming_adjoint * logit_multiplier / pairs
    shard, unit = ((rows, width), HALF), ((2 * rows, width), HALF)
    shard_full = ((rows, width), FULL)

    image_there = other_core(picture_vectors_raw)
    text_there = other_core(caption_vectors_raw)
    def own_shards(_, refs):
        units = unit_rows(refs[0][...])[0]
        return [units[:rows], units[rows:]]

    both = jnp.concatenate([picture_vectors_raw, caption_vectors_raw], 0)
    image, text = local(own_shards, [shard] * 2, [], [both])

    def own_units(scalars, refs):
        first = scalars[0][0] > 0
        image_there, text_there, image, text = [ref[...].astype(FULL) for ref in refs]
        images, texts = (image, unit_rows(image_there)[0]), (text, unit_rows(text_there)[0])
        results = [[], []]
        for k in range(2):
            of_image = jnp.where(first, images[k], images[1 - k])
            of_text = jnp.where(first, texts[k], texts[1 - k])
            results[0].append(jnp.where(first, of_image, of_text))
            results[1].append(jnp.where(first, of_text, of_image))
        return [jnp.concatenate(halves, 0) for halves in results]

    own, own_theirs = local(
        own_units, [unit] * 2, [first_flag], [image_there, text_there, image, text]
    )

    def stacked(ways, after=(), scalars=()):
        (stack,) = local(
            lambda _, refs: [jnp.concatenate([ref[...] for ref in refs], 0)],
            [((2 * rows * len(ways), width), HALF)],
            scalars,
            [mine[way] for way in ways],
            after,
        )
        return other_core(stack)

    mine = {"": own}
    for way in ONE:
        mine[way] = sent(own, way)
    mine["xyz"] = sent(mine["z"], "xy")
    mine["xy"] = sent(mine["x"], "y")
    mine["yz"] = sent(mine["y"], "z")
    mine["zx"] = sent(mine["z"], "x")
    near = ("", *ONE)
    one = [own_theirs, stacked(ONE, scalars=affine)]
    sums = sums_of(affine, [(mine[way], one, None) for way in near], diagonal=True, hides=False)
    sums = dict(zip(near, sums, strict=True))
    corner_there = stacked(["xyz"], [sums[""]])
    (sums["xyz"],) = sums_of(affine, [(mine["xyz"], one, None)], [sums[""]])
    two = [corner_there, stacked(TWO, [sums["xyz"], corner_there])]
    jobs = [(mine["xy"], one, None), (mine["zx"], one, None)]
    sums["xy"], sums["zx"] = sums_of(affine, jobs, [sums["xyz"]])

    def parts_of(ways, after, kind=FULL):
        return sums_of(affine, [(mine[way], two, sums[way]) for way in ways], after, kind)

    def added(part, other):
        (total,) = local(
            lambda _, refs: [refs[0][...] + refs[1][...].astype(FULL)], [unit], [], [part, other]
        )
        return total

    (part_xyz,) = parts_of(["xyz"], [sums["xy"]], HALF)
    for_yz = sent(part_xyz, "x")
    part_xy, part_zx = parts_of(["xy", "zx"], [part_xyz], HALF)
    for_x, for_z = sent(part_xy, "y"), sent(part_zx, "x")
    (part_yz,) = sums_of(affine, [(mine["yz"], one + two, None)], [part_xy])
    part_yz = added(part_yz, for_yz)
    for_y = sent(part_yz, "z")
    part_x, part_y, part_z = parts_of(ONE, [part_yz])
    part_x, part_z = added(part_x, for_x), added(part_z, for_z)
    from_x, from_z = sent(part_x, "x"), sent(part_z, "z")

    def halves(scalars, refs):
        core, total = scalars[0][0], refs[0]
        found = []
        for which in (core, 1 - core):
            at = pl.ds(pl.multiple_of(which * rows, rows), rows)
            half = total[at, :]
            for ref in refs[1:]:
                half = half + ref[at, :].astype(FULL)
            found.append(half)
        return found

    which = core.reshape(1)
    y_here, y_there = local(halves, [shard] * 2, [which], [part_y, for_y], [part_x, part_z])
    (own_part,) = parts_of([""], [y_here])
    y_here, y_there = sent(y_here, "y"), sent(y_there, "y", True)
    here, there = local(
        halves, [shard_full, shard], [which], [own_part, from_x, from_z], [y_there]
    )
    there = other_core(there)

    return tuple(
        pl.pallas_call(
            finish_kernel,
            out_shape=[jax.ShapeDtypeStruct(*shard_full)] * 2,
            in_specs=[SMEM] * 2 + [VMEM] * 6,
            out_specs=[ANY] * 2,
            scratch_shapes=[
                pltpu.VMEM((2, rows, width), FULL),
                pltpu.SemaphoreType.DMA((2 * CUTS,)),
            ],
            compiler_params=PARAMS,
        )(
            first_flag,
            multiplier,
            picture_vectors_raw,
            caption_vectors_raw,
            here,
            there,
            y_here,
            y_there,
        )
    )


def solution(mesh):
    fine = Mesh(mesh.devices.reshape(FINE_SIZES), FINE_AXES)
    rows = P(FINE_AXES, None)
    return jax.shard_map(
        on_device,
        mesh=fine,
        in_specs=(rows, rows, P(), P(), P()),
        out_specs=(rows, rows),
        check_vma=False,
    )
```

```python
import functools
import math

import jax
import jax.numpy as jnp
import numpy as np
from jax import lax
from jax.experimental import pallas as pl
from jax.experimental.pallas import tpu as pltpu
from jax.sharding import Mesh
from jax.sharding import PartitionSpec as P

FINE_AXES = ("y_lo", "core", "x", "z", "y_hi")
FINE_SIZES = (2, 2, 4, 4, 2)
RING = 4
VMEM_BYTES = 16 * 1024 * 1024
CUTS = 4
HALF = jnp.bfloat16
FULL = jnp.float32

VMEM = pl.BlockSpec(memory_space=pltpu.VMEM)
SMEM = pl.BlockSpec(memory_space=pltpu.SMEM)
ANY = pl.BlockSpec(memory_space=pl.ANY)
PARAMS = pltpu.CompilerParams(vmem_limit_bytes=VMEM_BYTES)

NAMES = ({"x": "x", "y": "y", "z": "z"}, {"x": "x", "y": "z", "z": "y"})
ONE = ("x", "y", "z")
TWO = ("xy", "yz", "zx")


def place(core, x, y, z):
    return int(np.ravel_multi_index((y % 2, core, x, z, y // 2), FINE_SIZES))


def mate(core, axis, k):
    if (core == 0) != (axis == "z"):
        return k ^ 1
    return (k + 1) % RING if k % 2 else (k - 1) % RING


def sent(value, way, crossing=False):
    pairs = []
    for at in np.ndindex(RING, RING, RING):
        for core in range(2):
            to = [
                mate(core, axis, k) if NAMES[core][axis] in way else k
                for axis, k in zip("xyz", at, strict=True)
            ]
            pairs.append((place(core, *at), place(1 - core if crossing else core, *to)))
    return lax.ppermute(value, FINE_AXES, pairs)


def other_core(value):
    return lax.ppermute(value, "core", [(0, 1), (1, 0)])


def dot(a, b, contract):
    return lax.dot_general(a, b, ((contract[:1], contract[1:]), ((), ())), preferred_element_type=FULL)


def unit_rows(raw):
    values = raw.astype(FULL)
    scale = lax.rsqrt(jnp.mean(values * values, axis=1, keepdims=True) + 1e-06) / math.sqrt(
        values.shape[1]
    )
    return values * scale, scale


def local(body, outs, scalars, arrays, after=()):
    n_scalars, n_arrays = len(scalars), len(arrays)

    def kernel(*refs):
        given = refs[: n_scalars + n_arrays]
        results = refs[n_scalars + n_arrays + len(after) :]
        for ref, value in zip(results, body(given[:n_scalars], given[n_scalars:]), strict=True):
            ref[...] = value.astype(ref.dtype)

    return pl.pallas_call(
        kernel,
        out_shape=[jax.ShapeDtypeStruct(s, d) for s, d in outs],
        in_specs=[SMEM] * n_scalars + [VMEM] * n_arrays + [ANY] * len(after),
        out_specs=[VMEM] * len(outs),
        compiler_params=PARAMS,
    )(*scalars, *arrays, *after)


def accumulate(affine, mine, theirs, coupling, start, diagonal):
    unit = mine.shape[0]
    slope, shift = 0.5 * affine[0][0], 0.5 * affine[1][0]
    pieces = [(ref, k) for ref in theirs for k in range(0, ref.shape[0], unit)]
    for n, (ref, k) in enumerate(pieces):
        energies = dot(mine, ref[pl.ds(k, unit), :], (1, 1))
        tile = 0.5 * jnp.tanh(slope * energies + shift) + 0.5
        if diagonal and n == 0:
            row = lax.broadcasted_iota(jnp.int32, tile.shape, 0)
            column = lax.broadcasted_iota(jnp.int32, tile.shape, 1)
            tile = tile - jnp.where(row == column, 1.0, 0.0)
        coupling[:, pl.ds(n * unit, unit)] = tile.astype(HALF)
    total, first = start, 0
    for ref in theirs:
        count = ref.shape[0]
        term = dot(coupling[:, pl.ds(first, count)], ref[...], (1, 0))
        total = term if total is None else total + term
        first += count
    return total


def sums_kernel(plan, n_inputs, n_after, diagonal, *refs):
    affine, refs = refs[:2], refs[2:]
    inputs, results, coupling = refs[:n_inputs], refs[n_inputs + n_after : -1], refs[-1]
    for k, (mine, theirs, start) in enumerate(plan):
        begin = None if start is None else inputs[start][...]
        total = accumulate(
            affine, inputs[mine][...], [inputs[n] for n in theirs], coupling, begin, diagonal and k == 0
        )
        results[k][...] = total.astype(results[k].dtype)


def sums_of(affine, jobs, after=(), kind=FULL, diagonal=False, hides=True):
    inputs, plan, tiles, widest = [], [], 0, 0

    def index(array):
        for n, known in enumerate(inputs):
            if known is array:
                return n
        inputs.append(array)
        return len(inputs) - 1

    unit, width = jobs[0][0].shape
    for mine, theirs, start in jobs:
        against = sum(array.shape[0] for array in theirs)
        tiles, widest = tiles + against // unit, max(widest, against)
        plan.append(
            (index(mine), [index(array) for array in theirs], None if start is None else index(start))
        )
    return pl.pallas_call(
        functools.partial(sums_kernel, plan, len(inputs), len(after), diagonal),
        out_shape=[jax.ShapeDtypeStruct((unit, width), kind)] * len(jobs),
        in_specs=[SMEM] * 2 + [VMEM] * len(inputs) + [ANY] * len(after),
        out_specs=[VMEM] * len(jobs),
        scratch_shapes=[pltpu.VMEM((unit, widest), HALF)],
        cost_estimate=pl.CostEstimate(
            flops=4 * tiles * unit**2 * width if hides else 0,
            bytes_accessed=8 * len(jobs) * unit * width if hides else 0,
            transcendentals=tiles * unit**2 if hides else 0,
        ),
        compiler_params=PARAMS,
    )(*affine, *inputs, *after)


def finish_kernel(is_first, multiplier, *refs):
    raws, (here, there, y_here, y_there), outs, (held, sems) = refs[:2], refs[2:6], refs[6:8], refs[8:]
    first = is_first[0] > 0
    cut = raws[0].shape[0] // CUTS
    copies = []
    for n in range(CUTS):
        at = pl.ds(n * cut, cut)
        totals = (here[at, :] + y_here[at, :].astype(FULL), there[at, :].astype(FULL) + y_there[at, :].astype(FULL))
        for k, raw in enumerate(raws):
            unit, scale = unit_rows(raw[at, :])
            grad = multiplier[0] * jnp.where(first, totals[k], totals[1 - k])
            held[k, at, :] = scale * (grad - unit * jnp.sum(unit * grad, axis=1, keepdims=True))
            copies.append(pltpu.make_async_copy(held.at[k, at], outs[k].at[at], sems.at[len(copies)]))
            copies[-1].start()
    for copy in copies:
        copy.wait()


def on_device(
    picture_vectors_raw, caption_vectors_raw, logit_multiplier, offset_term, incoming_adjoint
):
    rows, width = picture_vectors_raw.shape
    pairs = rows * math.prod(FINE_SIZES)
    core = lax.axis_index("core").astype(jnp.int32)
    is_first = core == 0
    first_flag = is_first.astype(FULL).reshape(1)
    affine = (logit_multiplier, offset_term)
    multiplier = incoming_adjoint * logit_multiplier / pairs
    shard, unit = ((rows, width), HALF), ((2 * rows, width), HALF)
    shard_full = ((rows, width), FULL)

    image_there = other_core(picture_vectors_raw)
    text_there = other_core(caption_vectors_raw)
    def own_shards(_, refs):
        units = unit_rows(refs[0][...])[0]
        return [units[:rows], units[rows:]]

    both = jnp.concatenate([picture_vectors_raw, caption_vectors_raw], 0)
    image, text = local(own_shards, [shard] * 2, [], [both])

    def own_units(scalars, refs):
        first = scalars[0][0] > 0
        image_there, text_there, image, text = [ref[...].astype(FULL) for ref in refs]
        images, texts = (image, unit_rows(image_there)[0]), (text, unit_rows(text_there)[0])
        results = [[], []]
        for k in range(2):
            of_image = jnp.where(first, images[k], images[1 - k])
            of_text = jnp.where(first, texts[k], texts[1 - k])
            results[0].append(jnp.where(first, of_image, of_text))
            results[1].append(jnp.where(first, of_text, of_image))
        return [jnp.concatenate(halves, 0) for halves in results]

    own, own_theirs = local(
        own_units, [unit] * 2, [first_flag], [image_there, text_there, image, text]
    )

    def stacked(ways, after=(), scalars=()):
        (stack,) = local(
            lambda _, refs: [jnp.concatenate([ref[...] for ref in refs], 0)],
            [((2 * rows * len(ways), width), HALF)],
            scalars,
            [mine[way] for way in ways],
            after,
        )
        return other_core(stack)

    mine = {"": own}
    for way in ONE:
        mine[way] = sent(own, way)
    mine["xyz"] = sent(mine["z"], "xy")
    mine["xy"] = sent(mine["x"], "y")
    mine["yz"] = sent(mine["y"], "z")
    mine["zx"] = sent(mine["z"], "x")
    near = ("", *ONE)
    one = [own_theirs, stacked(ONE, scalars=affine)]
    sums = sums_of(affine, [(mine[way], one, None) for way in near], diagonal=True, hides=False)
    sums = dict(zip(near, sums, strict=True))
    corner_there = stacked(["xyz"], [sums[""]])
    (sums["xyz"],) = sums_of(affine, [(mine["xyz"], one, None)], [sums[""]])
    two = [corner_there, stacked(TWO, [sums["xyz"], corner_there])]
    jobs = [(mine["xy"], one, None), (mine["zx"], one, None)]
    sums["xy"], sums["zx"] = sums_of(affine, jobs, [sums["xyz"]])

    def parts_of(ways, after, kind=FULL):
        return sums_of(affine, [(mine[way], two, sums[way]) for way in ways], after, kind)

    def added(part, other):
        (total,) = local(
            lambda _, refs: [refs[0][...] + refs[1][...].astype(FULL)], [unit], [], [part, other]
        )
        return total

    (part_xyz,) = parts_of(["xyz"], [sums["xy"]], HALF)
    for_yz = sent(part_xyz, "x")
    part_xy, part_zx = parts_of(["xy", "zx"], [part_xyz], HALF)
    for_x, for_z = sent(part_xy, "y"), sent(part_zx, "x")
    (part_yz,) = sums_of(affine, [(mine["yz"], one + two, None)], [part_xy])
    part_yz = added(part_yz, for_yz)
    for_y = sent(part_yz, "z")
    part_x, part_y, part_z = parts_of(ONE, [part_yz])
    part_x, part_z = added(part_x, for_x), added(part_z, for_z)
    from_x, from_z = sent(part_x, "x"), sent(part_z, "z")

    def halves(scalars, refs):
        core, total = scalars[0][0], refs[0]
        found = []
        for which in (core, 1 - core):
            at = pl.ds(pl.multiple_of(which * rows, rows), rows)
            half = total[at, :]
            for ref in refs[1:]:
                half = half + ref[at, :].astype(FULL)
            found.append(half)
        return found

    which = core.reshape(1)
    y_here, y_there = local(halves, [shard] * 2, [which], [part_y, for_y], [part_x, part_z])
    (own_part,) = parts_of([""], [y_here])
    y_here, y_there = sent(y_here, "y"), sent(y_there, "y", True)
    here, there = local(
        halves, [shard_full, shard], [which], [own_part, from_x, from_z], [y_there]
    )
    there = other_core(there)

    return tuple(
        pl.pallas_call(
            finish_kernel,
            out_shape=[jax.ShapeDtypeStruct(*shard_full)] * 2,
            in_specs=[SMEM] * 2 + [VMEM] * 6,
            out_specs=[ANY] * 2,
            scratch_shapes=[
                pltpu.VMEM((2, rows, width), FULL),
                pltpu.SemaphoreType.DMA((2 * CUTS,)),
            ],
            compiler_params=PARAMS,
        )(
            first_flag,
            multiplier,
            picture_vectors_raw,
            caption_vectors_raw,
            here,
            there,
            y_here,
            y_there,
        )
    )


def solution(mesh):
    fine = Mesh(mesh.devices.reshape(FINE_SIZES), FINE_AXES)
    rows = P(FINE_AXES, None)
    return jax.shard_map(
        on_device,
        mesh=fine,
        in_specs=(rows, rows, P(), P(), P()),
        out_specs=(rows, rows),
        check_vma=False,
    )
```

```python
import functools
import math

import jax
import jax.numpy as jnp
import numpy as np
from jax import lax
from jax.experimental import pallas as pl
from jax.experimental.pallas import tpu as pltpu
from jax.sharding import Mesh
from jax.sharding import PartitionSpec as P

FINE_AXES = ("y_lo", "core", "x", "z", "y_hi")
FINE_SIZES = (2, 2, 4, 4, 2)
RING = 4
VMEM_BYTES = 16 * 1024 * 1024
CUTS = 4
HALF = jnp.bfloat16
FULL = jnp.float32

VMEM = pl.BlockSpec(memory_space=pltpu.VMEM)
SMEM = pl.BlockSpec(memory_space=pltpu.SMEM)
ANY = pl.BlockSpec(memory_space=pl.ANY)
PARAMS = pltpu.CompilerParams(vmem_limit_bytes=VMEM_BYTES)

NAMES = ({"x": "x", "y": "y", "z": "z"}, {"x": "z", "y": "y", "z": "x"})
ONE = ("x", "y", "z")
TWO = ("xy", "yz", "zx")


def place(core, x, y, z):
    return int(np.ravel_multi_index((y % 2, core, x, z, y // 2), FINE_SIZES))


def mate(core, axis, k):
    if (core == 0) != (axis == "z"):
        return k ^ 1
    return (k + 1) % RING if k % 2 else (k - 1) % RING


def sent(value, way, crossing=False):
    pairs = []
    for at in np.ndindex(RING, RING, RING):
        for core in range(2):
            to = [
                mate(core, axis, k) if NAMES[core][axis] in way else k
                for axis, k in zip("xyz", at, strict=True)
            ]
            pairs.append((place(core, *at), place(1 - core if crossing else core, *to)))
    return lax.ppermute(value, FINE_AXES, pairs)


def other_core(value):
    return lax.ppermute(value, "core", [(0, 1), (1, 0)])


def dot(a, b, contract):
    return lax.dot_general(a, b, ((contract[:1], contract[1:]), ((), ())), preferred_element_type=FULL)


def unit_rows(raw):
    values = raw.astype(FULL)
    scale = lax.rsqrt(jnp.mean(values * values, axis=1, keepdims=True) + 1e-06) / math.sqrt(
        values.shape[1]
    )
    return values * scale, scale


def local(body, outs, scalars, arrays, after=()):
    n_scalars, n_arrays = len(scalars), len(arrays)

    def kernel(*refs):
        given = refs[: n_scalars + n_arrays]
        results = refs[n_scalars + n_arrays + len(after) :]
        for ref, value in zip(results, body(given[:n_scalars], given[n_scalars:]), strict=True):
            ref[...] = value.astype(ref.dtype)

    return pl.pallas_call(
        kernel,
        out_shape=[jax.ShapeDtypeStruct(s, d) for s, d in outs],
        in_specs=[SMEM] * n_scalars + [VMEM] * n_arrays + [ANY] * len(after),
        out_specs=[VMEM] * len(outs),
        compiler_params=PARAMS,
    )(*scalars, *arrays, *after)


def accumulate(affine, mine, theirs, coupling, start, diagonal):
    unit = mine.shape[0]
    slope, shift = 0.5 * affine[0][0], 0.5 * affine[1][0]
    pieces = [(ref, k) for ref in theirs for k in range(0, ref.shape[0], unit)]
    for n, (ref, k) in enumerate(pieces):
        energies = dot(mine, ref[pl.ds(k, unit), :], (1, 1))
        tile = 0.5 * jnp.tanh(slope * energies + shift) + 0.5
        if diagonal and n == 0:
            row = lax.broadcasted_iota(jnp.int32, tile.shape, 0)
            column = lax.broadcasted_iota(jnp.int32, tile.shape, 1)
            tile = tile - jnp.where(row == column, 1.0, 0.0)
        coupling[:, pl.ds(n * unit, unit)] = tile.astype(HALF)
    total, first = start, 0
    for ref in theirs:
        count = ref.shape[0]
        term = dot(coupling[:, pl.ds(first, count)], ref[...], (1, 0))
        total = term if total is None else total + term
        first += count
    return total


def sums_kernel(plan, n_inputs, n_after, diagonal, *refs):
    affine, refs = refs[:2], refs[2:]
    inputs, results, coupling = refs[:n_inputs], refs[n_inputs + n_after : -1], refs[-1]
    for k, (mine, theirs, start) in enumerate(plan):
        begin = None if start is None else inputs[start][...]
        total = accumulate(
            affine, inputs[mine][...], [inputs[n] for n in theirs], coupling, begin, diagonal and k == 0
        )
        results[k][...] = total.astype(results[k].dtype)


def sums_of(affine, jobs, after=(), kind=FULL, diagonal=False, hides=True):
    inputs, plan, tiles, widest = [], [], 0, 0

    def index(array):
        for n, known in enumerate(inputs):
            if known is array:
                return n
        inputs.append(array)
        return len(inputs) - 1

    unit, width = jobs[0][0].shape
    for mine, theirs, start in jobs:
        against = sum(array.shape[0] for array in theirs)
        tiles, widest = tiles + against // unit, max(widest, against)
        plan.append(
            (index(mine), [index(array) for array in theirs], None if start is None else index(start))
        )
    return pl.pallas_call(
        functools.partial(sums_kernel, plan, len(inputs), len(after), diagonal),
        out_shape=[jax.ShapeDtypeStruct((unit, width), kind)] * len(jobs),
        in_specs=[SMEM] * 2 + [VMEM] * len(inputs) + [ANY] * len(after),
        out_specs=[VMEM] * len(jobs),
        scratch_shapes=[pltpu.VMEM((unit, widest), HALF)],
        cost_estimate=pl.CostEstimate(
            flops=4 * tiles * unit**2 * width if hides else 0,
            bytes_accessed=8 * len(jobs) * unit * width if hides else 0,
            transcendentals=tiles * unit**2 if hides else 0,
        ),
        compiler_params=PARAMS,
    )(*affine, *inputs, *after)


def finish_kernel(is_first, multiplier, *refs):
    raws, (here, there, y_here, y_there), outs, (held, sems) = refs[:2], refs[2:6], refs[6:8], refs[8:]
    first = is_first[0] > 0
    cut = raws[0].shape[0] // CUTS
    copies = []
    for n in range(CUTS):
        at = pl.ds(n * cut, cut)
        totals = (here[at, :] + y_here[at, :].astype(FULL), there[at, :].astype(FULL) + y_there[at, :].astype(FULL))
        for k, raw in enumerate(raws):
            unit, scale = unit_rows(raw[at, :])
            grad = multiplier[0] * jnp.where(first, totals[k], totals[1 - k])
            held[k, at, :] = scale * (grad - unit * jnp.sum(unit * grad, axis=1, keepdims=True))
            copies.append(pltpu.make_async_copy(held.at[k, at], outs[k].at[at], sems.at[len(copies)]))
            copies[-1].start()
    for copy in copies:
        copy.wait()


def on_device(
    picture_vectors_raw, caption_vectors_raw, logit_multiplier, offset_term, incoming_adjoint
):
    rows, width = picture_vectors_raw.shape
    pairs = rows * math.prod(FINE_SIZES)
    core = lax.axis_index("core").astype(jnp.int32)
    is_first = core == 0
    first_flag = is_first.astype(FULL).reshape(1)
    affine = (logit_multiplier, offset_term)
    multiplier = incoming_adjoint * logit_multiplier / pairs
    shard, unit = ((rows, width), HALF), ((2 * rows, width), HALF)
    shard_full = ((rows, width), FULL)

    image_there = other_core(picture_vectors_raw)
    text_there = other_core(caption_vectors_raw)
    def own_shards(_, refs):
        units = unit_rows(refs[0][...])[0]
        return [units[:rows], units[rows:]]

    both = jnp.concatenate([picture_vectors_raw, caption_vectors_raw], 0)
    image, text = local(own_shards, [shard] * 2, [], [both])

    def own_units(scalars, refs):
        first = scalars[0][0] > 0
        image_there, text_there, image, text = [ref[...].astype(FULL) for ref in refs]
        images, texts = (image, unit_rows(image_there)[0]), (text, unit_rows(text_there)[0])
        results = [[], []]
        for k in range(2):
            of_image = jnp.where(first, images[k], images[1 - k])
            of_text = jnp.where(first, texts[k], texts[1 - k])
            results[0].append(jnp.where(first, of_image, of_text))
            results[1].append(jnp.where(first, of_text, of_image))
        return [jnp.concatenate(halves, 0) for halves in results]

    own, own_theirs = local(
        own_units, [unit] * 2, [first_flag], [image_there, text_there, image, text]
    )

    def stacked(ways, after=(), scalars=()):
        (stack,) = local(
            lambda _, refs: [jnp.concatenate([ref[...] for ref in refs], 0)],
            [((2 * rows * len(ways), width), HALF)],
            scalars,
            [mine[way] for way in ways],
            after,
        )
        return other_core(stack)

    mine = {"": own}
    for way in ONE:
        mine[way] = sent(own, way)
    mine["xyz"] = sent(mine["z"], "xy")
    mine["xy"] = sent(mine["x"], "y")
    mine["yz"] = sent(mine["y"], "z")
    mine["zx"] = sent(mine["z"], "x")
    near = ("", *ONE)
    one = [own_theirs, stacked(ONE, scalars=affine)]
    sums = sums_of(affine, [(mine[way], one, None) for way in near], diagonal=True, hides=False)
    sums = dict(zip(near, sums, strict=True))
    corner_there = stacked(["xyz"], [sums[""]])
    (sums["xyz"],) = sums_of(affine, [(mine["xyz"], one, None)], [sums[""]])
    two = [corner_there, stacked(TWO, [sums["xyz"], corner_there])]
    jobs = [(mine["xy"], one, None), (mine["zx"], one, None)]
    sums["xy"], sums["zx"] = sums_of(affine, jobs, [sums["xyz"]])

    def parts_of(ways, after, kind=FULL):
        return sums_of(affine, [(mine[way], two, sums[way]) for way in ways], after, kind)

    def added(part, other):
        (total,) = local(
            lambda _, refs: [refs[0][...] + refs[1][...].astype(FULL)], [unit], [], [part, other]
        )
        return total

    (part_xyz,) = parts_of(["xyz"], [sums["xy"]], HALF)
    for_yz = sent(part_xyz, "x")
    part_xy, part_zx = parts_of(["xy", "zx"], [part_xyz], HALF)
    for_x, for_z = sent(part_xy, "y"), sent(part_zx, "x")
    (part_yz,) = sums_of(affine, [(mine["yz"], one + two, None)], [part_xy])
    part_yz = added(part_yz, for_yz)
    for_y = sent(part_yz, "z")
    part_x, part_z = parts_of(["x", "z"], [part_yz])
    part_x, part_z = added(part_x, for_x), added(part_z, for_z)
    (part_y,) = parts_of(["y"], [part_x, part_z])
    from_x, from_z = sent(part_x, "x"), sent(part_z, "z")

    def halves(scalars, refs):
        core, total = scalars[0][0], refs[0]
        found = []
        for which in (core, 1 - core):
            at = pl.ds(pl.multiple_of(which * rows, rows), rows)
            half = total[at, :]
            for ref in refs[1:]:
                half = half + ref[at, :].astype(FULL)
            found.append(half)
        return found

    which = core.reshape(1)
    y_here, y_there = local(halves, [shard] * 2, [which], [part_y, for_y], [part_x, part_z])
    (own_part,) = parts_of([""], [y_here])
    y_here, y_there = sent(y_here, "y"), sent(y_there, "y", True)
    here, there = local(
        halves, [shard_full, shard], [which], [own_part, from_x, from_z], [y_there]
    )
    there = other_core(there)

    return tuple(
        pl.pallas_call(
            finish_kernel,
            out_shape=[jax.ShapeDtypeStruct(*shard_full)] * 2,
            in_specs=[SMEM] * 2 + [VMEM] * 6,
            out_specs=[ANY] * 2,
            scratch_shapes=[
                pltpu.VMEM((2, rows, width), FULL),
                pltpu.SemaphoreType.DMA((2 * CUTS,)),
            ],
            compiler_params=PARAMS,
        )(
            first_flag,
            multiplier,
            picture_vectors_raw,
            caption_vectors_raw,
            here,
            there,
            y_here,
            y_there,
        )
    )


def solution(mesh):
    fine = Mesh(mesh.devices.reshape(FINE_SIZES), FINE_AXES)
    rows = P(FINE_AXES, None)
    return jax.shard_map(
        on_device,
        mesh=fine,
        in_specs=(rows, rows, P(), P(), P()),
        out_specs=(rows, rows),
        check_vma=False,
    )
```

```python
import functools
import math

import jax
import jax.numpy as jnp
import numpy as np
from jax import lax
from jax.experimental import pallas as pl
from jax.experimental.pallas import tpu as pltpu
from jax.sharding import Mesh
from jax.sharding import PartitionSpec as P

FINE_AXES = ("y_lo", "core", "x", "z", "y_hi")
FINE_SIZES = (2, 2, 4, 4, 2)
RING = 4
VMEM_BYTES = 16 * 1024 * 1024
CUTS = 4
HALF = jnp.bfloat16
FULL = jnp.float32

VMEM = pl.BlockSpec(memory_space=pltpu.VMEM)
SMEM = pl.BlockSpec(memory_space=pltpu.SMEM)
ANY = pl.BlockSpec(memory_space=pl.ANY)
PARAMS = pltpu.CompilerParams(vmem_limit_bytes=VMEM_BYTES)

NAMES = ({"x": "x", "y": "y", "z": "z"}, {"x": "y", "y": "z", "z": "x"})
ONE = ("x", "y", "z")
TWO = ("xy", "yz", "zx")


def place(core, x, y, z):
    return int(np.ravel_multi_index((y % 2, core, x, z, y // 2), FINE_SIZES))


def mate(core, axis, k):
    if (core == 0) != (axis == "z"):
        return k ^ 1
    return (k + 1) % RING if k % 2 else (k - 1) % RING


def sent(value, way, crossing=False):
    pairs = []
    for at in np.ndindex(RING, RING, RING):
        for core in range(2):
            to = [
                mate(core, axis, k) if NAMES[core][axis] in way else k
                for axis, k in zip("xyz", at, strict=True)
            ]
            pairs.append((place(core, *at), place(1 - core if crossing else core, *to)))
    return lax.ppermute(value, FINE_AXES, pairs)


def other_core(value):
    return lax.ppermute(value, "core", [(0, 1), (1, 0)])


def dot(a, b, contract):
    return lax.dot_general(a, b, ((contract[:1], contract[1:]), ((), ())), preferred_element_type=FULL)


def unit_rows(raw):
    values = raw.astype(FULL)
    scale = lax.rsqrt(jnp.mean(values * values, axis=1, keepdims=True) + 1e-06) / math.sqrt(
        values.shape[1]
    )
    return values * scale, scale


def local(body, outs, scalars, arrays, after=()):
    n_scalars, n_arrays = len(scalars), len(arrays)

    def kernel(*refs):
        given = refs[: n_scalars + n_arrays]
        results = refs[n_scalars + n_arrays + len(after) :]
        for ref, value in zip(results, body(given[:n_scalars], given[n_scalars:]), strict=True):
            ref[...] = value.astype(ref.dtype)

    return pl.pallas_call(
        kernel,
        out_shape=[jax.ShapeDtypeStruct(s, d) for s, d in outs],
        in_specs=[SMEM] * n_scalars + [VMEM] * n_arrays + [ANY] * len(after),
        out_specs=[VMEM] * len(outs),
        compiler_params=PARAMS,
    )(*scalars, *arrays, *after)


def accumulate(affine, mine, theirs, coupling, start, diagonal):
    unit = mine.shape[0]
    slope, shift = 0.5 * affine[0][0], 0.5 * affine[1][0]
    pieces = [(ref, k) for ref in theirs for k in range(0, ref.shape[0], unit)]
    for n, (ref, k) in enumerate(pieces):
        energies = dot(mine, ref[pl.ds(k, unit), :], (1, 1))
        tile = 0.5 * jnp.tanh(slope * energies + shift) + 0.5
        if diagonal and n == 0:
            row = lax.broadcasted_iota(jnp.int32, tile.shape, 0)
            column = lax.broadcasted_iota(jnp.int32, tile.shape, 1)
            tile = tile - jnp.where(row == column, 1.0, 0.0)
        coupling[:, pl.ds(n * unit, unit)] = tile.astype(HALF)
    total, first = start, 0
    for ref in theirs:
        count = ref.shape[0]
        term = dot(coupling[:, pl.ds(first, count)], ref[...], (1, 0))
        total = term if total is None else total + term
        first += count
    return total


def sums_kernel(plan, n_inputs, n_after, diagonal, *refs):
    affine, refs = refs[:2], refs[2:]
    inputs, results, coupling = refs[:n_inputs], refs[n_inputs + n_after : -1], refs[-1]
    for k, (mine, theirs, start) in enumerate(plan):
        begin = None if start is None else inputs[start][...]
        total = accumulate(
            affine, inputs[mine][...], [inputs[n] for n in theirs], coupling, begin, diagonal and k == 0
        )
        results[k][...] = total.astype(results[k].dtype)


def sums_of(affine, jobs, after=(), kind=FULL, diagonal=False, hides=True):
    inputs, plan, tiles, widest = [], [], 0, 0

    def index(array):
        for n, known in enumerate(inputs):
            if known is array:
                return n
        inputs.append(array)
        return len(inputs) - 1

    unit, width = jobs[0][0].shape
    for mine, theirs, start in jobs:
        against = sum(array.shape[0] for array in theirs)
        tiles, widest = tiles + against // unit, max(widest, against)
        plan.append(
            (index(mine), [index(array) for array in theirs], None if start is None else index(start))
        )
    return pl.pallas_call(
        functools.partial(sums_kernel, plan, len(inputs), len(after), diagonal),
        out_shape=[jax.ShapeDtypeStruct((unit, width), kind)] * len(jobs),
        in_specs=[SMEM] * 2 + [VMEM] * len(inputs) + [ANY] * len(after),
        out_specs=[VMEM] * len(jobs),
        scratch_shapes=[pltpu.VMEM((unit, widest), HALF)],
        cost_estimate=pl.CostEstimate(
            flops=4 * tiles * unit**2 * width if hides else 0,
            bytes_accessed=8 * len(jobs) * unit * width if hides else 0,
            transcendentals=tiles * unit**2 if hides else 0,
        ),
        compiler_params=PARAMS,
    )(*affine, *inputs, *after)


def finish_kernel(is_first, multiplier, *refs):
    raws, (here, there, y_here, y_there), outs, (held, sems) = refs[:2], refs[2:6], refs[6:8], refs[8:]
    first = is_first[0] > 0
    cut = raws[0].shape[0] // CUTS
    copies = []
    for n in range(CUTS):
        at = pl.ds(n * cut, cut)
        totals = (here[at, :] + y_here[at, :].astype(FULL), there[at, :].astype(FULL) + y_there[at, :].astype(FULL))
        for k, raw in enumerate(raws):
            unit, scale = unit_rows(raw[at, :])
            grad = multiplier[0] * jnp.where(first, totals[k], totals[1 - k])
            held[k, at, :] = scale * (grad - unit * jnp.sum(unit * grad, axis=1, keepdims=True))
            copies.append(pltpu.make_async_copy(held.at[k, at], outs[k].at[at], sems.at[len(copies)]))
            copies[-1].start()
    for copy in copies:
        copy.wait()


def on_device(
    picture_vectors_raw, caption_vectors_raw, logit_multiplier, offset_term, incoming_adjoint
):
    rows, width = picture_vectors_raw.shape
    pairs = rows * math.prod(FINE_SIZES)
    core = lax.axis_index("core").astype(jnp.int32)
    is_first = core == 0
    first_flag = is_first.astype(FULL).reshape(1)
    affine = (logit_multiplier, offset_term)
    multiplier = incoming_adjoint * logit_multiplier / pairs
    shard, unit = ((rows, width), HALF), ((2 * rows, width), HALF)
    shard_full = ((rows, width), FULL)

    image_there = other_core(picture_vectors_raw)
    text_there = other_core(caption_vectors_raw)
    def own_shards(_, refs):
        units = unit_rows(refs[0][...])[0]
        return [units[:rows], units[rows:]]

    both = jnp.concatenate([picture_vectors_raw, caption_vectors_raw], 0)
    image, text = local(own_shards, [shard] * 2, [], [both])

    def own_units(scalars, refs):
        first = scalars[0][0] > 0
        image_there, text_there, image, text = [ref[...].astype(FULL) for ref in refs]
        images, texts = (image, unit_rows(image_there)[0]), (text, unit_rows(text_there)[0])
        results = [[], []]
        for k in range(2):
            of_image = jnp.where(first, images[k], images[1 - k])
            of_text = jnp.where(first, texts[k], texts[1 - k])
            results[0].append(jnp.where(first, of_image, of_text))
            results[1].append(jnp.where(first, of_text, of_image))
        return [jnp.concatenate(halves, 0) for halves in results]

    own, own_theirs = local(
        own_units, [unit] * 2, [first_flag], [image_there, text_there, image, text]
    )

    def stacked(ways, after=(), scalars=()):
        (stack,) = local(
            lambda _, refs: [jnp.concatenate([ref[...] for ref in refs], 0)],
            [((2 * rows * len(ways), width), HALF)],
            scalars,
            [mine[way] for way in ways],
            after,
        )
        return other_core(stack)

    mine = {"": own}
    for way in ONE:
        mine[way] = sent(own, way)
    mine["xyz"] = sent(mine["z"], "xy")
    mine["xy"] = sent(mine["x"], "y")
    mine["yz"] = sent(mine["y"], "z")
    mine["zx"] = sent(mine["z"], "x")
    near = ("", *ONE)
    one = [own_theirs, stacked(ONE, scalars=affine)]
    sums = sums_of(affine, [(mine[way], one, None) for way in near], diagonal=True, hides=False)
    sums = dict(zip(near, sums, strict=True))
    corner_there = stacked(["xyz"], [sums[""]])
    (sums["xyz"],) = sums_of(affine, [(mine["xyz"], one, None)], [sums[""]])
    two = [corner_there, stacked(TWO, [sums["xyz"], corner_there])]
    jobs = [(mine["xy"], one, None), (mine["zx"], one, None)]
    sums["xy"], sums["zx"] = sums_of(affine, jobs, [sums["xyz"]])

    def parts_of(ways, after, kind=FULL):
        return sums_of(affine, [(mine[way], two, sums[way]) for way in ways], after, kind)

    def added(part, other):
        (total,) = local(
            lambda _, refs: [refs[0][...] + refs[1][...].astype(FULL)], [unit], [], [part, other]
        )
        return total

    (part_xyz,) = parts_of(["xyz"], [sums["xy"]], HALF)
    for_yz = sent(part_xyz, "x")
    part_xy, part_zx = parts_of(["xy", "zx"], [part_xyz], HALF)
    for_x, for_z = sent(part_xy, "y"), sent(part_zx, "x")
    (part_yz,) = sums_of(affine, [(mine["yz"], one + two, None)], [part_xy])
    part_yz = added(part_yz, for_yz)
    for_y = sent(part_yz, "z")
    part_x, part_y, part_z = parts_of(ONE, [part_yz])
    part_x, part_z = added(part_x, for_x), added(part_z, for_z)
    from_x, from_z = sent(part_x, "x"), sent(part_z, "z")

    def halves(scalars, refs):
        core, total = scalars[0][0], refs[0]
        found = []
        for which in (core, 1 - core):
            at = pl.ds(pl.multiple_of(which * rows, rows), rows)
            half = total[at, :]
            for ref in refs[1:]:
                half = half + ref[at, :].astype(FULL)
            found.append(half)
        return found

    which = core.reshape(1)
    y_here, y_there = local(halves, [shard] * 2, [which], [part_y, for_y], [part_x, part_z])
    (own_part,) = parts_of([""], [y_here])
    y_here, y_there = sent(y_here, "y"), sent(y_there, "y", True)
    here, there = local(
        halves, [shard_full, shard], [which], [own_part, from_x, from_z], [y_there]
    )
    there = other_core(there)

    return tuple(
        pl.pallas_call(
            finish_kernel,
            out_shape=[jax.ShapeDtypeStruct(*shard_full)] * 2,
            in_specs=[SMEM] * 2 + [VMEM] * 6,
            out_specs=[ANY] * 2,
            scratch_shapes=[
                pltpu.VMEM((2, rows, width), FULL),
                pltpu.SemaphoreType.DMA((2 * CUTS,)),
            ],
            compiler_params=PARAMS,
        )(
            first_flag,
            multiplier,
            picture_vectors_raw,
            caption_vectors_raw,
            here,
            there,
            y_here,
            y_there,
        )
    )


def solution(mesh):
    fine = Mesh(mesh.devices.reshape(FINE_SIZES), FINE_AXES)
    rows = P(FINE_AXES, None)
    return jax.shard_map(
        on_device,
        mesh=fine,
        in_specs=(rows, rows, P(), P(), P()),
        out_specs=(rows, rows),
        check_vma=False,
    )
```
